128 devices in a mesh: wide: 16 (over z, x), narrow: 8 (over y, core).
Axes of the slice: x: 4, y: 4, z: 4, core: 2. Of those that a mesh axis runs over, the one named last changes fastest.
Arguments:
- load: float32 [3, 128, 128, 384], P(None, 'wide', 'narrow'), may hold values from -6 to 6
- density: float32 [128, 128, 384], P('wide', 'narrow'), may hold values from 0.55 to 1
Outputs:
- correction: float32 [3, 128, 128, 384], P(None, 'wide', 'narrow')
The draws below stay inside these ranges and needn't reach their ends.
All inputs are finite; a program needn't handle non-finite values.
Results may differ from the reference program's by a relative error of at most 0.0001.
Values sent between devices are 32-bit elements; how exact they have to be, the bound alone decides.
No kernel may reach another device: no remote copies, remote signals or barrier semaphores. Data moves between devices by JAX's collectives and lax.ppermute only.
A program may use at most 128 MiB of HBM per device.

```python
import jax
import jax.numpy as jnp

NX = 384
LEVELS = 4
SWEEPS = 2
NZ = 128
NY = 128


def draw_load(key, part):
    key = jax.random.fold_in(key, 11)
    return jnp.clip(1.5 * jax.random.normal(key, (3, NZ, NY, NX), jnp.float32), -6.0, 6.0)


def level_of(stream_key, dims, cuts, low, top_value):
    def one(axis_at, parts):
        steps = jax.random.uniform(jax.random.fold_in(jax.random.fold_in(stream_key, 6), axis_at), (parts,), jnp.float32, low / len(cuts), top_value / len(cuts))
        return jnp.repeat(jnp.exp(steps), dims[axis_at] // parts).reshape((-1,) + (1,) * (len(dims) - axis_at - 1))

    level = one(*cuts[0])
    for cut in cuts[1:]:
        level = level * one(*cut)
    return level


def setup_inputs(seed: int = 0) -> dict:
    arg_keys = jax.random.split(jax.random.key(seed), 3)
    load = draw_load(jax.random.fold_in(arg_keys[2], 71), 0)
    density = jnp.clip(0.55 + 0.45 * jax.random.uniform(arg_keys[1], (NZ, NY, NX), jnp.float32) ** level_of(arg_keys[1], (NZ, NY, NX), ((0, 16), (1, 8)), -0.2, 0.2), 0.55, 1.0)
    return dict(load=load, density=density)


damping = 0.5
mass_term = 0.02


def pad_cells(field):
    return jnp.pad(field, [(0, 0)] * (field.ndim - 3) + [(1, 1)] * 3)


def inner(padded, axis, step):
    count = padded.ndim
    index = [slice(None)] * (count - 3) + [slice(1, -1)] * 3
    extent = padded.shape[count - 3 + axis]
    index[count - 3 + axis] = slice(1 + step, extent - 1 + step)
    return padded[tuple(index)]


def coarsen_sum(field):
    shape = field.shape
    lead = shape[:-3]
    split = field.reshape(lead + (shape[-3] // 2, 2, shape[-2] // 2, 2, shape[-1] // 2, 2))
    return jnp.sum(split, axis=(-5, -3, -1))


def prolong(field):
    return jnp.repeat(jnp.repeat(jnp.repeat(field, 2, -3), 2, -2), 2, -1)


def moduli(dens):
    shear = dens * dens * dens
    bulk = shear * (0.5 + dens)
    return shear, bulk


def coefficients(shear, bulk):
    shear_pad = pad_cells(shear)
    bulk_pad = pad_cells(bulk)
    plus = [0.5 * (shear + inner(shear_pad, d, 1)) for d in range(3)]
    minus = [0.5 * (shear + inner(shear_pad, d, -1)) for d in range(3)]
    total = mass_term + plus[0] + minus[0] + plus[1] + minus[1] + plus[2] + minus[2]
    diag = jnp.stack([total + bulk + inner(bulk_pad, c, 1) for c in range(3)])
    return plus, minus, bulk, diag


def operate(field, coef):
    plus, minus, bulk, diag = coef
    padded = pad_cells(field)
    div = (field[0] - inner(padded[0], 0, -1)) + (field[1] - inner(padded[1], 1, -1)) + (field[2] - inner(padded[2], 2, -1))
    stress = bulk * div
    stress_pad = pad_cells(stress)
    grad = jnp.stack([stress - inner(stress_pad, c, 1) for c in range(3)])
    lap = plus[0] * (field - inner(padded, 0, 1)) + minus[0] * (field - inner(padded, 0, -1))
    lap = lap + plus[1] * (field - inner(padded, 1, 1)) + minus[1] * (field - inner(padded, 1, -1))
    lap = lap + plus[2] * (field - inner(padded, 2, 1)) + minus[2] * (field - inner(padded, 2, -1))
    return mass_term * field + lap + grad


def smooth(rhs, coef, count):
    field = damping * rhs / coef[3]
    for sweep in range(count - 1):
        field = field + damping * (rhs - operate(field, coef)) / coef[3]
    return field


def reference(load, density):
    dens = [density]
    for level in range(1, LEVELS):
        dens.append(coarsen_sum(dens[-1]) * 0.125)
    rhs = load
    saved = []
    for level in range(LEVELS - 1):
        shear, bulk = moduli(dens[level])
        coef = coefficients(shear, bulk)
        field = smooth(rhs, coef, SWEEPS)
        resid = rhs - operate(field, coef)
        saved.append((field, rhs, coef))
        rhs = 0.5 * coarsen_sum(resid)
    shear, bulk = moduli(dens[-1])
    field = smooth(rhs, coefficients(shear, bulk), 2 * SWEEPS)
    for level in reversed(range(LEVELS - 1)):
        fine_field, fine_rhs, coef = saved[level]
        field = fine_field + prolong(field)
        for sweep in range(SWEEPS):
            field = field + damping * (fine_rhs - operate(field, coef)) / coef[3]
    return field
```

```python
import functools

import jax
import jax.numpy as jnp
from jax import lax
from jax.experimental import pallas as pl
from jax.experimental.pallas import tpu as pltpu
from jax.sharding import Mesh, PartitionSpec as P

DAMPING = 0.5
MASS = 0.02
NARROW = ("y", "core")
F32 = jnp.float32
BF16 = jnp.bfloat16


def cyclic(count, step):
    return [(i, (i + step) % count) for i in range(count)]


def after(v, axis):
    return pltpu.roll(v, v.shape[axis] - 1, axis)


def before(v, axis):
    return pltpu.roll(v, 1, axis)


def times01(v, matrix):
    high = v.astype(BF16)
    rest = v - high.astype(F32)
    mid = rest.astype(BF16)
    low = (rest - mid.astype(F32)).astype(BF16)
    out = jnp.dot(high, matrix, preferred_element_type=F32)
    out = out + jnp.dot(mid, matrix, preferred_element_type=F32)
    return out + jnp.dot(low, matrix, preferred_element_type=F32)


def pair_sum_matrix(fine, coarse, factor):
    i = lax.broadcasted_iota(jnp.int32, (fine, coarse), 0)
    j = lax.broadcasted_iota(jnp.int32, (fine, coarse), 1)
    return jnp.where((i >> 1) == j, factor, 0.0).astype(BF16)


def copy_matrix(coarse, fine):
    j = lax.broadcasted_iota(jnp.int32, (coarse, fine), 0)
    i = lax.broadcasted_iota(jnp.int32, (coarse, fine), 1)
    return jnp.where((i >> 1) == j, 1.0, 0.0).astype(BF16)


class Level:
    def __init__(self, rows, lanes, wrap_x, wrap_y, gx, gy, gz, m, w, ms, base):
        self.rows, self.lanes = rows, lanes
        self.wrap_x, self.wrap_y = wrap_x, wrap_y
        self.gx, self.gy, self.gz, self.m, self.w, self.ms = gx, gy, gz, m, w, ms
        self.base = base

    def masks(self):
        row = lax.broadcasted_iota(jnp.int32, (self.rows, self.lanes), 0)
        lane = lax.broadcasted_iota(jnp.int32, (self.rows, self.lanes), 1)
        return (row == 0, row == self.rows - 1, lane == 0, lane == self.lanes - 1)


def after_in(v, axis, level, masks):
    r = after(v, axis)
    if axis == 0 and level.wrap_y:
        r = jnp.where(masks[1], 0.0, r)
    if axis == 1 and level.wrap_x:
        r = jnp.where(masks[3], 0.0, r)
    return r


def before_in(v, axis, level, masks):
    r = before(v, axis)
    if axis == 0 and level.wrap_y:
        r = jnp.where(masks[0], 0.0, r)
    if axis == 1 and level.wrap_x:
        r = jnp.where(masks[2], 0.0, r)
    return r


def coefficients(level, rho, lo, hi):
    masks = level.masks()

    def shear(z):
        d = rho(z)
        return d * d * d

    def plane(z, _):
        zb = z + level.base
        d = rho(z)
        dn = rho(z + 1)
        g = d * d * d
        gn = dn * dn * dn
        gp = shear(z - 1)
        m = g * (0.5 + d)
        mn = gn * (0.5 + dn)
        gx = 0.5 * (g + after(g, 1))
        gy = 0.5 * (g + after(g, 0))
        gz = 0.5 * (g + gn)
        total = MASS + gz + 0.5 * (g + gp)
        extra = None
        if level.wrap_x:
            gx = jnp.where(masks[3], 0.0, gx)
            extra = jnp.where(masks[2] | masks[3], 0.5 * g, 0.0)
        if level.wrap_y:
            gy = jnp.where(masks[1], 0.0, gy)
            more = jnp.where(masks[0] | masks[1], 0.5 * g, 0.0)
            extra = more if extra is None else extra + more
        if extra is not None:
            level.ms[zb] = MASS + extra
            total = total + extra
        total = total + (gx + before(gx, 1)) + (gy + before(gy, 0)) + m
        inside = d > 0.0
        level.gx[zb] = gx
        level.gy[zb] = gy
        level.gz[zb] = gz
        level.m[zb] = m
        level.w[0, zb] = jnp.where(inside, DAMPING / (total + mn), 0.0)
        level.w[1, zb] = jnp.where(inside, DAMPING / (total + after_in(m, 0, level, masks)), 0.0)
        level.w[2, zb] = jnp.where(inside, DAMPING / (total + after_in(m, 1, level, masks)), 0.0)
        return 0

    g0 = shear(lo - 1)
    level.gz[lo - 1 + level.base] = 0.5 * (g0 + shear(lo))
    dh = rho(hi)
    level.m[hi + level.base] = dh * dh * dh * (0.5 + dh)
    lax.fori_loop(lo, hi, plane, 0)


def operate(level, u, lo, hi, s_ref, f_ref, emit):
    masks = level.masks()

    def stress(z):
        uz, uy, ux = u(0, z), u(1, z), u(2, z)
        div = (uz - u(0, z - 1)) + (uy - before_in(uy, 0, level, masks))
        div = div + (ux - before_in(ux, 1, level, masks))
        return level.m[z + level.base] * div

    s_ref[...] = stress(lo)
    gz0 = level.gz[lo - 1 + level.base]
    for c in range(3):
        f_ref[c] = gz0 * (u(c, lo - 1) - u(c, lo))

    def plane(z, _):
        zb = z + level.base
        s = s_ref[...]
        sn = stress(z + 1)
        s_ref[...] = sn
        gx, gy, gz = level.gx[zb], level.gy[zb], level.gz[zb]
        for c in range(3):
            v = u(c, z)
            fz = gz * (v - u(c, z + 1))
            fx = gx * (v - after(v, 1))
            fy = gy * (v - after(v, 0))
            if c == 0:
                grad = s - sn
            elif c == 1:
                grad = s - after_in(s, 0, level, masks)
            else:
                grad = s - after_in(s, 1, level, masks)
            mass = MASS if level.ms is None else level.ms[zb]
            a = mass * v + (fz - f_ref[c]) + (fx - before(fx, 1)) + (fy - before(fy, 0)) + grad
            f_ref[c] = fz
            emit(z, c, v, a)
        return 0

    lax.fori_loop(lo, hi, plane, 0)


def compact_rows(scratch, v):
    parts = []
    rows = v.shape[0]
    for k in range(v.shape[1] // 128):
        ref = scratch.at[k]
        ref[pl.ds(0, rows), :] = v[:, 128 * k : 128 * (k + 1)]
        parts.append(
            ref[pl.ds(0, rows // 2, stride=2), :] + ref[pl.ds(1, rows // 2, stride=2), :]
        )
    return parts[0] if len(parts) == 1 else jnp.concatenate(parts, axis=1)


def copy_rows(scratch, v):
    rows = v.shape[0]
    for k in range(v.shape[1] // 128):
        ref = scratch.at[k]
        part = v[:, 128 * k : 128 * (k + 1)]
        ref[pl.ds(0, rows, stride=2), :] = part
        ref[pl.ds(1, rows, stride=2), :] = part


def cell_mask(rows, own, high, low, n, last):
    row = lax.broadcasted_iota(jnp.int32, (rows, 128), 0)
    bad_high = (row >= own) & (row < own + high) & (n == last)
    bad_low = (row >= rows - low) & (n == 0)
    return jnp.where(bad_high | bad_low, 0.0, 1.0)


def down0(idx, x1, lo, hi, b, gx, gy, gz, m, w, ms, ep, l1, rho, e1, rz, s_ref, f_ref, pack):
    wide, narrow = idx[0], idx[1]
    rowmask = jnp.concatenate([cell_mask(24, 16, 4, 4, narrow, 7)] * 3, axis=1)
    below = jnp.where(wide == 0, 0.0, 1.0) * rowmask
    above = jnp.where(wide == 15, 0.0, 1.0) * rowmask
    for z in range(4):
        rho[z] = lo[9 + z] * below
        rho[12 + z] = hi[9 + z] * above
    for z in range(8):
        rho[4 + z] = x1[3, z] * rowmask
    for c in range(3):
        for z in range(3):
            b[c, 1 + z] = lo[3 * c + z]
            b[c, 12 + z] = hi[3 * c + z]
        for z in range(8):
            b[c, 4 + z] = x1[c, z]
    level = Level(24, 384, True, False, gx, gy, gz, m, w, ms, 0)
    coefficients(level, lambda z: rho[z], 1, 15)

    def first(z, _):
        for c in range(3):
            e1[c, z] = w[c, z] * b[c, z]
        return 0

    lax.fori_loop(1, 15, first, 0)

    def sweep(z, c, v, a):
        ep[c, z] = v + w[c, z] * (b[c, z] - a)

    operate(level, lambda c, z: e1[c, z], 2, 14, s_ref, f_ref, sweep)
    rz[...] = jnp.zeros_like(rz)

    def residual(z, c, v, a):
        r = b[c, z] - a
        k = (z >> 1) - 2
        rz[c, k] = rz[c, k] + r[:16]

    operate(level, lambda c, z: ep[c, z], 4, 12, s_ref, f_ref, residual)
    half = pair_sum_matrix(384, 256, 0.5)
    v = times01(rz[...].reshape(192, 384), half)
    l1[0:12] = compact_rows(pack, v).reshape(12, 8, 256)
    eighth = pair_sum_matrix(384, 256, 0.125)
    d = jnp.stack([rho[2 * k + 2, :16] + rho[2 * k + 3, :16] for k in range(6)])
    l1[12:18] = compact_rows(pack, times01(d.reshape(96, 384), eighth)).reshape(6, 8, 256)


def down1(idx, own, lo, hi, b, gx, gy, gz, m, w, ep, chunk, rho, e1, rz, s_ref, f_ref, pack):
    wide, narrow = idx[0], idx[1]
    rowmask = jnp.concatenate([cell_mask(24, 8, 8, 8, narrow, 7)] * 2, axis=1)
    below = jnp.where(wide == 0, 0.0, 1.0) * rowmask
    above = jnp.where(wide == 15, 0.0, 1.0) * rowmask
    for z in range(5):
        rho[z] = lo[12 + z] * below
        rho[9 + z] = hi[12 + z] * above
    for z in range(4):
        rho[5 + z] = own[13 + z] * rowmask
        for c in range(3):
            b[c, 1 + z] = lo[4 * c + z]
            b[c, 5 + z] = own[4 * c + z]
            b[c, 9 + z] = hi[4 * c + z]
    level = Level(24, 256, False, False, gx, gy, gz, m, w, None, 0)
    coefficients(level, lambda z: rho[z], 1, 13)

    def first(z, _):
        for c in range(3):
            e1[c, z] = w[c, z] * b[c, z]
        return 0

    lax.fori_loop(1, 13, first, 0)

    def sweep(z, c, v, a):
        ep[c, z] = v + w[c, z] * (b[c, z] - a)

    operate(level, lambda c, z: e1[c, z], 2, 12, s_ref, f_ref, sweep)
    rz[...] = jnp.zeros_like(rz)

    def residual(z, c, v, a):
        r = b[c, z] - a
        k = ((z + 1) >> 1) - 3
        rz[c, k] = rz[c, k] + r[:8]

    operate(level, lambda c, z: ep[c, z], 5, 9, s_ref, f_ref, residual)
    rz[3, 0] = 0.25 * (rho[5, :8] + rho[6, :8])
    rz[3, 1] = 0.25 * (rho[7, :8] + rho[8, :8])
    half = pair_sum_matrix(256, 128, 0.5)
    v = compact_rows(pack, times01(rz[...].reshape(64, 256), half))
    lane = lax.broadcasted_iota(jnp.int32, (8, 128), 1)
    d = v[24:32]
    for c in range(3):
        moved = d if c == 3 else pltpu.roll(d, (96 - 32 * c) % 128, 1)
        chunk[:, 128 * c : 128 * (c + 1)] = jnp.where(lane < 96, v[8 * c : 8 * c + 8], moved)


def rest(
    idx, mine, other,
    b1, gx1, gy1, gz1, m1, w1, ep1,
    b0, gx0, gy0, gz0, m0, w0, ms0, ep0,
    out,
    rho2, b2, gx2, gy2, gz2, m2, w2, ms2, ea, ep2,
    rho3, b3, gx3, gy3, gz3, m3, w3, ms3, ec, ed,
    rz, rd, pack, s2, f2, s3, f3, ua, ub, va, vb, s1, f1, xa, xb, s0, f0,
):
    wide, narrow, core = idx[0], idx[1], idx[2]
    row8 = lax.broadcasted_iota(jnp.int32, (8, 128), 0)
    lane8 = lax.broadcasted_iota(jnp.int32, (8, 128), 1)
    zero2 = jnp.zeros((32, 128), F32)
    zero3 = jnp.zeros((16, 128), F32)
    for z in (0, 1, 2, 3, 36, 37, 38, 39):
        rho2[z] = zero2
        for ref in (gx2, gy2, gz2, m2, ms2):
            ref[z] = zero2
        for c in range(3):
            w2[c, z] = zero2
            b2[c, z] = zero2
            ea[c, z] = zero2
            ep2[c, z] = zero2
    for z in (0, 1, 18, 19):
        rho3[z] = zero3
        for ref in (gx3, gy3, gz3, m3, ms3):
            ref[z] = zero3
        for c in range(3):
            w3[c, z] = zero3
            ec[c, z] = zero3
            ed[c, z] = zero3

    def unpack(k, _):
        z = 2 * k + 4
        for y in range(4):
            a, c_ = mine[4 * k + y], other[4 * k + y]
            even = jnp.where(core == 0, a, c_)
            odd = jnp.where(core == 0, c_, a)
            rest_d = []
            for c in range(3):
                e = even[:, 128 * c : 128 * (c + 1)]
                o = odd[:, 128 * c : 128 * (c + 1)]
                first = jnp.where(row8 < 4, e, pltpu.roll(o, 4, 0))
                second = jnp.where(row8 < 4, pltpu.roll(e, 4, 0), o)
                b2[c, z, pl.ds(8 * y, 8), :] = jnp.where(lane8 < 96, first, 0.0)
                b2[c, z + 1, pl.ds(8 * y, 8), :] = jnp.where(lane8 < 96, second, 0.0)
                turn = (128 - (96 - 32 * c)) % 128
                rest_d.append((pltpu.roll(first, turn, 1), pltpu.roll(second, turn, 1)))
            for s in range(2):
                d = jnp.where(
                    lane8 < 32, rest_d[0][s], jnp.where(lane8 < 64, rest_d[1][s], rest_d[2][s])
                )
                rho2[z + s, pl.ds(8 * y, 8), :] = jnp.where(lane8 < 96, d, 0.0)
        return 0

    lax.fori_loop(0, 16, unpack, 0)

    level2 = Level(32, 128, False, True, gx2, gy2, gz2, m2, w2, ms2, 0)
    coefficients(level2, lambda z: rho2[z], 4, 36)

    def first2(z, _):
        for c in range(3):
            ea[c, z] = w2[c, z] * b2[c, z]
        return 0

    lax.fori_loop(4, 36, first2, 0)

    def sweep2(z, c, v, a):
        ep2[c, z] = v + w2[c, z] * (b2[c, z] - a)

    operate(level2, lambda c, z: ea[c, z], 4, 36, s2, f2, sweep2)
    rz[...] = jnp.zeros_like(rz)

    def residual2(z, c, v, a):
        k = (z >> 1) - 2
        rz[c, k] = rz[c, k] + (b2[c, z] - a)

    operate(level2, lambda c, z: ep2[c, z], 4, 36, s2, f2, residual2)

    def dens3(z, _):
        rz[3, z] = 0.25 * (rho2[2 * z + 4] + rho2[2 * z + 5])
        return 0

    lax.fori_loop(0, 16, dens3, 0)
    half = pair_sum_matrix(128, 128, 0.5)
    for c in range(4):
        v = compact_rows(pack, times01(rz[c].reshape(512, 128), half)).reshape(16, 16, 128)
        if c < 3:
            b3[c, 2:18] = v
        else:
            rho3[2:18] = v

    level3 = Level(16, 128, False, True, gx3, gy3, gz3, m3, w3, ms3, 0)
    coefficients(level3, lambda z: rho3[z], 2, 18)

    def first3(z, _):
        for c in range(3):
            ec[c, z] = w3[c, z] * b3[c, z]
        return 0

    lax.fori_loop(2, 18, first3, 0)

    for src, dst in ((ec, ed), (ed, ec), (ec, ed)):

        def sweep3(z, c, v, a, dst=dst):
            dst[c, z] = v + w3[c, z] * (b3[c, z] - a)

        operate(level3, lambda c, z, src=src: src[c, z], 2, 18, s3, f3, sweep3)

    dup = copy_matrix(128, 128)
    for c in range(3):
        copy_rows(pack, times01(ed[c, pl.ds(wide, 5)].reshape(80, 128), dup))
        for k in range(5):
            for s in range(2):
                z = 2 * k + s
                zb = 2 * wide + z
                inside = w2[0, zb] > 0.0
                up = pack[0, pl.ds(32 * k, 32), :]
                ua[c, z] = ep2[c, zb] + jnp.where(inside, up, 0.0)
    at2 = Level(32, 128, False, True, gx2, gy2, gz2, m2, w2, ms2, 2 * wide)

    def post2a(z, c, v, a):
        zb = z + 2 * wide
        ub[c, z] = v + w2[c, zb] * (b2[c, zb] - a)

    operate(at2, lambda c, z: ua[c, z], 1, 9, s2, f2, post2a)

    def post2b(z, c, v, a):
        zb = z + 2 * wide
        ua[c, z] = v + w2[c, zb] * (b2[c, zb] - a)

    operate(at2, lambda c, z: ub[c, z], 2, 8, s2, f2, post2b)

    wide1 = copy_matrix(128, 256)
    turn = idx[3]
    for c in range(3):
        parts = []
        for k in range(6):
            t = pltpu.roll(ua[c, 2 + k], turn, 0)
            parts += [t[0:8], t[24:32]]
        copy_rows(pack, times01(jnp.concatenate(parts, axis=0), wide1))
        for z in range(1, 11):
            k = z // 2
            inside = w1[0, z + 1] > 0.0
            top = jnp.concatenate([pack[j, pl.ds(32 * k, 16), :] for j in range(2)], axis=1)
            bot = jnp.concatenate([pack[j, pl.ds(32 * k + 24, 8), :] for j in range(2)], axis=1)
            up = jnp.concatenate([top, bot], axis=0)
            va[c, z + 1] = ep1[c, z + 1] + jnp.where(inside, up, 0.0)
    level1 = Level(24, 256, False, False, gx1, gy1, gz1, m1, w1, None, 0)

    def post1a(z, c, v, a):
        vb[c, z] = v + w1[c, z] * (b1[c, z] - a)

    operate(level1, lambda c, z: va[c, z], 3, 11, s1, f1, post1a)

    def post1b(z, c, v, a):
        va[c, z] = v + w1[c, z] * (b1[c, z] - a)

    operate(level1, lambda c, z: vb[c, z], 4, 10, s1, f1, post1b)

    wide0 = copy_matrix(256, 384)
    row = lax.broadcasted_iota(jnp.int32, (8, 256), 0)
    for c in range(3):
        parts = []
        for k in range(6):
            t = va[c, 4 + k]
            parts += [t[0:8], jnp.where(row < 2, t[8:16], pltpu.roll(t[16:24], 4, 0))]
        copy_rows(pack, times01(jnp.concatenate(parts, axis=0), wide0))
        for z in range(-2, 10):
            k = (z + 2) // 2
            inside = w0[0, z + 4] > 0.0
            up = jnp.concatenate([pack[j, pl.ds(32 * k, 24), :] for j in range(3)], axis=1)
            xa[c, z + 4] = ep0[c, z + 4] + jnp.where(inside, up, 0.0)
    level0 = Level(24, 384, True, False, gx0, gy0, gz0, m0, w0, ms0, 0)

    def post0a(z, c, v, a):
        xb[c, z] = v + w0[c, z] * (b0[c, z] - a)

    operate(level0, lambda c, z: xa[c, z], 3, 13, s0, f0, post0a)

    def post0b(z, c, v, a):
        out[c, z - 4] = (v + w0[c, z] * (b0[c, z] - a))[:16]

    operate(level0, lambda c, z: xb[c, z], 4, 12, s0, f0, post0b)


def call(kernel, outs, scratch, args, flops):
    vmem = pl.BlockSpec(memory_space=pltpu.VMEM)
    size = sum(4 * int(a.size) for a in args)
    size += sum(4 * functools.reduce(lambda p, q: p * q, s) for s in outs)
    return pl.pallas_call(
        kernel,
        out_shape=[jax.ShapeDtypeStruct(s, F32) for s in outs],
        in_specs=[pl.BlockSpec(memory_space=pltpu.SMEM)] + [vmem] * (len(args) - 1),
        out_specs=[vmem] * len(outs),
        scratch_shapes=[pltpu.VMEM(s, F32) for s in scratch],
        compiler_params=pltpu.CompilerParams(vmem_limit_bytes=56 * 1024 * 1024),
        cost_estimate=pl.CostEstimate(flops=flops, bytes_accessed=size, transcendentals=0),
    )(*args)


def shards(load, density):
    wide = lax.axis_index("wide")
    narrow = lax.axis_index(NARROW)
    core = lax.axis_index("core")
    idx = jnp.stack([wide, narrow, core, lax.rem(32 - 4 * narrow, 32)]).astype(jnp.int32)

    x0 = jnp.concatenate([load, density[None]], axis=0)
    low = lax.ppermute(x0[:, :, 12:], NARROW, cyclic(8, 1))
    high = lax.ppermute(x0[:, :, :4], NARROW, cyclic(8, -1))
    x1 = jnp.concatenate([x0, high, low], axis=2)
    up = jnp.concatenate([x1[:3, 5:].reshape(9, 24, 384), x1[3, 4:]], axis=0)
    down = jnp.concatenate([x1[:3, :3].reshape(9, 24, 384), x1[3, :4]], axis=0)
    lo = lax.ppermute(up, "wide", cyclic(16, 1))
    hi = lax.ppermute(down, "wide", cyclic(16, -1))
    p0 = (16, 24, 384)
    b0, gx0, gy0, gz0, m0, w0, ms0, ep0, l1 = call(
        down0,
        [(3,) + p0, p0, p0, p0, p0, (3,) + p0, p0, (3,) + p0, (18, 8, 256)],
        [p0, (3,) + p0, (3, 4, 16, 384), (24, 384), (3, 24, 384), (2, 192, 128)],
        [idx, x1, lo, hi],
        10**8,
    )

    low = lax.ppermute(l1, NARROW, cyclic(8, 1))
    high = lax.ppermute(l1, NARROW, cyclic(8, -1))
    own = jnp.concatenate([l1, high, low], axis=1)
    lo = lax.ppermute(own[:17], "wide", cyclic(16, 1))
    hi = lax.ppermute(jnp.concatenate([own[:12], own[13:18]], axis=0), "wide", cyclic(16, -1))
    p1 = (14, 24, 256)
    b1, gx1, gy1, gz1, m1, w1, ep1, chunk = call(
        down1,
        [(3,) + p1, p1, p1, p1, p1, (3,) + p1, (3,) + p1, (8, 384)],
        [p1, (3,) + p1, (4, 2, 8, 256), (24, 256), (3, 24, 256), (1, 64, 128)],
        [idx, own, lo, hi],
        10**8,
    )

    mine = lax.all_to_all(jnp.broadcast_to(chunk[None], (64, 8, 384)), ("wide", "y"), 0, 0)
    other = lax.ppermute(mine, "core", cyclic(2, 1))
    p2, p3 = (40, 32, 128), (20, 16, 128)
    u2 = (3, 10, 32, 128)
    (out,) = call(
        rest,
        [(3, 8, 16, 384)],
        [p2, (3,) + p2, p2, p2, p2, p2, (3,) + p2, p2, (3,) + p2, (3,) + p2]
        + [p3, (3,) + p3, p3, p3, p3, p3, (3,) + p3, p3, (3,) + p3, (3,) + p3]
        + [(4, 16, 32, 128), (8, 128), (3, 512, 128)]
        + [(32, 128), (3, 32, 128), (16, 128), (3, 16, 128), u2, u2]
        + [(3,) + p1, (3,) + p1, (24, 256), (3, 24, 256)]
        + [(3,) + p0, (3,) + p0, (24, 384), (3, 24, 384)],
        [idx, mine, other, b1, gx1, gy1, gz1, m1, w1, ep1, b0, gx0, gy0, gz0, m0, w0, ms0, ep0],
        3 * 10**8,
    )
    return out


def solution(mesh):
    split = Mesh(mesh.devices.reshape(16, 4, 2), ("wide", "y", "core"))
    in_specs = (P(None, "wide", NARROW, None), P("wide", NARROW, None))
    out_specs = P(None, "wide", NARROW, None)
    return jax.shard_map(shards, mesh=split, in_specs=in_specs, out_specs=out_specs, check_vma=False)
```

```python
import functools

import jax
import jax.numpy as jnp
from jax import lax
from jax.experimental import pallas as pl
from jax.experimental.pallas import tpu as pltpu
from jax.sharding import Mesh, PartitionSpec as P

DAMPING = 0.5
MASS = 0.02
NARROW = ("y", "core")
F32 = jnp.float32
BF16 = jnp.bfloat16


def cyclic(count, step):
    return [(i, (i + step) % count) for i in range(count)]


def after_y(v):
    return jnp.concatenate([v[1:], pltpu.roll(v[0], 7, 0)[None]], axis=0)


def before_y(v):
    return jnp.concatenate([pltpu.roll(v[v.shape[0] - 1], 1, 0)[None], v[:-1]], axis=0)


def after_x(v):
    return pltpu.roll(v, v.shape[2] - 1, 2)


def before_x(v):
    return pltpu.roll(v, 1, 2)


def times01(v, matrix):
    high = v.astype(BF16)
    rest = v - high.astype(F32)
    mid = rest.astype(BF16)
    low = (rest - mid.astype(F32)).astype(BF16)
    out = jnp.dot(high, matrix, preferred_element_type=F32)
    out = out + jnp.dot(mid, matrix, preferred_element_type=F32)
    return out + jnp.dot(low, matrix, preferred_element_type=F32)


def pair_sum_matrix(fine, coarse, start, factor):
    i = lax.broadcasted_iota(jnp.int32, (fine, coarse), 0)
    j = lax.broadcasted_iota(jnp.int32, (fine, coarse), 1)
    return jnp.where((i >> 1) + start == j, factor, 0.0).astype(BF16)


def copy_matrix(coarse, fine):
    j = lax.broadcasted_iota(jnp.int32, (coarse, fine), 0)
    i = lax.broadcasted_iota(jnp.int32, (coarse, fine), 1)
    return jnp.where((i >> 1) == j, 1.0, 0.0).astype(BF16)


def lane_tiles(v):
    return [v[..., 128 * k : 128 * (k + 1)] for k in range(v.shape[-1] // 128)]


def join(parts):
    return parts[0] if len(parts) == 1 else jnp.concatenate(parts, axis=-1)


def interleaved(ref, tiles, *at):
    lanes = ref.shape[len(at)]
    return jnp.stack(
        [
            join([ref[(*at, k, pl.ds(t, 8, stride=tiles), slice(None))] for k in range(lanes)])
            for t in range(tiles)
        ]
    )


def to_natural(ref, v, *at):
    tiles = v.shape[0]
    for t in range(tiles):
        for k, part in enumerate(lane_tiles(v[t])):
            ref[(*at, k, pl.ds(t, 8, stride=tiles), slice(None))] = part


def row_pairs(ref, start, *at):
    parts = []
    for k in range(ref.shape[len(at)]):
        a = ref[(*at, k, pl.ds(start, 8, stride=2), slice(None))]
        b = ref[(*at, k, pl.ds(start + 1, 8, stride=2), slice(None))]
        parts.append(a + b)
    return join(parts)


def copy_rows(ref, v, start, *at):
    for k, part in enumerate(lane_tiles(v)):
        ref[(*at, k, pl.ds(start, 8, stride=2), slice(None))] = part
        ref[(*at, k, pl.ds(start + 1, 8, stride=2), slice(None))] = part


class Level:
    def __init__(self, tiles, lanes, wrap_x, wrap_y, gx, gy, gz, m, w, ms):
        self.shape = (tiles, 8, lanes)
        self.wrap_x, self.wrap_y = wrap_x, wrap_y
        self.gx, self.gy, self.gz, self.m, self.w, self.ms = gx, gy, gz, m, w, ms

    def masks(self):
        tiles, _, lanes = self.shape
        t = lax.broadcasted_iota(jnp.int32, self.shape, 0)
        s = lax.broadcasted_iota(jnp.int32, self.shape, 1)
        lane = lax.broadcasted_iota(jnp.int32, self.shape, 2)
        row = tiles * s + t
        return (row == 0, row == 8 * tiles - 1, lane == 0, lane == lanes - 1)

    def after(self, v, axis, masks):
        r = after_y(v) if axis == 1 else after_x(v)
        if axis == 1 and self.wrap_y:
            r = jnp.where(masks[1], 0.0, r)
        if axis == 2 and self.wrap_x:
            r = jnp.where(masks[3], 0.0, r)
        return r

    def before(self, v, axis, masks):
        r = before_y(v) if axis == 1 else before_x(v)
        if axis == 1 and self.wrap_y:
            r = jnp.where(masks[0], 0.0, r)
        if axis == 2 and self.wrap_x:
            r = jnp.where(masks[2], 0.0, r)
        return r


def coefficients(level, rho, lo, hi):
    masks = level.masks()

    def shear(z):
        d = rho[z]
        return d * d * d

    def plane(z, _):
        d = rho[z]
        dn = rho[z + 1]
        g = d * d * d
        gn = dn * dn * dn
        gp = shear(z - 1)
        m = g * (0.5 + d)
        mn = gn * (0.5 + dn)
        gx = 0.5 * (g + after_x(g))
        gy = 0.5 * (g + after_y(g))
        gz = 0.5 * (g + gn)
        total = MASS + gz + 0.5 * (g + gp)
        extra = None
        if level.wrap_x:
            gx = jnp.where(masks[3], 0.0, gx)
            extra = jnp.where(masks[2] | masks[3], 0.5 * g, 0.0)
        if level.wrap_y:
            gy = jnp.where(masks[1], 0.0, gy)
            more = jnp.where(masks[0] | masks[1], 0.5 * g, 0.0)
            extra = more if extra is None else extra + more
        if extra is not None:
            level.ms[z] = MASS + extra
            total = total + extra
        total = total + (gx + before_x(gx)) + (gy + before_y(gy)) + m
        inside = d > 0.0
        level.gx[z] = gx
        level.gy[z] = gy
        level.gz[z] = gz
        level.m[z] = m
        level.w[0, z] = jnp.where(inside, DAMPING / (total + mn), 0.0)
        level.w[1, z] = jnp.where(inside, DAMPING / (total + level.after(m, 1, masks)), 0.0)
        level.w[2, z] = jnp.where(inside, DAMPING / (total + level.after(m, 2, masks)), 0.0)
        return 0

    level.gz[lo - 1] = 0.5 * (shear(lo - 1) + shear(lo))
    last = rho[hi]
    level.m[hi] = last * last * last * (0.5 + last)
    lax.fori_loop(lo, hi, plane, 0)


def operate(level, u, lo, hi, s_ref, f_ref, emit):
    masks = level.masks()

    def stress(z):
        uz, uy, ux = u[0, z], u[1, z], u[2, z]
        div = (uz - u[0, z - 1]) + (uy - level.before(uy, 1, masks))
        return level.m[z] * (div + (ux - level.before(ux, 2, masks)))

    s_ref[...] = stress(lo)
    for c in range(3):
        f_ref[c] = level.gz[lo - 1] * (u[c, lo - 1] - u[c, lo])

    def plane(z, _):
        s = s_ref[...]
        sn = stress(z + 1)
        s_ref[...] = sn
        gx, gy, gz = level.gx[z], level.gy[z], level.gz[z]
        for c in range(3):
            v = u[c, z]
            fz = gz * (v - u[c, z + 1])
            fx = gx * (v - after_x(v))
            fy = gy * (v - after_y(v))
            grad = s - (sn if c == 0 else level.after(s, c, masks))
            mass = MASS if level.ms is None else level.ms[z]
            a = mass * v + (fz - f_ref[c]) + (fx - before_x(fx)) + (fy - before_y(fy)) + grad
            f_ref[c] = fz
            emit(z, c, v, a)
        return 0

    lax.fori_loop(lo, hi, plane, 0)


def scaled(w, b, e, lo, hi):
    def plane(z, _):
        for c in range(3):
            e[c, z] = w[c, z] * b[c, z]
        return 0

    lax.fori_loop(lo, hi, plane, 0)


def smoothed(level, b, src, dst, lo, hi, s_ref, f_ref):
    def emit(z, c, v, a):
        dst[c, z] = v + level.w[c, z] * (b[c, z] - a)

    operate(level, src, lo, hi, s_ref, f_ref, emit)


def in_grid(shape, own, high, n, last):
    t = lax.broadcasted_iota(jnp.int32, shape, 0)
    s = lax.broadcasted_iota(jnp.int32, shape, 1)
    row = shape[0] * s + t
    bad_high = (row >= own) & (row < own + high) & (n == last)
    bad_low = (row >= own + high) & (n == 0)
    return jnp.where(bad_high | bad_low, 0.0, 1.0)


def down0(
    idx, load, dens, rows, lo, hi,
    b, gx, gy, gz, m, w, ms, ep, edge_low, edge_high, l1,
    nat, rho, e1, rz, back, s_ref, f_ref,
):
    wide, narrow = idx[0], idx[1]
    for c in range(4):
        for z in range(8):
            own = dens[z] if c == 3 else load[c, z]
            for k in range(3):
                nat[c, z + 3, k, 0:16] = own[:, 128 * k : 128 * (k + 1)]
                nat[c, z + 3, k, 16:24] = rows[c, z, :, 128 * k : 128 * (k + 1)]
    for c in range(4):
        for j in range(3 if c == 3 else 2):
            for k in range(3):
                nat[c, j + (0 if c == 3 else 1), k] = lo[2 * c + j, :, 128 * k : 128 * (k + 1)]
                nat[c, j + 11, k] = hi[2 * c + j, :, 128 * k : 128 * (k + 1)]
    grid = in_grid((3, 8, 384), 16, 4, narrow, 7)
    below = jnp.where(wide == 0, 0.0, 1.0) * grid
    above = jnp.where(wide == 15, 0.0, 1.0) * grid
    for z in range(14):
        rho[z] = interleaved(nat, 3, 3, z) * (below if z < 3 else above if z > 10 else grid)
    level = Level(3, 384, True, False, gx, gy, gz, m, w, ms)
    coefficients(level, rho, 1, 13)

    def first(z, _):
        for c in range(3):
            v = interleaved(nat, 3, c, z)
            b[c, z] = v
            e1[c, z] = w[c, z] * v
        return 0

    lax.fori_loop(1, 13, first, 0)
    smoothed(level, b, e1, ep, 2, 12, s_ref, f_ref)
    for c in range(3):
        edge_low[c] = ep[c, 4]
        edge_high[c] = ep[c, 9]
    rz[...] = jnp.zeros_like(rz)

    def residual(z, c, v, a):
        k = ((z + 1) >> 1) - 2
        rz[c, k] = rz[c, k] + (b[c, z] - a)

    operate(level, ep, 3, 11, s_ref, f_ref, residual)
    even, odd = [], []
    for c in range(3):
        for k in range(4):
            to_natural(back, rz[c, k], c, k)
            (odd if k % 2 else even).append(row_pairs(back, 0, c, k))
    for k in range(6):
        d = 0.25 * (row_pairs(nat, 0, 3, 2 * k + 1) + row_pairs(nat, 0, 3, 2 * k + 2))
        if k == 0:
            d = d * jnp.where(wide == 0, 0.0, 1.0)
        if k == 5:
            d = d * jnp.where(wide == 15, 0.0, 1.0)
        (odd if k % 2 else even).append(d)
    left = pair_sum_matrix(384, 384, 0, 0.5)
    right = pair_sum_matrix(384, 384, 192, 0.5)
    out = times01(jnp.concatenate(even, axis=0), left)
    out = out + times01(jnp.concatenate(odd, axis=0), right)
    l1[...] = out.reshape(9, 8, 384)


def halves(v):
    lane = lax.broadcasted_iota(jnp.int32, (v.shape[0], 256), 1)
    first = jnp.where(lane < 192, v[:, :256], 0.0)
    second = jnp.where(lane < 192, pltpu.roll(v, 192, 1)[:, :256], 0.0)
    return first, second


def down1(
    idx, own, after, before, lo, hi,
    b, gx, gy, gz, m, w, ep, l2,
    nat, rho, e1, rz, back, s_ref, f_ref,
):
    wide, narrow = idx[0], idx[1]
    row = lax.broadcasted_iota(jnp.int32, (8, 256), 0)

    def put(c, z, r, v):
        for k in range(2):
            nat[c, z, k, pl.ds(r, 8), :] = v[:, 128 * k : 128 * (k + 1)]

    for c in range(4):
        for q in range(3 if c == 3 else 2):
            i = 2 * c + q
            zo = 2 * q - 1 if c == 3 else 2 * q
            for r, ref in ((0, own), (8, after), (16, before)):
                for s, v in enumerate(halves(ref[i])):
                    if 0 <= zo + s < 4:
                        put(c, zo + s + 5, r, v)
            for shift, ref in ((-4, lo), (4, hi)):
                if c < 3:
                    tiles = [halves(ref[pl.ds(16 * i + 8 * r, 8), :]) for r in range(2)]
                else:
                    tiles = [halves(ref[pl.ds(96 + 24 * q + 8 * r, 8), :]) for r in range(3)]
                for s in range(2):
                    z = zo + s + shift
                    if 0 <= z < 4:
                        continue
                    put(c, z + 5, 0, tiles[0][s])
                    if c < 3:
                        put(c, z + 5, 8, jnp.where(row < 4, tiles[1][s], 0.0))
                        put(c, z + 5, 16, jnp.where(row >= 4, tiles[1][s], 0.0))
                    else:
                        put(c, z + 5, 8, tiles[1][s])
                        put(c, z + 5, 16, tiles[2][s])
    grid = in_grid((3, 8, 256), 8, 8, narrow, 7)
    below = jnp.where(wide == 0, 0.0, 1.0) * grid
    above = jnp.where(wide == 15, 0.0, 1.0) * grid
    for z in range(14):
        rho[z] = interleaved(nat, 3, 3, z) * (below if z < 5 else above if z > 8 else grid)
    level = Level(3, 256, False, False, gx, gy, gz, m, w, None)
    coefficients(level, rho, 1, 13)

    def first(z, _):
        for c in range(3):
            v = interleaved(nat, 3, c, z)
            b[c, z] = v
            e1[c, z] = w[c, z] * v
        return 0

    lax.fori_loop(1, 13, first, 0)
    smoothed(level, b, e1, ep, 2, 12, s_ref, f_ref)
    rz[...] = jnp.zeros_like(rz)

    def residual(z, c, v, a):
        k = ((z + 1) >> 1) - 2
        rz[c, k] = rz[c, k] + (b[c, z] - a)

    operate(level, ep, 3, 11, s_ref, f_ref, residual)
    parts = []
    for c in range(3):
        for k in range(4):
            to_natural(back, rz[c, k], c, k)
            parts.append(jnp.where(row < 6, row_pairs(back, 0, c, k), row_pairs(back, 8, c, k)))
    for k in range(6):
        d = [row_pairs(nat, r, 3, 2 * k + 1) + row_pairs(nat, r, 3, 2 * k + 2) for r in (0, 8)]
        parts.append(0.25 * jnp.where(row < 6, d[0], d[1]))
    out = times01(jnp.concatenate(parts, axis=0), pair_sum_matrix(256, 128, 0, 0.5))
    l2[...] = out.reshape(len(parts), 8, 128)


def down2(
    idx, own, lo, lo2, hi, hi2,
    b, gx, gy, gz, m, w, ep, chunk,
    rho, e1, s_ref, f_ref,
):
    wide, narrow = idx[0], idx[1]
    t = lax.broadcasted_iota(jnp.int32, (2, 8, 128), 0)
    s = lax.broadcasted_iota(jnp.int32, (2, 8, 128), 1)
    row = 2 * s + t
    y = 4 * narrow + jnp.where(row < 10, row, row - 16)
    grid = jnp.where((y >= 0) & (y < 32), 1.0, 0.0)

    def rows(ref, i):
        return jnp.stack([ref[i, pl.ds(k, 8, stride=2), :] for k in range(2)])

    for z in range(14):
        if z < 4:
            ref, i = (lo2 if z < 2 else lo), 6 + z % 2
        elif z < 10:
            ref, i = own, 12 + z - 4
        else:
            ref, i = (hi if z < 12 else hi2), 6 + z % 2
        zg = 2 * wide + z - 6
        factor = jnp.where((zg >= 0) & (zg < 32), 1.0, 0.0)
        rho[z] = rows(ref, i) * (grid * factor)
    for c in range(3):
        for z in range(1, 13):
            if z < 5:
                ref, i = (lo2 if z < 3 else lo), 2 * c + (z - 1) % 2
            elif z < 9:
                ref, i = own, 4 * c + z - 5
            else:
                ref, i = (hi if z < 11 else hi2), 2 * c + (z - 9) % 2
            b[c, z] = rows(ref, i)
    level = Level(2, 128, False, False, gx, gy, gz, m, w, None)
    coefficients(level, rho, 1, 13)
    scaled(w, b, e1, 1, 13)
    smoothed(level, b, e1, ep, 2, 12, s_ref, f_ref)
    row8 = lax.broadcasted_iota(jnp.int32, (8, 128), 0)
    sums = [0.25 * (rho[6] + rho[7])]

    def residual(z, c, v, a):
        e1[c, z] = b[c, z] - a

    operate(level, ep, 6, 8, s_ref, f_ref, residual)
    total = jnp.zeros((8, 128), F32)
    for c in range(4):
        v = e1[c, 6] + e1[c, 7] if c < 3 else sums[0]
        v = v[0] + v[1]
        v = pltpu.roll(v, 2 * c, 0) if c else v
        total = jnp.where((row8 >> 1) == c, v, total)
    chunk[...] = times01(total, pair_sum_matrix(128, 128, 0, 0.5))


def rest(
    idx, mine, other, edge0, edge9,
    b2, gx2, gy2, gz2, m2, w2, ep2,
    b1, gx1, gy1, gz1, m1, w1, ep1,
    b0, gx0, gy0, gz0, m0, w0, ms0, ep0,
    out,
    rho3, b3, gx3, gy3, gz3, m3, w3, ms3, ec, ed,
    nat2, nat1, nat0, s3, f3, ua, ub, s2, f2, va, vb, s1, f1, xa, xb, s0, f0,
):
    wide, turn, core = idx[0], idx[2], idx[3]
    zero3 = jnp.zeros((2, 8, 128), F32)
    for z in (1, 18):
        rho3[z] = zero3
    for z in (0, 1, 18, 19):
        for c in range(3):
            ec[c, z] = zero3
            ed[c, z] = zero3

    def unpack(z, _):
        for c in range(4):
            for t in range(2):
                own = mine[z, pl.ds(2 * c + t, 4, stride=8), :]
                off = other[z, pl.ds(2 * c + t, 4, stride=8), :]
                even = jnp.where(core == 0, own, off)
                odd = jnp.where(core == 0, off, own)
                if c < 3:
                    b3[c, z + 2, t, pl.ds(0, 4, stride=2), :] = even
                    b3[c, z + 2, t, pl.ds(1, 4, stride=2), :] = odd
                else:
                    rho3[z + 2, t, pl.ds(0, 4, stride=2), :] = even
                    rho3[z + 2, t, pl.ds(1, 4, stride=2), :] = odd
        return 0

    lax.fori_loop(0, 16, unpack, 0)
    level3 = Level(2, 128, False, True, gx3, gy3, gz3, m3, w3, ms3)
    coefficients(level3, rho3, 2, 18)
    scaled(w3, b3, ec, 2, 18)
    for src, dst in ((ec, ed), (ed, ec), (ec, ed)):
        smoothed(level3, b3, src, dst, 2, 18, s3, f3)

    row8 = lax.broadcasted_iota(jnp.int32, (8, 128), 0)
    parts = []
    for c in range(3):
        for k in range(5):
            v = ed[c, wide + k]
            r = jnp.stack([pltpu.roll(v[0], turn, 0), pltpu.roll(v[1], turn, 0)])
            to_natural(nat2, r, c, k)
            parts.append(jnp.where(row8 < 4, nat2[c, k, 0, 0:8], nat2[c, k, 0, 8:16]))
    up = times01(jnp.concatenate(parts, axis=0), copy_matrix(128, 128))
    for c in range(3):
        for k in range(5):
            tile = up[8 * (5 * c + k) : 8 * (5 * c + k) + 8]
            both = jnp.stack([tile, tile])
            for z in (2 * k + 2, 2 * k + 3):
                ua[c, z] = jnp.where(w2[0, z] > 0.0, ep2[c, z] + both, 0.0)
    level2 = Level(2, 128, False, False, gx2, gy2, gz2, m2, w2, None)
    smoothed(level2, b2, ua, ub, 3, 11, s2, f2)
    smoothed(level2, b2, ub, ua, 4, 10, s2, f2)

    parts = []
    for c in range(3):
        for k in range(6):
            to_natural(nat2, ua[c, 4 + k], c, k)
            parts += [nat2[c, k, 0, 0:8], nat2[c, k, 0, 8:16]]
    up = times01(jnp.concatenate(parts, axis=0), copy_matrix(128, 256))
    for c in range(3):
        for k in range(6):
            at = 16 * (6 * c + k)
            copy_rows(nat1, up[at + 8 : at + 16], 8, c, k)
            copy_rows(nat1, up[at : at + 8], 0, c, k)
            both = interleaved(nat1, 3, c, k)
            for z in (2 * k + 1, 2 * k + 2):
                if 2 <= z < 12:
                    va[c, z] = jnp.where(w1[0, z] > 0.0, ep1[c, z] + both, 0.0)
    level1 = Level(3, 256, False, False, gx1, gy1, gz1, m1, w1, None)
    smoothed(level1, b1, va, vb, 3, 11, s1, f1)
    smoothed(level1, b1, vb, va, 4, 10, s1, f1)

    row8 = lax.broadcasted_iota(jnp.int32, (8, 256), 0)
    parts = []
    for c in range(3):
        for k in range(6):
            to_natural(nat1, va[c, 4 + k], c, k)
            t = [join([nat1[c, k, j, 8 * r : 8 * r + 8] for j in range(2)]) for r in range(3)]
            parts += [t[0], jnp.where(row8 < 2, t[1], pltpu.roll(t[2], 4, 0))]
    up = times01(jnp.concatenate(parts, axis=0), copy_matrix(256, 384))
    for c in range(3):
        for k in range(6):
            at = 16 * (6 * c + k)
            copy_rows(nat0, up[at + 8 : at + 16], 16, c, k)
            copy_rows(nat0, up[at : at + 8], 0, c, k)
            both = interleaved(nat0, 3, c, k)
            for z in (2 * k + 1, 2 * k + 2):
                old = edge0[c] if z == 1 else edge9[c] if z == 12 else ep0[c, z]
                xa[c, z] = jnp.where(w0[0, z] > 0.0, old + both, 0.0)
    level0 = Level(3, 384, True, False, gx0, gy0, gz0, m0, w0, ms0)
    smoothed(level0, b0, xa, xb, 2, 12, s0, f0)

    def last(z, c, v, a):
        to_natural(nat0, v + w0[c, z] * (b0[c, z] - a), c, 0)
        for k in range(3):
            out[c, z - 3, :, 128 * k : 128 * (k + 1)] = nat0[c, 0, k, 0:16]

    operate(level0, xb, 3, 11, s0, f0, last)


def call(kernel, outs, scratch, args, flops, mib):
    vmem = pl.BlockSpec(memory_space=pltpu.VMEM)
    size = sum(4 * int(a.size) for a in args)
    size += sum(4 * functools.reduce(lambda p, q: p * q, s) for s in outs)
    return pl.pallas_call(
        kernel,
        out_shape=[jax.ShapeDtypeStruct(s, F32) for s in outs],
        in_specs=[pl.BlockSpec(memory_space=pltpu.SMEM)] + [vmem] * (len(args) - 1),
        out_specs=[vmem] * len(outs),
        scratch_shapes=[pltpu.VMEM(s, F32) for s in scratch],
        compiler_params=pltpu.CompilerParams(vmem_limit_bytes=mib * 1024 * 1024),
        cost_estimate=pl.CostEstimate(flops=flops, bytes_accessed=size, transcendentals=0),
    )(*args)


def shards(load, density):
    wide = lax.axis_index("wide")
    narrow = lax.axis_index(NARROW)
    turn = lax.rem(8 - narrow, 8)
    idx = jnp.stack([wide, narrow, turn, lax.axis_index("core")]).astype(jnp.int32)

    def next_rows(v):
        return lax.ppermute(v, NARROW, cyclic(8, -1))

    def previous_rows(v):
        return lax.ppermute(v, NARROW, cyclic(8, 1))

    def above(v, steps=1):
        return lax.ppermute(v, "wide", cyclic(16, -steps))

    def below(v, steps=1):
        return lax.ppermute(v, "wide", cyclic(16, steps))

    low = previous_rows(jnp.concatenate([load[:, :, 12:], density[None, :, 12:]], axis=0))
    high = next_rows(jnp.concatenate([load[:, :, :4], density[None, :, :4]], axis=0))
    rows = jnp.concatenate([high, low], axis=2)

    def planes(lz, dz):
        l = jnp.concatenate([load[:, lz], rows[:3, lz]], axis=2).reshape(6, 24, 384)
        d = jnp.concatenate([density[dz], rows[3, dz]], axis=1)
        return jnp.concatenate([l, d], axis=0)

    lo = below(planes(slice(6, 8), slice(5, 8)))
    hi = above(planes(slice(0, 2), slice(0, 3)))
    p0, c0 = (14, 3, 8, 384), (3, 8, 384)
    b0, gx0, gy0, gz0, m0, w0, ms0, ep0, edge_low, edge_high, l1 = call(
        down0,
        [(3,) + p0, p0, p0, p0, p0, (3,) + p0, p0, (3,) + p0, (3,) + c0, (3,) + c0, (9, 8, 384)],
        [(4, 14, 3, 24, 128), p0, (3,) + p0, (3, 4) + c0, (3, 4, 3, 24, 128), c0, (3,) + c0],
        [idx, load, density, rows, lo, hi],
        10**7,
        17,
    )

    after, before = next_rows(l1), previous_rows(l1)
    bz = jnp.concatenate([l1[:6], after[:6, :4], before[:6, 4:]], axis=1).reshape(96, 384)
    dz = jnp.concatenate([l1[6:], after[6:], before[6:]], axis=1).reshape(72, 384)
    slab = jnp.concatenate([bz, dz], axis=0)
    lo, hi = below(slab), above(slab)
    edge_low, edge_high, _ = lax.optimization_barrier((edge_low, edge_high, slab))
    edge9, edge0 = above(edge_low), below(edge_high)
    p1, c1 = (14, 3, 8, 256), (3, 8, 256)
    b1, gx1, gy1, gz1, m1, w1, ep1, l2 = call(
        down1,
        [(3,) + p1, p1, p1, p1, p1, (3,) + p1, (3,) + p1, (18, 8, 128)],
        [(4, 14, 2, 24, 128), p1, (3,) + p1, (3, 4) + c1, (3, 4, 2, 24, 128), c1, (3,) + c1],
        [idx, l1, after, before, lo, hi],
        10**7,
        10,
    )

    after, before = next_rows(l2), previous_rows(l2)
    own = jnp.concatenate([l2[:, :4], after[:, :6], before[:, 6:], before[:, :4]], axis=1)
    up = jnp.concatenate([own[4 * c : 4 * c + 2] for c in range(3)] + [own[12:14]], axis=0)
    down = jnp.concatenate([own[4 * c + 2 : 4 * c + 4] for c in range(3)] + [own[16:18]], axis=0)
    lo, hi, lo2, hi2 = below(up), above(down), below(up, 2), above(down, 2)
    p2, c2 = (14, 2, 8, 128), (2, 8, 128)
    b2, gx2, gy2, gz2, m2, w2, ep2, chunk = call(
        down2,
        [(3,) + p2, p2, p2, p2, p2, (3,) + p2, (3,) + p2, (8, 128)],
        [p2, (3,) + p2, c2, (3,) + c2],
        [idx, own, lo, lo2, hi, hi2],
        10**6,
        5,
    )

    everywhere = jnp.broadcast_to(chunk[None], (64, 8, 128))
    mine = lax.all_to_all(everywhere, ("wide", "y"), 0, 0).reshape(16, 32, 128)
    other = lax.ppermute(mine, "core", cyclic(2, 1))
    p3, c3 = (20, 2, 8, 128), (2, 8, 128)
    (out,) = call(
        rest,
        [(3, 8, 16, 384)],
        [p3, (3,) + p3, p3, p3, p3, p3, (3,) + p3, p3, (3,) + p3, (3,) + p3]
        + [(3, 6, 1, 16, 128), (3, 6, 2, 24, 128), (3, 6, 3, 32, 128)]
        + [c3, (3,) + c3, (3,) + p2, (3,) + p2, c2, (3,) + c2]
        + [(3,) + p1, (3,) + p1, c1, (3,) + c1, (3,) + p0, (3,) + p0, c0, (3,) + c0],
        [idx, mine, other, edge0, edge9]
        + [b2, gx2, gy2, gz2, m2, w2, ep2]
        + [b1, gx1, gy1, gz1, m1, w1, ep1]
        + [b0, gx0, gy0, gz0, m0, w0, ms0, ep0],
        10**8,
        28,
    )
    return out


def solution(mesh):
    split = Mesh(mesh.devices.reshape(16, 4, 2), ("wide",) + NARROW)
    in_specs = (P(None, "wide", NARROW, None), P("wide", NARROW, None))
    out_specs = P(None, "wide", NARROW, None)
    return jax.shard_map(shards, mesh=split, in_specs=in_specs, out_specs=out_specs, check_vma=False)
```

```python
import functools

import jax
import jax.numpy as jnp
from jax import lax
from jax.experimental import pallas as pl
from jax.experimental.pallas import tpu as pltpu
from jax.sharding import Mesh, PartitionSpec as P

DAMPING = 0.5
MASS = 0.02
NARROW = ("y", "core")
F32 = jnp.float32
BF16 = jnp.bfloat16


def cyclic(count, step):
    return [(i, (i + step) % count) for i in range(count)]


def after_y(v):
    return jnp.concatenate([v[1:], pltpu.roll(v[0], 7, 0)[None]], axis=0)


def before_y(v):
    return jnp.concatenate([pltpu.roll(v[v.shape[0] - 1], 1, 0)[None], v[:-1]], axis=0)


def after_x(v):
    return pltpu.roll(v, v.shape[2] - 1, 2)


def before_x(v):
    return pltpu.roll(v, 1, 2)


def times01(v, matrix):
    high = v.astype(BF16)
    rest = v - high.astype(F32)
    mid = rest.astype(BF16)
    low = (rest - mid.astype(F32)).astype(BF16)
    out = jnp.dot(high, matrix, preferred_element_type=F32)
    out = out + jnp.dot(mid, matrix, preferred_element_type=F32)
    return out + jnp.dot(low, matrix, preferred_element_type=F32)


def pair_sum_matrix(fine, coarse, start, factor):
    i = lax.broadcasted_iota(jnp.int32, (fine, coarse), 0)
    j = lax.broadcasted_iota(jnp.int32, (fine, coarse), 1)
    return jnp.where((i >> 1) + start == j, factor, 0.0).astype(BF16)


def copy_matrix(coarse, fine):
    j = lax.broadcasted_iota(jnp.int32, (coarse, fine), 0)
    i = lax.broadcasted_iota(jnp.int32, (coarse, fine), 1)
    return jnp.where((i >> 1) == j, 1.0, 0.0).astype(BF16)


def lane_tiles(v):
    return [v[..., 128 * k : 128 * (k + 1)] for k in range(v.shape[-1] // 128)]


def join(parts):
    return parts[0] if len(parts) == 1 else jnp.concatenate(parts, axis=-1)


def interleaved(ref, tiles, *at):
    lanes = ref.shape[len(at)]
    return jnp.stack(
        [
            join([ref[(*at, k, pl.ds(t, 8, stride=tiles), slice(None))] for k in range(lanes)])
            for t in range(tiles)
        ]
    )


def to_natural(ref, v, *at):
    tiles = v.shape[0]
    for t in range(tiles):
        for k, part in enumerate(lane_tiles(v[t])):
            ref[(*at, k, pl.ds(t, 8, stride=tiles), slice(None))] = part


def row_pairs(ref, start, *at):
    parts = []
    for k in range(ref.shape[len(at)]):
        a = ref[(*at, k, pl.ds(start, 8, stride=2), slice(None))]
        b = ref[(*at, k, pl.ds(start + 1, 8, stride=2), slice(None))]
        parts.append(a + b)
    return join(parts)


def copy_rows(ref, v, start, *at):
    for k, part in enumerate(lane_tiles(v)):
        ref[(*at, k, pl.ds(start, 8, stride=2), slice(None))] = part
        ref[(*at, k, pl.ds(start + 1, 8, stride=2), slice(None))] = part


UNROLL = {2: 5, 6: 5, 9: 5}


def planes_loop(level, lo, hi, body):
    tiles, _, lanes = level.shape
    unroll = UNROLL[tiles * (lanes // 128)]
    while (hi - lo) % unroll:
        unroll -= 1
    lax.fori_loop(lo, hi, body, 0, unroll=unroll)


class Level:
    def __init__(self, tiles, lanes, wrap_x, wrap_y, gx, gxm, gy, gz, m, w, ms):
        self.shape = (tiles, 8, lanes)
        self.wrap_x, self.wrap_y = wrap_x, wrap_y
        self.gx, self.gxm, self.gy, self.gz = gx, gxm, gy, gz
        self.m, self.w, self.ms = m, w, ms

    def masks(self):
        tiles, _, lanes = self.shape
        t = lax.broadcasted_iota(jnp.int32, self.shape, 0)
        s = lax.broadcasted_iota(jnp.int32, self.shape, 1)
        lane = lax.broadcasted_iota(jnp.int32, self.shape, 2)
        row = tiles * s + t
        return (row == 0, row == 8 * tiles - 1, lane == 0, lane == lanes - 1)

    def after(self, v, axis, masks):
        r = after_y(v) if axis == 1 else after_x(v)
        if axis == 1 and self.wrap_y:
            r = jnp.where(masks[1], 0.0, r)
        if axis == 2 and self.wrap_x:
            r = jnp.where(masks[3], 0.0, r)
        return r

    def before(self, v, axis, masks):
        r = before_y(v) if axis == 1 else before_x(v)
        if axis == 1 and self.wrap_y:
            r = jnp.where(masks[0], 0.0, r)
        if axis == 2 and self.wrap_x:
            r = jnp.where(masks[2], 0.0, r)
        return r


def coefficients(level, rho, lo, hi):
    masks = level.masks()

    def shear(z):
        d = rho[z]
        return d * d * d

    def plane(z, _):
        d = rho[z]
        dn = rho[z + 1]
        g = d * d * d
        gn = dn * dn * dn
        gp = shear(z - 1)
        m = g * (0.5 + d)
        mn = gn * (0.5 + dn)
        gx = 0.5 * (g + after_x(g))
        gxm = 0.5 * (g + before_x(g))
        gy = 0.5 * (g + after_y(g))
        gz = 0.5 * (g + gn)
        total = MASS + gz + 0.5 * (g + gp)
        extra = None
        if level.wrap_x:
            gx = jnp.where(masks[3], 0.0, gx)
            gxm = jnp.where(masks[2], 0.0, gxm)
            extra = jnp.where(masks[2] | masks[3], 0.5 * g, 0.0)
        if level.wrap_y:
            gy = jnp.where(masks[1], 0.0, gy)
            more = jnp.where(masks[0] | masks[1], 0.5 * g, 0.0)
            extra = more if extra is None else extra + more
        if extra is not None:
            level.ms[z] = MASS + extra
            total = total + extra
        total = total + (gx + gxm) + (gy + before_y(gy)) + m
        inside = d > 0.0
        level.gx[z] = gx
        level.gxm[z] = gxm
        level.gy[z] = gy
        level.gz[z] = gz
        level.m[z] = m
        level.w[0, z] = jnp.where(inside, DAMPING / (total + mn), 0.0)
        level.w[1, z] = jnp.where(inside, DAMPING / (total + level.after(m, 1, masks)), 0.0)
        level.w[2, z] = jnp.where(inside, DAMPING / (total + level.after(m, 2, masks)), 0.0)
        return 0

    level.gz[lo - 1] = 0.5 * (shear(lo - 1) + shear(lo))
    last = rho[hi]
    level.m[hi] = last * last * last * (0.5 + last)
    planes_loop(level, lo, hi, plane)


def operate(level, u, lo, hi, s_ref, f_ref, emit):
    masks = level.masks()

    def stress(z):
        uz, uy, ux = u[0, z], u[1, z], u[2, z]
        div = (uz - u[0, z - 1]) + (uy - level.before(uy, 1, masks))
        return level.m[z] * (div + (ux - level.before(ux, 2, masks)))

    s_ref[...] = stress(lo)
    for c in range(3):
        f_ref[c] = level.gz[lo - 1] * (u[c, lo - 1] - u[c, lo])

    def plane(z, _):
        s = s_ref[...]
        sn = stress(z + 1)
        s_ref[...] = sn
        gx, gxm, gy, gz = level.gx[z], level.gxm[z], level.gy[z], level.gz[z]
        for c in range(3):
            v = u[c, z]
            fz = gz * (v - u[c, z + 1])
            fx = gx * (v - after_x(v)) + gxm * (v - before_x(v))
            fy = gy * (v - after_y(v))
            grad = s - (sn if c == 0 else level.after(s, c, masks))
            mass = MASS if level.ms is None else level.ms[z]
            a = mass * v + (fz - f_ref[c]) + fx + (fy - before_y(fy)) + grad
            f_ref[c] = fz
            emit(z, c, v, a)
        return 0

    planes_loop(level, lo, hi, plane)


def scaled(w, b, e, lo, hi):
    def plane(z, _):
        for c in range(3):
            e[c, z] = w[c, z] * b[c, z]
        return 0

    unroll = next(k for k in (4, 5, 3, 2, 1) if (hi - lo) % k == 0)
    lax.fori_loop(lo, hi, plane, 0, unroll=unroll)


def smoothed(level, b, src, dst, lo, hi, s_ref, f_ref):
    def emit(z, c, v, a):
        dst[c, z] = v + level.w[c, z] * (b[c, z] - a)

    operate(level, src, lo, hi, s_ref, f_ref, emit)


def in_grid(shape, own, high, n, last):
    t = lax.broadcasted_iota(jnp.int32, shape, 0)
    s = lax.broadcasted_iota(jnp.int32, shape, 1)
    row = shape[0] * s + t
    bad_high = (row >= own) & (row < own + high) & (n == last)
    bad_low = (row >= own + high) & (n == 0)
    return jnp.where(bad_high | bad_low, 0.0, 1.0)


def down0(
    idx, load, dens, rows, lo, hi,
    b, gx, gxm, gy, gz, m, w, ms, ep, edge_low, edge_high, l1,
    nat, rho, e1, rz, back, s_ref, f_ref,
):
    wide, narrow = idx[0], idx[1]
    for c in range(4):
        for z in range(8):
            own = dens[z] if c == 3 else load[c, z]
            for k in range(3):
                nat[c, z + 3, k, 0:16] = own[:, 128 * k : 128 * (k + 1)]
                nat[c, z + 3, k, 16:24] = rows[c, z, :, 128 * k : 128 * (k + 1)]
    for c in range(4):
        for j in range(3 if c == 3 else 2):
            for k in range(3):
                nat[c, j + (0 if c == 3 else 1), k] = lo[2 * c + j, :, 128 * k : 128 * (k + 1)]
                nat[c, j + 11, k] = hi[2 * c + j, :, 128 * k : 128 * (k + 1)]
    grid = in_grid((3, 8, 384), 16, 4, narrow, 7)
    below = jnp.where(wide == 0, 0.0, 1.0) * grid
    above = jnp.where(wide == 15, 0.0, 1.0) * grid
    for z in range(14):
        rho[z] = interleaved(nat, 3, 3, z) * (below if z < 3 else above if z > 10 else grid)
    level = Level(3, 384, True, False, gx, gxm, gy, gz, m, w, ms)
    coefficients(level, rho, 1, 13)

    def first(z, _):
        for c in range(3):
            v = interleaved(nat, 3, c, z)
            b[c, z] = v
            e1[c, z] = w[c, z] * v
        return 0

    lax.fori_loop(1, 13, first, 0, unroll=3)
    smoothed(level, b, e1, ep, 2, 12, s_ref, f_ref)
    for c in range(3):
        for t in range(3):
            for k in range(3):
                edge_low[c, t, k] = ep[c, 4, t, :, 128 * k : 128 * (k + 1)]
                edge_high[c, t, k] = ep[c, 9, t, :, 128 * k : 128 * (k + 1)]
    rz[...] = jnp.zeros_like(rz)

    def residual(z, c, v, a):
        k = ((z + 1) >> 1) - 2
        rz[c, k] = rz[c, k] + (b[c, z] - a)

    operate(level, ep, 3, 11, s_ref, f_ref, residual)
    even, odd = [], []
    for c in range(3):
        for k in range(4):
            to_natural(back, rz[c, k], c, k)
            (odd if k % 2 else even).append(row_pairs(back, 0, c, k))
    for k in range(6):
        d = 0.25 * (row_pairs(nat, 0, 3, 2 * k + 1) + row_pairs(nat, 0, 3, 2 * k + 2))
        if k == 0:
            d = d * jnp.where(wide == 0, 0.0, 1.0)
        if k == 5:
            d = d * jnp.where(wide == 15, 0.0, 1.0)
        (odd if k % 2 else even).append(d)
    left = pair_sum_matrix(384, 384, 0, 0.5)
    right = pair_sum_matrix(384, 384, 192, 0.5)
    out = times01(jnp.concatenate(even, axis=0), left)
    out = out + times01(jnp.concatenate(odd, axis=0), right)
    l1[...] = out.reshape(9, 8, 384)


def halves(v):
    lane = lax.broadcasted_iota(jnp.int32, (v.shape[0], 256), 1)
    first = jnp.where(lane < 192, v[:, :256], 0.0)
    second = jnp.where(lane < 192, pltpu.roll(v, 192, 1)[:, :256], 0.0)
    return first, second


def down1(
    idx, own, after, before, lo, hi,
    b, gx, gxm, gy, gz, m, w, ep, l2,
    nat, rho, e1, rz, back, s_ref, f_ref,
):
    wide, narrow = idx[0], idx[1]
    row = lax.broadcasted_iota(jnp.int32, (8, 256), 0)

    def put(c, z, r, v):
        for k in range(2):
            nat[c, z, k, pl.ds(r, 8), :] = v[:, 128 * k : 128 * (k + 1)]

    for c in range(4):
        for q in range(3 if c == 3 else 2):
            i = 2 * c + q
            zo = 2 * q - 1 if c == 3 else 2 * q
            for r, ref in ((0, own), (8, after), (16, before)):
                for s, v in enumerate(halves(ref[i])):
                    if 0 <= zo + s < 4:
                        put(c, zo + s + 5, r, v)
            for shift, ref in ((-4, lo), (4, hi)):
                if c < 3:
                    tiles = [halves(ref[pl.ds(16 * i + 8 * r, 8), :]) for r in range(2)]
                else:
                    tiles = [halves(ref[pl.ds(96 + 24 * q + 8 * r, 8), :]) for r in range(3)]
                for s in range(2):
                    z = zo + s + shift
                    if 0 <= z < 4:
                        continue
                    put(c, z + 5, 0, tiles[0][s])
                    if c < 3:
                        put(c, z + 5, 8, jnp.where(row < 4, tiles[1][s], 0.0))
                        put(c, z + 5, 16, jnp.where(row >= 4, tiles[1][s], 0.0))
                    else:
                        put(c, z + 5, 8, tiles[1][s])
                        put(c, z + 5, 16, tiles[2][s])
    grid = in_grid((3, 8, 256), 8, 8, narrow, 7)
    below = jnp.where(wide == 0, 0.0, 1.0) * grid
    above = jnp.where(wide == 15, 0.0, 1.0) * grid
    for z in range(14):
        rho[z] = interleaved(nat, 3, 3, z) * (below if z < 5 else above if z > 8 else grid)
    level = Level(3, 256, False, False, gx, gxm, gy, gz, m, w, None)
    coefficients(level, rho, 1, 13)

    def first(z, _):
        for c in range(3):
            v = interleaved(nat, 3, c, z)
            b[c, z] = v
            e1[c, z] = w[c, z] * v
        return 0

    lax.fori_loop(1, 13, first, 0, unroll=3)
    smoothed(level, b, e1, ep, 2, 12, s_ref, f_ref)
    rz[...] = jnp.zeros_like(rz)

    def residual(z, c, v, a):
        k = ((z + 1) >> 1) - 2
        rz[c, k] = rz[c, k] + (b[c, z] - a)

    operate(level, ep, 3, 11, s_ref, f_ref, residual)
    parts = []
    for c in range(3):
        for k in range(4):
            to_natural(back, rz[c, k], c, k)
            parts.append(jnp.where(row < 6, row_pairs(back, 0, c, k), row_pairs(back, 8, c, k)))
    for k in range(6):
        d = [row_pairs(nat, r, 3, 2 * k + 1) + row_pairs(nat, r, 3, 2 * k + 2) for r in (0, 8)]
        parts.append(0.25 * jnp.where(row < 6, d[0], d[1]))
    out = times01(jnp.concatenate(parts, axis=0), pair_sum_matrix(256, 128, 0, 0.5))
    l2[...] = out.reshape(len(parts), 8, 128)


def down2(
    idx, own, lo, lo2, hi, hi2,
    b, gx, gxm, gy, gz, m, w, ep, chunk,
    rho, e1, s_ref, f_ref,
):
    wide, narrow = idx[0], idx[1]
    t = lax.broadcasted_iota(jnp.int32, (2, 8, 128), 0)
    s = lax.broadcasted_iota(jnp.int32, (2, 8, 128), 1)
    row = 2 * s + t
    y = 4 * narrow + jnp.where(row < 10, row, row - 16)
    grid = jnp.where((y >= 0) & (y < 32), 1.0, 0.0)

    def rows(ref, i):
        if ref is own:
            return jnp.stack([ref[i, pl.ds(k, 8, stride=2), :] for k in range(2)])
        return jnp.stack([ref[pl.ds(16 * i + k, 8, stride=2), :] for k in range(2)])

    for z in range(14):
        if z < 4:
            ref, i = (lo2 if z < 2 else lo), 6 + z % 2
        elif z < 10:
            ref, i = own, 12 + z - 4
        else:
            ref, i = (hi if z < 12 else hi2), 6 + z % 2
        zg = 2 * wide + z - 6
        factor = jnp.where((zg >= 0) & (zg < 32), 1.0, 0.0)
        rho[z] = rows(ref, i) * (grid * factor)
    for c in range(3):
        for z in range(1, 13):
            if z < 5:
                ref, i = (lo2 if z < 3 else lo), 2 * c + (z - 1) % 2
            elif z < 9:
                ref, i = own, 4 * c + z - 5
            else:
                ref, i = (hi if z < 11 else hi2), 2 * c + (z - 9) % 2
            b[c, z] = rows(ref, i)
    level = Level(2, 128, False, False, gx, gxm, gy, gz, m, w, None)
    coefficients(level, rho, 1, 13)
    scaled(w, b, e1, 1, 13)
    smoothed(level, b, e1, ep, 2, 12, s_ref, f_ref)
    row8 = lax.broadcasted_iota(jnp.int32, (8, 128), 0)
    sums = [0.25 * (rho[6] + rho[7])]

    def residual(z, c, v, a):
        e1[c, z] = b[c, z] - a

    operate(level, ep, 6, 8, s_ref, f_ref, residual)
    total = jnp.zeros((8, 128), F32)
    for c in range(4):
        v = e1[c, 6] + e1[c, 7] if c < 3 else sums[0]
        v = v[0] + v[1]
        v = pltpu.roll(v, 2 * c, 0) if c else v
        total = jnp.where((row8 >> 1) == c, v, total)
    chunk[...] = times01(total, pair_sum_matrix(128, 128, 0, 0.5))


def rest(
    idx, mine, other, lo, hi,
    b2, gx2, gxm2, gy2, gz2, m2, w2, ep2,
    b1, gx1, gxm1, gy1, gz1, m1, w1, ep1,
    b0, gx0, gxm0, gy0, gz0, m0, w0, ms0, ep0,
    out,
    rho3, b3, gx3, gxm3, gy3, gz3, m3, w3, ms3, ec, ed,
    nat2, nat1, nat0, s3, f3, ua, ub, s2, f2, va, vb, s1, f1, xa, xb, s0, f0,
):
    wide, turn, core = idx[0], idx[2], idx[3]
    zero3 = jnp.zeros((2, 8, 128), F32)
    for z in (1, 18):
        rho3[z] = zero3
    for z in (0, 1, 18, 19):
        for c in range(3):
            ec[c, z] = zero3
            ed[c, z] = zero3

    def unpack(z, _):
        for c in range(4):
            for t in range(2):
                own = mine[z, pl.ds(2 * c + t, 4, stride=8), :]
                off = other[z, pl.ds(2 * c + t, 4, stride=8), :]
                ref = rho3.at[z + 2, t] if c == 3 else b3.at[c, z + 2, t]
                ref[pl.ds(0, 4, stride=2), :] = jnp.where(core == 0, own, off)
                ref[pl.ds(1, 4, stride=2), :] = jnp.where(core == 0, off, own)
        return 0

    lax.fori_loop(0, 16, unpack, 0, unroll=4)
    level3 = Level(2, 128, False, True, gx3, gxm3, gy3, gz3, m3, w3, ms3)
    coefficients(level3, rho3, 2, 18)
    scaled(w3, b3, ec, 2, 18)
    for src, dst in ((ec, ed), (ed, ec), (ec, ed)):
        smoothed(level3, b3, src, dst, 2, 18, s3, f3)

    row8 = lax.broadcasted_iota(jnp.int32, (8, 128), 0)
    parts = []
    for c in range(3):
        for k in range(5):
            v = ed[c, wide + k]
            r = jnp.stack([pltpu.roll(v[0], turn, 0), pltpu.roll(v[1], turn, 0)])
            to_natural(nat2, r, c, k)
            parts.append(jnp.where(row8 < 4, nat2[c, k, 0, 0:8], nat2[c, k, 0, 8:16]))
    up = times01(jnp.concatenate(parts, axis=0), copy_matrix(128, 128))
    for c in range(3):
        for k in range(5):
            tile = up[8 * (5 * c + k) : 8 * (5 * c + k) + 8]
            both = jnp.stack([tile, tile])
            for z in (2 * k + 2, 2 * k + 3):
                ua[c, z] = jnp.where(w2[0, z] > 0.0, ep2[c, z] + both, 0.0)
    level2 = Level(2, 128, False, False, gx2, gxm2, gy2, gz2, m2, w2, None)
    smoothed(level2, b2, ua, ub, 3, 11, s2, f2)
    smoothed(level2, b2, ub, ua, 4, 10, s2, f2)

    parts = []
    for c in range(3):
        for k in range(6):
            to_natural(nat2, ua[c, 4 + k], c, k)
            parts += [nat2[c, k, 0, 0:8], nat2[c, k, 0, 8:16]]
    up = times01(jnp.concatenate(parts, axis=0), copy_matrix(128, 256))
    for c in range(3):
        for k in range(6):
            at = 16 * (6 * c + k)
            copy_rows(nat1, up[at + 8 : at + 16], 8, c, k)
            copy_rows(nat1, up[at : at + 8], 0, c, k)
            both = interleaved(nat1, 3, c, k)
            for z in (2 * k + 1, 2 * k + 2):
                if 2 <= z < 12:
                    va[c, z] = jnp.where(w1[0, z] > 0.0, ep1[c, z] + both, 0.0)
    level1 = Level(3, 256, False, False, gx1, gxm1, gy1, gz1, m1, w1, None)
    smoothed(level1, b1, va, vb, 3, 11, s1, f1)
    smoothed(level1, b1, vb, va, 4, 10, s1, f1)

    def edge(ref, c):
        at = [[128 + 8 * (9 * c + 3 * t + k) for k in range(3)] for t in range(3)]
        return jnp.stack([join([ref[r : r + 8, :] for r in line]) for line in at])

    row8 = lax.broadcasted_iota(jnp.int32, (8, 256), 0)
    parts = []
    for c in range(3):
        for k in range(6):
            to_natural(nat1, va[c, 4 + k], c, k)
            t = [join([nat1[c, k, j, 8 * r : 8 * r + 8] for j in range(2)]) for r in range(3)]
            parts += [t[0], jnp.where(row8 < 2, t[1], pltpu.roll(t[2], 4, 0))]
    up = times01(jnp.concatenate(parts, axis=0), copy_matrix(256, 384))
    for c in range(3):
        for k in range(6):
            at = 16 * (6 * c + k)
            copy_rows(nat0, up[at + 8 : at + 16], 16, c, k)
            copy_rows(nat0, up[at : at + 8], 0, c, k)
            both = interleaved(nat0, 3, c, k)
            for z in (2 * k + 1, 2 * k + 2):
                old = edge(lo, c) if z == 1 else edge(hi, c) if z == 12 else ep0[c, z]
                xa[c, z] = jnp.where(w0[0, z] > 0.0, old + both, 0.0)
    level0 = Level(3, 384, True, False, gx0, gxm0, gy0, gz0, m0, w0, ms0)
    smoothed(level0, b0, xa, xb, 2, 12, s0, f0)

    def last(z, c, v, a):
        to_natural(nat0, v + w0[c, z] * (b0[c, z] - a), c, 0)
        for k in range(3):
            out[c, z - 3, :, 128 * k : 128 * (k + 1)] = nat0[c, 0, k, 0:16]

    operate(level0, xb, 3, 11, s0, f0, last)


def call(kernel, outs, scratch, args, flops, mib):
    vmem = pl.BlockSpec(memory_space=pltpu.VMEM)
    size = sum(4 * int(a.size) for a in args)
    size += sum(4 * functools.reduce(lambda p, q: p * q, s) for s in outs)
    return pl.pallas_call(
        kernel,
        out_shape=[jax.ShapeDtypeStruct(s, F32) for s in outs],
        in_specs=[pl.BlockSpec(memory_space=pltpu.SMEM)] + [vmem] * (len(args) - 1),
        out_specs=[vmem] * len(outs),
        scratch_shapes=[pltpu.VMEM(s, F32) for s in scratch],
        compiler_params=pltpu.CompilerParams(vmem_limit_bytes=mib * 1024 * 1024),
        cost_estimate=pl.CostEstimate(flops=flops, bytes_accessed=size, transcendentals=0),
    )(*args)


def shards(load, density):
    wide = lax.axis_index("wide")
    narrow = lax.axis_index(NARROW)
    turn = lax.rem(8 - narrow, 8)
    idx = jnp.stack([wide, narrow, turn, lax.axis_index("core")]).astype(jnp.int32)

    def next_rows(v):
        return lax.ppermute(v, NARROW, cyclic(8, -1))

    def previous_rows(v):
        return lax.ppermute(v, NARROW, cyclic(8, 1))

    def above(v, steps=1):
        return lax.ppermute(v, "wide", cyclic(16, -steps))

    def below(v, steps=1):
        return lax.ppermute(v, "wide", cyclic(16, steps))

    low = previous_rows(jnp.concatenate([load[:, :, 12:], density[None, :, 12:]], axis=0))
    high = next_rows(jnp.concatenate([load[:, :, :4], density[None, :, :4]], axis=0))
    rows = jnp.concatenate([high, low], axis=2)

    def planes(lz, dz):
        l = jnp.concatenate([load[:, lz], rows[:3, lz]], axis=2).reshape(6, 24, 384)
        d = jnp.concatenate([density[dz], rows[3, dz]], axis=1)
        return jnp.concatenate([l, d], axis=0)

    lo = below(planes(slice(6, 8), slice(5, 8)))
    hi = above(planes(slice(0, 2), slice(0, 3)))
    p0, c0 = (14, 3, 8, 384), (3, 8, 384)
    b0, gx0, gxm0, gy0, gz0, m0, w0, ms0, ep0, edge_low, edge_high, l1 = call(
        down0,
        [(3,) + p0, p0, p0, p0, p0, p0, (3,) + p0, p0, (3,) + p0, (3, 3, 3, 8, 128), (3, 3, 3, 8, 128), (9, 8, 384)],
        [(4, 14, 3, 24, 128), p0, (3,) + p0, (3, 4) + c0, (3, 4, 3, 24, 128), c0, (3,) + c0],
        [idx, load, density, rows, lo, hi],
        10**7,
        17,
    )

    after, before = next_rows(l1), previous_rows(l1)
    bz = jnp.concatenate([l1[:6], after[:6, :4], before[:6, 4:]], axis=1).reshape(96, 384)
    dz = jnp.concatenate([l1[6:], after[6:], before[6:]], axis=1).reshape(72, 384)
    slab = jnp.concatenate([bz, dz], axis=0)
    lo, hi = below(slab), above(slab)
    p1, c1 = (14, 3, 8, 256), (3, 8, 256)
    b1, gx1, gxm1, gy1, gz1, m1, w1, ep1, l2 = call(
        down1,
        [(3,) + p1, p1, p1, p1, p1, p1, (3,) + p1, (3,) + p1, (18, 8, 128)],
        [(4, 14, 2, 24, 128), p1, (3,) + p1, (3, 4) + c1, (3, 4, 2, 24, 128), c1, (3,) + c1],
        [idx, l1, after, before, lo, hi],
        10**7,
        10,
    )

    after, before = next_rows(l2), previous_rows(l2)
    own = jnp.concatenate([l2[:, :4], after[:, :6], before[:, 6:], before[:, :4]], axis=1)
    up = jnp.concatenate([own[4 * c : 4 * c + 2] for c in range(3)] + [own[12:14]], axis=0)
    down = jnp.concatenate([own[4 * c + 2 : 4 * c + 4] for c in range(3)] + [own[16:18]], axis=0)
    up, down = up.reshape(128, 128), down.reshape(128, 128)
    lo = below(jnp.concatenate([up, edge_high.reshape(216, 128)], axis=0))
    hi = above(jnp.concatenate([down, edge_low.reshape(216, 128)], axis=0))
    lo2, hi2 = below(up, 2), above(down, 2)
    p2, c2 = (14, 2, 8, 128), (2, 8, 128)
    b2, gx2, gxm2, gy2, gz2, m2, w2, ep2, chunk = call(
        down2,
        [(3,) + p2, p2, p2, p2, p2, p2, (3,) + p2, (3,) + p2, (8, 128)],
        [p2, (3,) + p2, c2, (3,) + c2],
        [idx, own, lo, lo2, hi, hi2],
        10**6,
        5,
    )

    everywhere = jnp.broadcast_to(chunk[None], (64, 8, 128))
    mine = lax.all_to_all(everywhere, ("wide", "y"), 0, 0).reshape(16, 32, 128)
    other = lax.ppermute(mine, "core", cyclic(2, 1))
    p3, c3 = (20, 2, 8, 128), (2, 8, 128)
    (out,) = call(
        rest,
        [(3, 8, 16, 384)],
        [p3, (3,) + p3, p3, p3, p3, p3, p3, (3,) + p3, p3, (3,) + p3, (3,) + p3]
        + [(3, 6, 1, 16, 128), (3, 6, 2, 24, 128), (3, 6, 3, 32, 128)]
        + [c3, (3,) + c3, (3,) + p2, (3,) + p2, c2, (3,) + c2]
        + [(3,) + p1, (3,) + p1, c1, (3,) + c1, (3,) + p0, (3,) + p0, c0, (3,) + c0],
        [idx, mine, other, lo, hi]
        + [b2, gx2, gxm2, gy2, gz2, m2, w2, ep2]
        + [b1, gx1, gxm1, gy1, gz1, m1, w1, ep1]
        + [b0, gx0, gxm0, gy0, gz0, m0, w0, ms0, ep0],
        10**8,
        28,
    )
    return out


def solution(mesh):
    split = Mesh(mesh.devices.reshape(16, 4, 2), ("wide",) + NARROW)
    in_specs = (P(None, "wide", NARROW, None), P("wide", NARROW, None))
    out_specs = P(None, "wide", NARROW, None)
    return jax.shard_map(shards, mesh=split, in_specs=in_specs, out_specs=out_specs, check_vma=False)
```

```python
import functools

import jax
import jax.numpy as jnp
from jax import lax
from jax.experimental import pallas as pl
from jax.experimental.pallas import tpu as pltpu
from jax.sharding import Mesh, PartitionSpec as P

DAMPING = 0.5
MASS = 0.02
NARROW = ("y", "core")
F32 = jnp.float32
BF16 = jnp.bfloat16


def cyclic(count, step):
    return [(i, (i + step) % count) for i in range(count)]


def after_y(v):
    return jnp.concatenate([v[1:], pltpu.roll(v[0], 7, 0)[None]], axis=0)


def before_y(v):
    return jnp.concatenate([pltpu.roll(v[v.shape[0] - 1], 1, 0)[None], v[:-1]], axis=0)


def after_x(v):
    return pltpu.roll(v, v.shape[2] - 1, 2)


def before_x(v):
    return pltpu.roll(v, 1, 2)


def times01(v, matrix):
    high = v.astype(BF16)
    rest = v - high.astype(F32)
    mid = rest.astype(BF16)
    low = (rest - mid.astype(F32)).astype(BF16)
    out = jnp.dot(high, matrix, preferred_element_type=F32)
    out = out + jnp.dot(mid, matrix, preferred_element_type=F32)
    return out + jnp.dot(low, matrix, preferred_element_type=F32)


def pair_sum_matrix(fine, coarse, start, factor):
    i = lax.broadcasted_iota(jnp.int32, (fine, coarse), 0)
    j = lax.broadcasted_iota(jnp.int32, (fine, coarse), 1)
    return jnp.where((i >> 1) + start == j, factor, 0.0).astype(BF16)


def copy_matrix(coarse, fine):
    j = lax.broadcasted_iota(jnp.int32, (coarse, fine), 0)
    i = lax.broadcasted_iota(jnp.int32, (coarse, fine), 1)
    return jnp.where((i >> 1) == j, 1.0, 0.0).astype(BF16)


def lane_tiles(v):
    return [v[..., 128 * k : 128 * (k + 1)] for k in range(v.shape[-1] // 128)]


def join(parts):
    return parts[0] if len(parts) == 1 else jnp.concatenate(parts, axis=-1)


def interleaved(ref, tiles, *at):
    lanes = ref.shape[len(at)]
    return jnp.stack(
        [
            join([ref[(*at, k, pl.ds(t, 8, stride=tiles), slice(None))] for k in range(lanes)])
            for t in range(tiles)
        ]
    )


def to_natural(ref, v, *at):
    tiles = v.shape[0]
    for t in range(tiles):
        for k, part in enumerate(lane_tiles(v[t])):
            ref[(*at, k, pl.ds(t, 8, stride=tiles), slice(None))] = part


def row_pairs(ref, start, *at):
    parts = []
    for k in range(ref.shape[len(at)]):
        a = ref[(*at, k, pl.ds(start, 8, stride=2), slice(None))]
        b = ref[(*at, k, pl.ds(start + 1, 8, stride=2), slice(None))]
        parts.append(a + b)
    return join(parts)


def copy_rows(ref, v, start, *at):
    for k, part in enumerate(lane_tiles(v)):
        ref[(*at, k, pl.ds(start, 8, stride=2), slice(None))] = part
        ref[(*at, k, pl.ds(start + 1, 8, stride=2), slice(None))] = part


UNROLL = {2: 5, 4: 5, 6: 5, 9: 5}


def planes_loop(level, lo, hi, body):
    tiles, _, lanes = level.shape
    unroll = UNROLL[tiles * (lanes // 128)]
    while (hi - lo) % unroll:
        unroll -= 1
    lax.fori_loop(lo, hi, body, 0, unroll=unroll)


class Level:
    def __init__(self, tiles, lanes, wrap_x, wrap_y, gx, gxm, gy, gz, m, w, ms):
        self.shape = (tiles, 8, lanes)
        self.wrap_x, self.wrap_y = wrap_x, wrap_y
        self.gx, self.gxm, self.gy, self.gz = gx, gxm, gy, gz
        self.m, self.w, self.ms = m, w, ms

    def masks(self):
        tiles, _, lanes = self.shape
        t = lax.broadcasted_iota(jnp.int32, self.shape, 0)
        s = lax.broadcasted_iota(jnp.int32, self.shape, 1)
        lane = lax.broadcasted_iota(jnp.int32, self.shape, 2)
        row = tiles * s + t
        return (row == 0, row == 8 * tiles - 1, lane == 0, lane == lanes - 1)

    def after(self, v, axis, masks):
        r = after_y(v) if axis == 1 else after_x(v)
        if axis == 1 and self.wrap_y:
            r = jnp.where(masks[1], 0.0, r)
        if axis == 2 and self.wrap_x:
            r = jnp.where(masks[3], 0.0, r)
        return r

    def before(self, v, axis, masks):
        r = before_y(v) if axis == 1 else before_x(v)
        if axis == 1 and self.wrap_y:
            r = jnp.where(masks[0], 0.0, r)
        if axis == 2 and self.wrap_x:
            r = jnp.where(masks[2], 0.0, r)
        return r


def coefficients(level, rho, lo, hi):
    masks = level.masks()

    def shear(z):
        d = rho[z]
        return d * d * d

    def plane(z, _):
        d = rho[z]
        dn = rho[z + 1]
        g = d * d * d
        gn = dn * dn * dn
        gp = shear(z - 1)
        m = g * (0.5 + d)
        mn = gn * (0.5 + dn)
        gx = 0.5 * (g + after_x(g))
        gxm = 0.5 * (g + before_x(g))
        gy = 0.5 * (g + after_y(g))
        gz = 0.5 * (g + gn)
        total = MASS + gz + 0.5 * (g + gp)
        extra = None
        if level.wrap_x:
            gx = jnp.where(masks[3], 0.0, gx)
            gxm = jnp.where(masks[2], 0.0, gxm)
            extra = jnp.where(masks[2] | masks[3], 0.5 * g, 0.0)
        if level.wrap_y:
            gy = jnp.where(masks[1], 0.0, gy)
            more = jnp.where(masks[0] | masks[1], 0.5 * g, 0.0)
            extra = more if extra is None else extra + more
        if extra is not None:
            level.ms[z] = MASS + extra
            total = total + extra
        total = total + (gx + gxm) + (gy + before_y(gy)) + m
        inside = d > 0.0
        level.gx[z] = gx
        level.gxm[z] = gxm
        level.gy[z] = gy
        level.gz[z] = gz
        level.m[z] = m
        level.w[0, z] = jnp.where(inside, DAMPING / (total + mn), 0.0)
        level.w[1, z] = jnp.where(inside, DAMPING / (total + level.after(m, 1, masks)), 0.0)
        level.w[2, z] = jnp.where(inside, DAMPING / (total + level.after(m, 2, masks)), 0.0)
        return 0

    level.gz[lo - 1] = 0.5 * (shear(lo - 1) + shear(lo))
    last = rho[hi]
    level.m[hi] = last * last * last * (0.5 + last)
    planes_loop(level, lo, hi, plane)


def operate(level, u, lo, hi, s_ref, f_ref, emit):
    masks = level.masks()

    def stress(z):
        uz, uy, ux = u[0, z], u[1, z], u[2, z]
        div = (uz - u[0, z - 1]) + (uy - level.before(uy, 1, masks))
        return level.m[z] * (div + (ux - level.before(ux, 2, masks)))

    s_ref[...] = stress(lo)
    for c in range(3):
        f_ref[c] = level.gz[lo - 1] * (u[c, lo - 1] - u[c, lo])

    def plane(z, _):
        s = s_ref[...]
        sn = stress(z + 1)
        s_ref[...] = sn
        gx, gxm, gy, gz = level.gx[z], level.gxm[z], level.gy[z], level.gz[z]
        for c in range(3):
            v = u[c, z]
            fz = gz * (v - u[c, z + 1])
            fx = gx * (v - after_x(v)) + gxm * (v - before_x(v))
            fy = gy * (v - after_y(v))
            grad = s - (sn if c == 0 else level.after(s, c, masks))
            mass = MASS if level.ms is None else level.ms[z]
            a = mass * v + (fz - f_ref[c]) + fx + (fy - before_y(fy)) + grad
            f_ref[c] = fz
            emit(z, c, v, a)
        return 0

    planes_loop(level, lo, hi, plane)


def scaled(w, b, e, lo, hi):
    def plane(z, _):
        for c in range(3):
            e[c, z] = w[c, z] * b[c, z]
        return 0

    unroll = next(k for k in (4, 5, 3, 2, 1) if (hi - lo) % k == 0)
    lax.fori_loop(lo, hi, plane, 0, unroll=unroll)


def smoothed(level, b, src, dst, lo, hi, s_ref, f_ref):
    def emit(z, c, v, a):
        dst[c, z] = v + level.w[c, z] * (b[c, z] - a)

    operate(level, src, lo, hi, s_ref, f_ref, emit)


def in_grid(shape, own, high, n, last):
    t = lax.broadcasted_iota(jnp.int32, shape, 0)
    s = lax.broadcasted_iota(jnp.int32, shape, 1)
    row = shape[0] * s + t
    bad_high = (row >= own) & (row < own + high) & (n == last)
    bad_low = (row >= own + high) & (n == 0)
    return jnp.where(bad_high | bad_low, 0.0, 1.0)


def down0(
    idx, load, dens, rows, lo, hi,
    b, gx, gxm, gy, gz, m, w, ms, ep, edge_low, edge_high, l1,
    nat, rho, e1, rz, back, s_ref, f_ref,
):
    wide, narrow = idx[0], idx[1]
    for c in range(4):
        first = 0 if c == 3 else 1
        for z in range(first, 14 - first):
            if z < 3:
                own = lo[2 * c + z - first]
            elif z < 11:
                own = dens[z - 3] if c == 3 else load[c, z - 3]
            else:
                own = hi[2 * c + z - 11]
            halo = rows[12 * c + z - first]
            for k in range(3):
                nat[c, z, k, 0:16] = own[:, 128 * k : 128 * (k + 1)]
                nat[c, z, k, 16:24] = halo[:, 128 * k : 128 * (k + 1)]
    grid = in_grid((3, 8, 384), 16, 4, narrow, 7)
    below = jnp.where(wide == 0, 0.0, 1.0) * grid
    above = jnp.where(wide == 15, 0.0, 1.0) * grid
    for z in range(14):
        rho[z] = interleaved(nat, 3, 3, z) * (below if z < 3 else above if z > 10 else grid)
    level = Level(3, 384, True, False, gx, gxm, gy, gz, m, w, ms)
    coefficients(level, rho, 1, 13)

    def first(z, _):
        for c in range(3):
            v = interleaved(nat, 3, c, z)
            b[c, z] = v
            e1[c, z] = w[c, z] * v
        return 0

    lax.fori_loop(1, 13, first, 0, unroll=3)
    smoothed(level, b, e1, ep, 2, 12, s_ref, f_ref)
    for c in range(3):
        edge_low[c] = ep[c, 4]
        edge_high[c] = ep[c, 9]
    rz[...] = jnp.zeros_like(rz)

    def residual(z, c, v, a):
        k = ((z + 1) >> 1) - 2
        rz[c, k] = rz[c, k] + (b[c, z] - a)

    operate(level, ep, 3, 11, s_ref, f_ref, residual)
    even, odd = [], []
    for c in range(3):
        for k in range(4):
            to_natural(back, rz[c, k], c, k)
            (odd if k % 2 else even).append(row_pairs(back, 0, c, k))
    for k in range(6):
        d = 0.25 * (row_pairs(nat, 0, 3, 2 * k + 1) + row_pairs(nat, 0, 3, 2 * k + 2))
        if k == 0:
            d = d * jnp.where(wide == 0, 0.0, 1.0)
        if k == 5:
            d = d * jnp.where(wide == 15, 0.0, 1.0)
        (odd if k % 2 else even).append(d)
    left = pair_sum_matrix(384, 384, 0, 0.5)
    right = pair_sum_matrix(384, 384, 192, 0.5)
    out = times01(jnp.concatenate(even, axis=0), left)
    out = out + times01(jnp.concatenate(odd, axis=0), right)
    l1[...] = out.reshape(9, 8, 384)


def halves(v):
    lane = lax.broadcasted_iota(jnp.int32, (v.shape[0], 256), 1)
    first = jnp.where(lane < 192, v[:, :256], 0.0)
    second = jnp.where(lane < 192, pltpu.roll(v, 192, 1)[:, :256], 0.0)
    return first, second


def down1(
    idx, own, lo, hi, after, before,
    b, gx, gxm, gy, gz, m, w, ep, chunk,
    nat, rho, e1, rz, back, s_ref, f_ref,
):
    wide, narrow = idx[0], idx[1]
    row = lax.broadcasted_iota(jnp.int32, (8, 256), 0)

    def put(c, z, r, v):
        for k in range(2):
            nat[c, z, k, pl.ds(r, 8), :] = v[:, 128 * k : 128 * (k + 1)]

    for c in range(4):
        for q in range(3 if c == 3 else 2):
            i = 2 * c + q
            zo = 2 * q - 1 if c == 3 else 2 * q
            for source, (shift, ref) in enumerate(((0, own), (-4, lo), (4, hi))):
                tiles = [halves(ref[i])]
                j = 6 * source + i
                at = j // 2 if c < 3 else 9 + 3 * source + q
                for k, ref in enumerate((after, before)):
                    v = ref[at]
                    tiles.append(halves(pltpu.roll(v, 4, 0) if c < 3 and j % 2 != k else v))
                for s in range(2):
                    z = zo + s + shift
                    if (0 <= z < 4) != (shift == 0):
                        continue
                    put(c, z + 5, 0, tiles[0][s])
                    if c < 3:
                        put(c, z + 5, 8, jnp.where(row < 4, tiles[1][s], 0.0))
                        put(c, z + 5, 16, jnp.where(row >= 4, tiles[2][s], 0.0))
                    else:
                        put(c, z + 5, 8, tiles[1][s])
                        put(c, z + 5, 16, tiles[2][s])
    grid = in_grid((3, 8, 256), 8, 8, narrow, 7)
    below = jnp.where(wide == 0, 0.0, 1.0) * grid
    above = jnp.where(wide == 15, 0.0, 1.0) * grid
    for z in range(14):
        rho[z] = interleaved(nat, 3, 3, z) * (below if z < 5 else above if z > 8 else grid)
    level = Level(3, 256, False, False, gx, gxm, gy, gz, m, w, None)
    coefficients(level, rho, 1, 13)

    def first(z, _):
        for c in range(3):
            v = interleaved(nat, 3, c, z)
            b[c, z] = v
            e1[c, z] = w[c, z] * v
        return 0

    lax.fori_loop(1, 13, first, 0, unroll=3)
    smoothed(level, b, e1, ep, 2, 12, s_ref, f_ref)
    rz[...] = jnp.zeros_like(rz)

    def residual(z, c, v, a):
        k = ((z + 1) >> 1) - 3
        rz[c, k] = rz[c, k] + (b[c, z] - a)

    operate(level, ep, 5, 9, s_ref, f_ref, residual)
    parts = []
    for c in range(3):
        for k in range(2):
            to_natural(back, rz[c, k], c, k)
            parts.append(row_pairs(back, 0, c, k))
    for k in range(2):
        d = row_pairs(nat, 0, 3, 2 * k + 5) + row_pairs(nat, 0, 3, 2 * k + 6)
        parts.append(0.25 * d)
    out = times01(jnp.concatenate(parts, axis=0), pair_sum_matrix(256, 128, 0, 0.5))
    row8 = lax.broadcasted_iota(jnp.int32, (8, 128), 0)
    lane = lax.broadcasted_iota(jnp.int32, (8, 128), 1)
    four = []
    for c in range(4):
        low, high = out[16 * c : 16 * c + 8], out[16 * c + 8 : 16 * c + 16]
        four.append(jnp.where(row8 < 4, low, pltpu.roll(high, 4, 0)))
    for c in range(3):
        d = four[3] if c == 3 else pltpu.roll(four[3], 96 - 32 * c, 1)
        chunk[c] = jnp.where(lane < 96, four[c], d)


def rest(
    idx, mine, other, lo, hi,
    b1, gx1, gxm1, gy1, gz1, m1, w1, ep1,
    b0, gx0, gxm0, gy0, gz0, m0, w0, ms0, ep0,
    out,
    rho2, b2, gx2, gxm2, gy2, gz2, m2, w2, ms2, ea, ep2,
    rho3, b3, gx3, gxm3, gy3, gz3, m3, w3, ms3, ec, ed,
    rz, nat2, nat1, nat0, s3, f3, ua, ub, s2, f2, va, vb, s1, f1, xa, xb, s0, f0,
):
    wide, narrow = idx[0], idx[1]
    core = narrow & 1
    zero2 = jnp.zeros((4, 8, 128), F32)
    zero3 = jnp.zeros((2, 8, 128), F32)

    def outside(i, _):
        z = jnp.where(i < 4, i, i + 32)
        for ref in (rho2, gx2, gxm2, gy2, gz2, m2, ms2):
            ref[z] = zero2
        for ref in (b2, w2, ea, ep2):
            for c in range(3):
                ref[c, z] = zero2
        return 0

    lax.fori_loop(0, 8, outside, 0)
    for z in (1, 18):
        rho3[z] = zero3
    for z in (0, 1, 18, 19):
        for c in range(3):
            ec[c, z] = zero3
            ed[c, z] = zero3

    lane = lax.broadcasted_iota(jnp.int32, (4, 8, 128), 2)

    def unpack(w, _):
        for c in range(3):
            for r in range(8):
                own = mine[w, pl.ds(8 * c + r, 4, stride=24), :]
                off = other[w, pl.ds(8 * c + r, 4, stride=24), :]
                ref = ea.at[c, 2 * w + 4 + r // 4, r % 4]
                ref[pl.ds(0, 4, stride=2), :] = jnp.where(core == 0, own, off)
                ref[pl.ds(1, 4, stride=2), :] = jnp.where(core == 0, off, own)
        return 0

    lax.fori_loop(0, 16, unpack, 0)

    def split(z, _):
        d = jnp.zeros((4, 8, 128), F32)
        for c in range(3):
            v = ea[c, z]
            b2[c, z] = jnp.where(lane < 96, v, 0.0)
            moved = pltpu.roll(v, 32 + 32 * c, 2) if c < 3 else v
            d = jnp.where((lane >> 5) == c, moved, d)
        rho2[z] = d
        return 0

    lax.fori_loop(4, 36, split, 0, unroll=4)

    level2 = Level(4, 128, False, True, gx2, gxm2, gy2, gz2, m2, w2, ms2)
    coefficients(level2, rho2, 4, 36)
    scaled(w2, b2, ea, 4, 36)
    smoothed(level2, b2, ea, ep2, 4, 36, s2, f2)
    rz[...] = jnp.zeros_like(rz)

    def residual(z, c, v, a):
        r = b2[c, z] - a
        k = (z >> 1) - 2
        rz[c, k] = rz[c, k] + jnp.stack([r[0] + r[1], r[2] + r[3]])

    operate(level2, ep2, 4, 36, s2, f2, residual)

    def coarse_density(z, _):
        d = 0.25 * (rho2[2 * z + 4] + rho2[2 * z + 5])
        rz[3, z] = jnp.stack([d[0] + d[1], d[2] + d[3]])
        return 0

    lax.fori_loop(0, 16, coarse_density, 0, unroll=4)
    half = pair_sum_matrix(128, 128, 0, 0.5)
    for c in range(4):
        v = times01(rz[c].reshape(256, 128), half).reshape(16, 2, 8, 128)
        if c < 3:
            b3[c, 2:18] = v
        else:
            rho3[2:18] = v

    level3 = Level(2, 128, False, True, gx3, gxm3, gy3, gz3, m3, w3, ms3)
    coefficients(level3, rho3, 2, 18)
    scaled(w3, b3, ec, 2, 18)
    for src, dst in ((ec, ed), (ed, ec), (ec, ed)):
        smoothed(level3, b3, src, dst, 2, 18, s3, f3)

    near = pl.ds(2 * wide, 10)
    gx2, gxm2, gy2, gz2, m2, ms2 = (v.at[near] for v in (gx2, gxm2, gy2, gz2, m2, ms2))
    b2, w2, ep2 = (v.at[:, near] for v in (b2, w2, ep2))
    parts = [ed[c, wide + k].reshape(16, 128) for c in range(3) for k in range(5)]
    up = times01(jnp.concatenate(parts, axis=0), copy_matrix(128, 128))
    for c in range(3):
        for k in range(5):
            at = 16 * (5 * c + k)
            t = [up[at : at + 8], up[at + 8 : at + 16]]
            both = jnp.stack([t[0], t[0], t[1], t[1]])
            for z in (2 * k, 2 * k + 1):
                ua[c, z] = jnp.where(w2[0, z] > 0.0, ep2[c, z] + both, 0.0)
    at2 = Level(4, 128, False, True, gx2, gxm2, gy2, gz2, m2, w2, ms2)
    smoothed(at2, b2, ua, ub, 1, 9, s2, f2)
    smoothed(at2, b2, ub, ua, 2, 8, s2, f2)

    turn = (8 - narrow) & 7
    parts = []
    for c in range(3):
        for k in range(6):
            v = ua[c, 2 + k]
            to_natural(nat2, jnp.stack([pltpu.roll(v[t], turn, 0) for t in range(4)]), c, k)
            parts += [nat2[c, k, 0, 0:8], nat2[c, k, 0, 24:32]]
    up = times01(jnp.concatenate(parts, axis=0), copy_matrix(128, 256))
    for c in range(3):
        for k in range(6):
            at = 16 * (6 * c + k)
            copy_rows(nat1, up[at + 8 : at + 16], 8, c, k)
            copy_rows(nat1, up[at : at + 8], 0, c, k)
            both = interleaved(nat1, 3, c, k)
            for z in (2 * k + 1, 2 * k + 2):
                if 2 <= z < 12:
                    va[c, z] = jnp.where(w1[0, z] > 0.0, ep1[c, z] + both, 0.0)
    level1 = Level(3, 256, False, False, gx1, gxm1, gy1, gz1, m1, w1, None)
    smoothed(level1, b1, va, vb, 3, 11, s1, f1)
    smoothed(level1, b1, vb, va, 4, 10, s1, f1)

    row8 = lax.broadcasted_iota(jnp.int32, (8, 256), 0)
    parts = []
    for c in range(3):
        for k in range(6):
            to_natural(nat1, va[c, 4 + k], c, k)
            t = [join([nat1[c, k, j, 8 * r : 8 * r + 8] for j in range(2)]) for r in range(3)]
            parts += [t[0], jnp.where(row8 < 2, t[1], pltpu.roll(t[2], 4, 0))]
    up = times01(jnp.concatenate(parts, axis=0), copy_matrix(256, 384))
    for c in range(3):
        for k in range(6):
            at = 16 * (6 * c + k)
            copy_rows(nat0, up[at + 8 : at + 16], 16, c, k)
            copy_rows(nat0, up[at : at + 8], 0, c, k)
            both = interleaved(nat0, 3, c, k)
            for z in (2 * k + 1, 2 * k + 2):
                if z in (1, 12):
                    ref = lo if z == 1 else hi
                    old = jnp.stack([ref[9 + 3 * c + t] for t in range(3)])
                else:
                    old = ep0[c, z]
                xa[c, z] = jnp.where(w0[0, z] > 0.0, old + both, 0.0)
    level0 = Level(3, 384, True, False, gx0, gxm0, gy0, gz0, m0, w0, ms0)
    smoothed(level0, b0, xa, xb, 2, 12, s0, f0)

    def last(z, c, v, a):
        to_natural(nat0, v + w0[c, z] * (b0[c, z] - a), c, 0)
        for k in range(3):
            out[c, z - 3, :, 128 * k : 128 * (k + 1)] = nat0[c, 0, k, 0:16]

    operate(level0, xb, 3, 11, s0, f0, last)


def call(kernel, outs, scratch, args, flops, mib):
    vmem = pl.BlockSpec(memory_space=pltpu.VMEM)
    size = sum(4 * int(a.size) for a in args)
    size += sum(4 * functools.reduce(lambda p, q: p * q, s) for s in outs)
    return pl.pallas_call(
        kernel,
        out_shape=[jax.ShapeDtypeStruct(s, F32) for s in outs],
        in_specs=[pl.BlockSpec(memory_space=pltpu.SMEM)] + [vmem] * (len(args) - 1),
        out_specs=[vmem] * len(outs),
        scratch_shapes=[pltpu.VMEM(s, F32) for s in scratch],
        compiler_params=pltpu.CompilerParams(vmem_limit_bytes=mib * 1024 * 1024),
        cost_estimate=pl.CostEstimate(flops=flops, bytes_accessed=size, transcendentals=0),
    )(*args)


def shards(load, density):
    wide = lax.axis_index("wide")
    narrow = lax.axis_index(NARROW)
    idx = jnp.stack([wide, narrow]).astype(jnp.int32)
    load, density, idx = lax.optimization_barrier((load, density, idx))

    def next_rows(v):
        return lax.ppermute(v, NARROW, cyclic(8, -1))

    def previous_rows(v):
        return lax.ppermute(v, NARROW, cyclic(8, 1))

    def above(v, steps=1):
        return lax.ppermute(v, "wide", cyclic(16, -steps))

    def below(v, steps=1):
        return lax.ppermute(v, "wide", cyclic(16, steps))

    lo = below(jnp.concatenate([load[:, 6:].reshape(6, 16, 384), density[5:]], axis=0))
    hi = above(jnp.concatenate([load[:, :2].reshape(6, 16, 384), density[:3]], axis=0))

    def rows_of(at):
        parts = []
        for c in range(4):
            own = density if c == 3 else load[c]
            end = 9 if c == 3 else 2 * c + 2
            parts += [lo[2 * c : end, at], own[:, at], hi[2 * c : end, at]]
        return jnp.concatenate(parts, axis=0)

    low, high = previous_rows(rows_of(slice(12, 16))), next_rows(rows_of(slice(0, 4)))
    rows = jnp.concatenate([high, low], axis=1)
    p0, c0 = (14, 3, 8, 384), (3, 8, 384)
    b0, gx0, gxm0, gy0, gz0, m0, w0, ms0, ep0, edge_low, edge_high, l1 = call(
        down0,
        [(3,) + p0, p0, p0, p0, p0, p0, (3,) + p0, p0, (3,) + p0, (3,) + c0, (3,) + c0, (9, 8, 384)],
        [(4, 14, 3, 24, 128), p0, (3,) + p0, (3, 4) + c0, (3, 4, 3, 24, 128), c0, (3,) + c0],
        [idx, load, density, rows, lo, hi],
        10**7,
        17,
    )

    lo = below(jnp.concatenate([l1, edge_high.reshape(9, 8, 384)], axis=0))
    hi = above(jnp.concatenate([l1, edge_low.reshape(9, 8, 384)], axis=0))

    def level1_rows(at):
        b = [jnp.concatenate([v[0:6:2, at], v[1:6:2, at]], axis=1) for v in (l1, lo, hi)]
        return jnp.concatenate(b + [v[6:9] for v in (l1, lo, hi)], axis=0)

    after, before = next_rows(level1_rows(slice(0, 4))), previous_rows(level1_rows(slice(4, 8)))
    p1, c1 = (14, 3, 8, 256), (3, 8, 256)
    b1, gx1, gxm1, gy1, gz1, m1, w1, ep1, chunk = call(
        down1,
        [(3,) + p1, p1, p1, p1, p1, p1, (3,) + p1, (3,) + p1, (3, 8, 128)],
        [(4, 14, 2, 24, 128), p1, (3,) + p1, (3, 4) + c1, (3, 4, 2, 24, 128), c1, (3,) + c1],
        [idx, l1, lo, hi, after, before],
        10**7,
        10,
    )

    chunks = jnp.broadcast_to(chunk[None], (64, 3, 8, 128))
    mine = lax.all_to_all(chunks, ("wide", "y"), 0, 0).reshape(16, 96, 128)
    other = lax.ppermute(mine, "core", cyclic(2, 1))
    p2, c2 = (40, 4, 8, 128), (4, 8, 128)
    u2 = (3, 10, 4, 8, 128)
    p3, c3 = (20, 2, 8, 128), (2, 8, 128)
    (out,) = call(
        rest,
        [(3, 8, 16, 384)],
        [p2, (3,) + p2, p2, p2, p2, p2, p2, (3,) + p2, p2, (3,) + p2, (3,) + p2]
        + [p3, (3,) + p3, p3, p3, p3, p3, p3, (3,) + p3, p3, (3,) + p3, (3,) + p3]
        + [(4, 16, 2, 8, 128), (3, 6, 1, 32, 128), (3, 6, 2, 24, 128), (3, 6, 3, 32, 128)]
        + [c3, (3,) + c3, u2, u2, c2, (3,) + c2]
        + [(3,) + p1, (3,) + p1, c1, (3,) + c1, (3,) + p0, (3,) + p0, c0, (3,) + c0],
        [idx, mine, other, lo, hi]
        + [b1, gx1, gxm1, gy1, gz1, m1, w1, ep1]
        + [b0, gx0, gxm0, gy0, gz0, m0, w0, ms0, ep0],
        10**8,
        40,
    )
    return out


def solution(mesh):
    split = Mesh(mesh.devices.reshape(16, 4, 2), ("wide",) + NARROW)
    in_specs = (P(None, "wide", NARROW, None), P("wide", NARROW, None))
    out_specs = P(None, "wide", NARROW, None)
    return jax.shard_map(shards, mesh=split, in_specs=in_specs, out_specs=out_specs, check_vma=False)
```

```python
import functools

import jax
import jax.numpy as jnp
from jax import lax
from jax.experimental import pallas as pl
from jax.experimental.pallas import tpu as pltpu
from jax.sharding import Mesh, PartitionSpec as P

DAMPING = 0.5
MASS = 0.02
NARROW = ("y", "core")
F32 = jnp.float32
BF16 = jnp.bfloat16


def cyclic(count, step):
    return [(i, (i + step) % count) for i in range(count)]


def after_y(v):
    return jnp.concatenate([v[1:], pltpu.roll(v[0], 7, 0)[None]], axis=0)


def before_y(v):
    return jnp.concatenate([pltpu.roll(v[v.shape[0] - 1], 1, 0)[None], v[:-1]], axis=0)


def after_x(v):
    return pltpu.roll(v, v.shape[2] - 1, 2)


def before_x(v):
    return pltpu.roll(v, 1, 2)


def times01(v, matrix):
    high = v.astype(BF16)
    rest = (v - high.astype(F32)).astype(BF16)
    out = jnp.dot(high, matrix, preferred_element_type=F32)
    return out + jnp.dot(rest, matrix, preferred_element_type=F32)


def pair_sum_matrix(fine, coarse, start, factor):
    i = lax.broadcasted_iota(jnp.int32, (fine, coarse), 0)
    j = lax.broadcasted_iota(jnp.int32, (fine, coarse), 1)
    return jnp.where((i >> 1) + start == j, factor, 0.0).astype(BF16)


def copy_matrix(coarse, fine):
    j = lax.broadcasted_iota(jnp.int32, (coarse, fine), 0)
    i = lax.broadcasted_iota(jnp.int32, (coarse, fine), 1)
    return jnp.where((i >> 1) == j, 1.0, 0.0).astype(BF16)


def lane_tiles(v):
    return [v[..., 128 * k : 128 * (k + 1)] for k in range(v.shape[-1] // 128)]


def join(parts):
    return parts[0] if len(parts) == 1 else jnp.concatenate(parts, axis=-1)


def interleaved(ref, tiles, *at):
    lanes = ref.shape[len(at)]
    return jnp.stack(
        [
            join([ref[(*at, k, pl.ds(t, 8, stride=tiles), slice(None))] for k in range(lanes)])
            for t in range(tiles)
        ]
    )


def to_natural(ref, v, *at):
    tiles = v.shape[0]
    for t in range(tiles):
        for k, part in enumerate(lane_tiles(v[t])):
            ref[(*at, k, pl.ds(t, 8, stride=tiles), slice(None))] = part


def row_pairs(ref, start, *at):
    parts = []
    for k in range(ref.shape[len(at)]):
        a = ref[(*at, k, pl.ds(start, 8, stride=2), slice(None))]
        b = ref[(*at, k, pl.ds(start + 1, 8, stride=2), slice(None))]
        parts.append(a + b)
    return join(parts)


def copy_rows(ref, v, start, *at):
    for k, part in enumerate(lane_tiles(v)):
        ref[(*at, k, pl.ds(start, 8, stride=2), slice(None))] = part
        ref[(*at, k, pl.ds(start + 1, 8, stride=2), slice(None))] = part


UNROLL = {2: 8, 4: 8, 6: 5, 9: 5}


def planes_loop(level, lo, hi, body):
    tiles, _, lanes = level.shape
    unroll = UNROLL[tiles * (lanes // 128)]
    while (hi - lo) % unroll:
        unroll -= 1
    lax.fori_loop(lo, hi, body, 0, unroll=unroll)


class Level:
    def __init__(self, tiles, lanes, wrap_x, wrap_y, gx, gxm, gy, gz, m, w, ms):
        self.shape = (tiles, 8, lanes)
        self.wrap_x, self.wrap_y = wrap_x, wrap_y
        self.gx, self.gxm, self.gy, self.gz = gx, gxm, gy, gz
        self.m, self.w, self.ms = m, w, ms

    def masks(self):
        tiles, _, lanes = self.shape
        t = lax.broadcasted_iota(jnp.int32, self.shape, 0)
        s = lax.broadcasted_iota(jnp.int32, self.shape, 1)
        lane = lax.broadcasted_iota(jnp.int32, self.shape, 2)
        row = tiles * s + t
        return (row == 0, row == 8 * tiles - 1, lane == 0, lane == lanes - 1)

    def after(self, v, axis, masks):
        r = after_y(v) if axis == 1 else after_x(v)
        if axis == 1 and self.wrap_y:
            r = jnp.where(masks[1], 0.0, r)
        if axis == 2 and self.wrap_x:
            r = jnp.where(masks[3], 0.0, r)
        return r

    def before(self, v, axis, masks):
        r = before_y(v) if axis == 1 else before_x(v)
        if axis == 1 and self.wrap_y:
            r = jnp.where(masks[0], 0.0, r)
        if axis == 2 and self.wrap_x:
            r = jnp.where(masks[2], 0.0, r)
        return r


def coefficients(level, rho, lo, hi):
    masks = level.masks()

    def shear(z):
        d = rho[z]
        return d * d * d

    def plane(z, _):
        d = rho[z]
        dn = rho[z + 1]
        g = d * d * d
        gn = dn * dn * dn
        gp = shear(z - 1)
        m = g * (0.5 + d)
        mn = gn * (0.5 + dn)
        gx = 0.5 * (g + after_x(g))
        gxm = 0.5 * (g + before_x(g))
        gy = 0.5 * (g + after_y(g))
        gz = 0.5 * (g + gn)
        total = MASS + gz + 0.5 * (g + gp)
        extra = None
        if level.wrap_x:
            gx = jnp.where(masks[3], 0.0, gx)
            gxm = jnp.where(masks[2], 0.0, gxm)
            extra = jnp.where(masks[2] | masks[3], 0.5 * g, 0.0)
        if level.wrap_y:
            gy = jnp.where(masks[1], 0.0, gy)
            more = jnp.where(masks[0] | masks[1], 0.5 * g, 0.0)
            extra = more if extra is None else extra + more
        if extra is not None:
            level.ms[z] = MASS + extra
            total = total + extra
        total = total + (gx + gxm) + (gy + before_y(gy)) + m
        inside = d > 0.0
        level.gx[z] = gx
        level.gxm[z] = gxm
        level.gy[z] = gy
        level.gz[z] = gz
        level.m[z] = m
        level.w[0, z] = jnp.where(inside, DAMPING / (total + mn), 0.0)
        level.w[1, z] = jnp.where(inside, DAMPING / (total + level.after(m, 1, masks)), 0.0)
        level.w[2, z] = jnp.where(inside, DAMPING / (total + level.after(m, 2, masks)), 0.0)
        return 0

    level.gz[lo - 1] = 0.5 * (shear(lo - 1) + shear(lo))
    last = rho[hi]
    level.m[hi] = last * last * last * (0.5 + last)
    planes_loop(level, lo, hi, plane)


def operate(level, u, lo, hi, s_ref, f_ref, emit):
    masks = level.masks()

    def stress(z):
        uz, uy, ux = u[0, z], u[1, z], u[2, z]
        div = (uz - u[0, z - 1]) + (uy - level.before(uy, 1, masks))
        return level.m[z] * (div + (ux - level.before(ux, 2, masks)))

    s_ref[...] = stress(lo)
    for c in range(3):
        f_ref[c] = level.gz[lo - 1] * (u[c, lo - 1] - u[c, lo])

    def plane(z, _):
        s = s_ref[...]
        sn = stress(z + 1)
        s_ref[...] = sn
        gx, gxm, gy, gz = level.gx[z], level.gxm[z], level.gy[z], level.gz[z]
        for c in range(3):
            v = u[c, z]
            fz = gz * (v - u[c, z + 1])
            fx = gx * (v - after_x(v)) + gxm * (v - before_x(v))
            fy = gy * (v - after_y(v))
            grad = s - (sn if c == 0 else level.after(s, c, masks))
            mass = MASS if level.ms is None else level.ms[z]
            a = mass * v + (fz - f_ref[c]) + fx + (fy - before_y(fy)) + grad
            f_ref[c] = fz
            emit(z, c, v, a)
        return 0

    planes_loop(level, lo, hi, plane)


def scaled(w, b, e, lo, hi):
    def plane(z, _):
        for c in range(3):
            e[c, z] = w[c, z] * b[c, z]
        return 0

    unroll = next(k for k in (4, 5, 3, 2, 1) if (hi - lo) % k == 0)
    lax.fori_loop(lo, hi, plane, 0, unroll=unroll)


def smoothed(level, b, src, dst, lo, hi, s_ref, f_ref):
    def emit(z, c, v, a):
        dst[c, z] = v + level.w[c, z] * (b[c, z] - a)

    operate(level, src, lo, hi, s_ref, f_ref, emit)


def in_grid(shape, own, high, n, last):
    t = lax.broadcasted_iota(jnp.int32, shape, 0)
    s = lax.broadcasted_iota(jnp.int32, shape, 1)
    row = shape[0] * s + t
    bad_high = (row >= own) & (row < own + high) & (n == last)
    bad_low = (row >= own + high) & (n == 0)
    return jnp.where(bad_high | bad_low, 0.0, 1.0)


def down0(
    idx, load, dens, rows, lo, hi,
    b, gx, gxm, gy, gz, m, w, ms, ep, edge_low, edge_high, l1,
    nat, rho, e1, rz, back, s_ref, f_ref,
):
    wide, narrow = idx[0], idx[1]
    for c in range(4):
        first = 0 if c == 3 else 1
        for z in range(first, 14 - first):
            if z < 3:
                own = lo[2 * c + z - first]
            elif z < 11:
                own = dens[z - 3] if c == 3 else load[c, z - 3]
            else:
                own = hi[2 * c + z - 11]
            halo = rows[12 * c + z - first]
            for k in range(3):
                nat[c, z, k, 0:16] = own[:, 128 * k : 128 * (k + 1)]
                nat[c, z, k, 16:24] = halo[:, 128 * k : 128 * (k + 1)]
    grid = in_grid((3, 8, 384), 16, 4, narrow, 7)
    below = jnp.where(wide == 0, 0.0, 1.0) * grid
    above = jnp.where(wide == 15, 0.0, 1.0) * grid
    for z in range(14):
        rho[z] = interleaved(nat, 3, 3, z) * (below if z < 3 else above if z > 10 else grid)
    level = Level(3, 384, True, False, gx, gxm, gy, gz, m, w, ms)
    coefficients(level, rho, 1, 13)

    def first(z, _):
        for c in range(3):
            v = interleaved(nat, 3, c, z)
            b[c, z] = v
            e1[c, z] = w[c, z] * v
        return 0

    lax.fori_loop(1, 13, first, 0, unroll=3)
    smoothed(level, b, e1, ep, 2, 12, s_ref, f_ref)
    for c in range(3):
        edge_low[c] = ep[c, 4]
        edge_high[c] = ep[c, 9]
    rz[...] = jnp.zeros_like(rz)

    def residual(z, c, v, a):
        k = ((z + 1) >> 1) - 2
        rz[c, k] = rz[c, k] + (b[c, z] - a)

    operate(level, ep, 3, 11, s_ref, f_ref, residual)
    even, odd = [], []
    for c in range(3):
        for k in range(4):
            to_natural(back, rz[c, k], c, k)
            (odd if k % 2 else even).append(row_pairs(back, 0, c, k))
    for k in range(6):
        d = 0.25 * (row_pairs(nat, 0, 3, 2 * k + 1) + row_pairs(nat, 0, 3, 2 * k + 2))
        if k == 0:
            d = d * jnp.where(wide == 0, 0.0, 1.0)
        if k == 5:
            d = d * jnp.where(wide == 15, 0.0, 1.0)
        (odd if k % 2 else even).append(d)
    left = pair_sum_matrix(384, 384, 0, 0.5)
    right = pair_sum_matrix(384, 384, 192, 0.5)
    out = times01(jnp.concatenate(even, axis=0), left)
    out = out + times01(jnp.concatenate(odd, axis=0), right)
    l1[...] = out.reshape(9, 8, 384)


def halves(v):
    lane = lax.broadcasted_iota(jnp.int32, (v.shape[0], 256), 1)
    first = jnp.where(lane < 192, v[:, :256], 0.0)
    second = jnp.where(lane < 192, pltpu.roll(v, 192, 1)[:, :256], 0.0)
    return first, second


def down1(
    idx, own, lo, hi, after, before,
    b, gx, gxm, gy, gz, m, w, ep, chunk,
    nat, rho, e1, rz, back, s_ref, f_ref,
):
    wide, narrow = idx[0], idx[1]
    row = lax.broadcasted_iota(jnp.int32, (8, 256), 0)

    def put(c, z, r, v):
        for k in range(2):
            nat[c, z, k, pl.ds(r, 8), :] = v[:, 128 * k : 128 * (k + 1)]

    for c in range(4):
        for q in range(3 if c == 3 else 2):
            i = 2 * c + q
            zo = 2 * q - 1 if c == 3 else 2 * q
            for source, (shift, ref) in enumerate(((0, own), (-4, lo), (4, hi))):
                tiles = [halves(ref[i])]
                j = 6 * source + i
                at = j // 2 if c < 3 else 9 + 3 * source + q
                for k, ref in enumerate((after, before)):
                    v = ref[at]
                    tiles.append(halves(pltpu.roll(v, 4, 0) if c < 3 and j % 2 != k else v))
                for s in range(2):
                    z = zo + s + shift
                    if (0 <= z < 4) != (shift == 0):
                        continue
                    put(c, z + 5, 0, tiles[0][s])
                    if c < 3:
                        put(c, z + 5, 8, jnp.where(row < 4, tiles[1][s], 0.0))
                        put(c, z + 5, 16, jnp.where(row >= 4, tiles[2][s], 0.0))
                    else:
                        put(c, z + 5, 8, tiles[1][s])
                        put(c, z + 5, 16, tiles[2][s])
    grid = in_grid((3, 8, 256), 8, 8, narrow, 7)
    below = jnp.where(wide == 0, 0.0, 1.0) * grid
    above = jnp.where(wide == 15, 0.0, 1.0) * grid
    for z in range(14):
        rho[z] = interleaved(nat, 3, 3, z) * (below if z < 5 else above if z > 8 else grid)
    level = Level(3, 256, False, False, gx, gxm, gy, gz, m, w, None)
    coefficients(level, rho, 1, 13)

    def first(z, _):
        for c in range(3):
            v = interleaved(nat, 3, c, z)
            b[c, z] = v
            e1[c, z] = w[c, z] * v
        return 0

    lax.fori_loop(1, 13, first, 0, unroll=3)
    smoothed(level, b, e1, ep, 2, 12, s_ref, f_ref)
    rz[...] = jnp.zeros_like(rz)

    def residual(z, c, v, a):
        k = ((z + 1) >> 1) - 3
        rz[c, k] = rz[c, k] + (b[c, z] - a)

    operate(level, ep, 5, 9, s_ref, f_ref, residual)
    parts = []
    for c in range(3):
        for k in range(2):
            to_natural(back, rz[c, k], c, k)
            parts.append(row_pairs(back, 0, c, k))
    for k in range(2):
        d = row_pairs(nat, 0, 3, 2 * k + 5) + row_pairs(nat, 0, 3, 2 * k + 6)
        parts.append(0.25 * d)
    out = times01(jnp.concatenate(parts, axis=0), pair_sum_matrix(256, 128, 0, 0.5))
    row8 = lax.broadcasted_iota(jnp.int32, (8, 128), 0)
    lane = lax.broadcasted_iota(jnp.int32, (8, 128), 1)
    four = []
    for c in range(4):
        low, high = out[16 * c : 16 * c + 8], out[16 * c + 8 : 16 * c + 16]
        four.append(jnp.where(row8 < 4, low, pltpu.roll(high, 4, 0)))
    for c in range(3):
        d = four[3] if c == 3 else pltpu.roll(four[3], 96 - 32 * c, 1)
        chunk[c] = jnp.where(lane < 96, four[c], d)


def rest(
    idx, mine, other, lo, hi,
    b1, gx1, gxm1, gy1, gz1, m1, w1, ep1,
    b0, gx0, gxm0, gy0, gz0, m0, w0, ms0, ep0,
    out,
    rho2, b2, gx2, gxm2, gy2, gz2, m2, w2, ms2, ea, ep2,
    rho3, b3, gx3, gxm3, gy3, gz3, m3, w3, ms3, ec, ed,
    rz, nat2, nat1, nat0, s3, f3, ua, ub, s2, f2, va, vb, s1, f1, xa, xb, s0, f0,
):
    wide, narrow = idx[0], idx[1]
    core = narrow & 1
    zero2 = jnp.zeros((4, 8, 128), F32)
    zero3 = jnp.zeros((2, 8, 128), F32)

    def outside(i, _):
        z = jnp.where(i < 4, i, i + 32)
        for ref in (rho2, gx2, gxm2, gy2, gz2, m2, ms2):
            ref[z] = zero2
        for ref in (b2, w2, ea, ep2):
            for c in range(3):
                ref[c, z] = zero2
        return 0

    lax.fori_loop(0, 8, outside, 0)
    for z in (1, 18):
        rho3[z] = zero3
    for z in (0, 1, 18, 19):
        for c in range(3):
            ec[c, z] = zero3
            ed[c, z] = zero3

    lane = lax.broadcasted_iota(jnp.int32, (4, 8, 128), 2)

    def unpack(w, _):
        for c in range(3):
            for r in range(8):
                own = mine[w, pl.ds(8 * c + r, 4, stride=24), :]
                off = other[w, pl.ds(8 * c + r, 4, stride=24), :]
                ref = ea.at[c, 2 * w + 4 + r // 4, r % 4]
                ref[pl.ds(0, 4, stride=2), :] = jnp.where(core == 0, own, off)
                ref[pl.ds(1, 4, stride=2), :] = jnp.where(core == 0, off, own)
        return 0

    lax.fori_loop(0, 16, unpack, 0)

    def split(z, _):
        d = jnp.zeros((4, 8, 128), F32)
        for c in range(3):
            v = ea[c, z]
            b2[c, z] = jnp.where(lane < 96, v, 0.0)
            moved = pltpu.roll(v, 32 + 32 * c, 2) if c < 3 else v
            d = jnp.where((lane >> 5) == c, moved, d)
        rho2[z] = d
        return 0

    lax.fori_loop(4, 36, split, 0, unroll=4)

    level2 = Level(4, 128, False, True, gx2, gxm2, gy2, gz2, m2, w2, ms2)
    coefficients(level2, rho2, 4, 36)
    scaled(w2, b2, ea, 4, 36)
    smoothed(level2, b2, ea, ep2, 4, 36, s2, f2)
    rz[...] = jnp.zeros_like(rz)

    def residual(z, c, v, a):
        r = b2[c, z] - a
        k = (z >> 1) - 2
        rz[c, k] = rz[c, k] + jnp.stack([r[0] + r[1], r[2] + r[3]])

    operate(level2, ep2, 4, 36, s2, f2, residual)

    def coarse_density(z, _):
        d = 0.25 * (rho2[2 * z + 4] + rho2[2 * z + 5])
        rz[3, z] = jnp.stack([d[0] + d[1], d[2] + d[3]])
        return 0

    lax.fori_loop(0, 16, coarse_density, 0, unroll=4)
    half = pair_sum_matrix(128, 128, 0, 0.5)
    for c in range(4):
        v = times01(rz[c].reshape(256, 128), half).reshape(16, 2, 8, 128)
        if c < 3:
            b3[c, 2:18] = v
        else:
            rho3[2:18] = v

    level3 = Level(2, 128, False, True, gx3, gxm3, gy3, gz3, m3, w3, ms3)
    coefficients(level3, rho3, 2, 18)
    scaled(w3, b3, ec, 2, 18)
    for src, dst in ((ec, ed), (ed, ec), (ec, ed)):
        smoothed(level3, b3, src, dst, 2, 18, s3, f3)

    near = pl.ds(2 * wide, 10)
    gx2, gxm2, gy2, gz2, m2, ms2 = (v.at[near] for v in (gx2, gxm2, gy2, gz2, m2, ms2))
    b2, w2, ep2 = (v.at[:, near] for v in (b2, w2, ep2))
    parts = [ed[c, wide + k].reshape(16, 128) for c in range(3) for k in range(5)]
    up = times01(jnp.concatenate(parts, axis=0), copy_matrix(128, 128))
    for c in range(3):
        for k in range(5):
            at = 16 * (5 * c + k)
            t = [up[at : at + 8], up[at + 8 : at + 16]]
            both = jnp.stack([t[0], t[0], t[1], t[1]])
            for z in (2 * k, 2 * k + 1):
                ua[c, z] = jnp.where(w2[0, z] > 0.0, ep2[c, z] + both, 0.0)
    at2 = Level(4, 128, False, True, gx2, gxm2, gy2, gz2, m2, w2, ms2)
    smoothed(at2, b2, ua, ub, 1, 9, s2, f2)
    smoothed(at2, b2, ub, ua, 2, 8, s2, f2)

    turn = (8 - narrow) & 7
    parts = []
    for c in range(3):
        for k in range(6):
            v = ua[c, 2 + k]
            to_natural(nat2, jnp.stack([pltpu.roll(v[t], turn, 0) for t in range(4)]), c, k)
            parts += [nat2[c, k, 0, 0:8], nat2[c, k, 0, 24:32]]
    up = times01(jnp.concatenate(parts, axis=0), copy_matrix(128, 256))
    for c in range(3):
        for k in range(6):
            at = 16 * (6 * c + k)
            copy_rows(nat1, up[at + 8 : at + 16], 8, c, k)
            copy_rows(nat1, up[at : at + 8], 0, c, k)
            both = interleaved(nat1, 3, c, k)
            for z in (2 * k + 1, 2 * k + 2):
                if 2 <= z < 12:
                    va[c, z] = jnp.where(w1[0, z] > 0.0, ep1[c, z] + both, 0.0)
    level1 = Level(3, 256, False, False, gx1, gxm1, gy1, gz1, m1, w1, None)
    smoothed(level1, b1, va, vb, 3, 11, s1, f1)
    smoothed(level1, b1, vb, va, 4, 10, s1, f1)

    row8 = lax.broadcasted_iota(jnp.int32, (8, 256), 0)
    parts = []
    for c in range(3):
        for k in range(6):
            to_natural(nat1, va[c, 4 + k], c, k)
            t = [join([nat1[c, k, j, 8 * r : 8 * r + 8] for j in range(2)]) for r in range(3)]
            parts += [t[0], jnp.where(row8 < 2, t[1], pltpu.roll(t[2], 4, 0))]
    up = times01(jnp.concatenate(parts, axis=0), copy_matrix(256, 384))
    for c in range(3):
        for k in range(6):
            at = 16 * (6 * c + k)
            copy_rows(nat0, up[at + 8 : at + 16], 16, c, k)
            copy_rows(nat0, up[at : at + 8], 0, c, k)
            both = interleaved(nat0, 3, c, k)
            for z in (2 * k + 1, 2 * k + 2):
                if z in (1, 12):
                    ref = lo if z == 1 else hi
                    old = jnp.stack([ref[9 + 3 * c + t] for t in range(3)])
                else:
                    old = ep0[c, z]
                xa[c, z] = jnp.where(w0[0, z] > 0.0, old + both, 0.0)
    level0 = Level(3, 384, True, False, gx0, gxm0, gy0, gz0, m0, w0, ms0)
    smoothed(level0, b0, xa, xb, 2, 12, s0, f0)

    def last(z, c, v, a):
        to_natural(nat0, v + w0[c, z] * (b0[c, z] - a), c, 0)
        for k in range(3):
            out[c, z - 3, :, 128 * k : 128 * (k + 1)] = nat0[c, 0, k, 0:16]

    operate(level0, xb, 3, 11, s0, f0, last)


def call(kernel, outs, scratch, args, flops, mib):
    vmem = pl.BlockSpec(memory_space=pltpu.VMEM)
    size = sum(4 * int(a.size) for a in args)
    size += sum(4 * functools.reduce(lambda p, q: p * q, s) for s in outs)
    return pl.pallas_call(
        kernel,
        out_shape=[jax.ShapeDtypeStruct(s, F32) for s in outs],
        in_specs=[pl.BlockSpec(memory_space=pltpu.SMEM)] + [vmem] * (len(args) - 1),
        out_specs=[vmem] * len(outs),
        scratch_shapes=[pltpu.VMEM(s, F32) for s in scratch],
        compiler_params=pltpu.CompilerParams(vmem_limit_bytes=mib * 1024 * 1024),
        cost_estimate=pl.CostEstimate(flops=flops, bytes_accessed=size, transcendentals=0),
    )(*args)


def shards(load, density):
    wide = lax.axis_index("wide")
    narrow = lax.axis_index(NARROW)
    idx = jnp.stack([wide, narrow]).astype(jnp.int32)
    load, density, idx = lax.optimization_barrier((load, density, idx))

    def next_rows(v):
        return lax.ppermute(v, NARROW, cyclic(8, -1))

    def previous_rows(v):
        return lax.ppermute(v, NARROW, cyclic(8, 1))

    def above(v, steps=1):
        return lax.ppermute(v, "wide", cyclic(16, -steps))

    def below(v, steps=1):
        return lax.ppermute(v, "wide", cyclic(16, steps))

    lo = below(jnp.concatenate([load[:, 6:].reshape(6, 16, 384), density[5:]], axis=0))
    hi = above(jnp.concatenate([load[:, :2].reshape(6, 16, 384), density[:3]], axis=0))

    def rows_of(at):
        parts = []
        for c in range(4):
            own = density if c == 3 else load[c]
            end = 9 if c == 3 else 2 * c + 2
            parts += [lo[2 * c : end, at], own[:, at], hi[2 * c : end, at]]
        return jnp.concatenate(parts, axis=0)

    low, high = previous_rows(rows_of(slice(12, 16))), next_rows(rows_of(slice(0, 4)))
    rows = jnp.concatenate([high, low], axis=1)
    p0, c0 = (14, 3, 8, 384), (3, 8, 384)
    b0, gx0, gxm0, gy0, gz0, m0, w0, ms0, ep0, edge_low, edge_high, l1 = call(
        down0,
        [(3,) + p0, p0, p0, p0, p0, p0, (3,) + p0, p0, (3,) + p0, (3,) + c0, (3,) + c0, (9, 8, 384)],
        [(4, 14, 3, 24, 128), p0, (3,) + p0, (3, 4) + c0, (3, 4, 3, 24, 128), c0, (3,) + c0],
        [idx, load, density, rows, lo, hi],
        10**7,
        17,
    )

    lo = below(jnp.concatenate([l1, edge_high.reshape(9, 8, 384)], axis=0))
    hi = above(jnp.concatenate([l1, edge_low.reshape(9, 8, 384)], axis=0))

    def level1_rows(at):
        b = [jnp.concatenate([v[0:6:2, at], v[1:6:2, at]], axis=1) for v in (l1, lo, hi)]
        return jnp.concatenate(b + [v[6:9] for v in (l1, lo, hi)], axis=0)

    after, before = next_rows(level1_rows(slice(0, 4))), previous_rows(level1_rows(slice(4, 8)))
    p1, c1 = (14, 3, 8, 256), (3, 8, 256)
    b1, gx1, gxm1, gy1, gz1, m1, w1, ep1, chunk = call(
        down1,
        [(3,) + p1, p1, p1, p1, p1, p1, (3,) + p1, (3,) + p1, (3, 8, 128)],
        [(4, 14, 2, 24, 128), p1, (3,) + p1, (3, 4) + c1, (3, 4, 2, 24, 128), c1, (3,) + c1],
        [idx, l1, lo, hi, after, before],
        10**7,
        10,
    )

    chunks = jnp.broadcast_to(chunk[None], (64, 3, 8, 128))
    mine = lax.all_to_all(chunks, ("wide", "y"), 0, 0).reshape(16, 96, 128)
    other = lax.ppermute(mine, "core", cyclic(2, 1))
    p2, c2 = (40, 4, 8, 128), (4, 8, 128)
    u2 = (3, 10, 4, 8, 128)
    p3, c3 = (20, 2, 8, 128), (2, 8, 128)
    (out,) = call(
        rest,
        [(3, 8, 16, 384)],
        [p2, (3,) + p2, p2, p2, p2, p2, p2, (3,) + p2, p2, (3,) + p2, (3,) + p2]
        + [p3, (3,) + p3, p3, p3, p3, p3, p3, (3,) + p3, p3, (3,) + p3, (3,) + p3]
        + [(4, 16, 2, 8, 128), (3, 6, 1, 32, 128), (3, 6, 2, 24, 128), (3, 6, 3, 32, 128)]
        + [c3, (3,) + c3, u2, u2, c2, (3,) + c2]
        + [(3,) + p1, (3,) + p1, c1, (3,) + c1, (3,) + p0, (3,) + p0, c0, (3,) + c0],
        [idx, mine, other, lo, hi]
        + [b1, gx1, gxm1, gy1, gz1, m1, w1, ep1]
        + [b0, gx0, gxm0, gy0, gz0, m0, w0, ms0, ep0],
        10**8,
        40,
    )
    return out


def solution(mesh):
    split = Mesh(mesh.devices.reshape(16, 4, 2), ("wide",) + NARROW)
    in_specs = (P(None, "wide", NARROW, None), P("wide", NARROW, None))
    out_specs = P(None, "wide", NARROW, None)
    return jax.shard_map(shards, mesh=split, in_specs=in_specs, out_specs=out_specs, check_vma=False)
```

```python
import functools

import jax
import jax.numpy as jnp
from jax import lax
from jax.experimental import pallas as pl
from jax.experimental.pallas import tpu as pltpu
from jax.sharding import Mesh, PartitionSpec as P

DAMPING = 0.5
MASS = 0.02
NARROW = ("y", "core")
F32 = jnp.float32
BF16 = jnp.bfloat16


def cyclic(count, step):
    return [(i, (i + step) % count) for i in range(count)]


def after_y(v):
    return jnp.concatenate([v[1:], pltpu.roll(v[0], 7, 0)[None]], axis=0)


def before_y(v):
    return jnp.concatenate([pltpu.roll(v[v.shape[0] - 1], 1, 0)[None], v[:-1]], axis=0)


def after_x(v):
    return pltpu.roll(v, v.shape[2] - 1, 2)


def before_x(v):
    return pltpu.roll(v, 1, 2)


def times01(v, matrix):
    high = v.astype(BF16)
    rest = (v - high.astype(F32)).astype(BF16)
    out = jnp.dot(high, matrix, preferred_element_type=F32)
    return out + jnp.dot(rest, matrix, preferred_element_type=F32)


def pair_sum_matrix(fine, coarse, start, factor):
    i = lax.broadcasted_iota(jnp.int32, (fine, coarse), 0)
    j = lax.broadcasted_iota(jnp.int32, (fine, coarse), 1)
    return jnp.where((i >> 1) + start == j, factor, 0.0).astype(BF16)


def copy_matrix(coarse, fine):
    j = lax.broadcasted_iota(jnp.int32, (coarse, fine), 0)
    i = lax.broadcasted_iota(jnp.int32, (coarse, fine), 1)
    return jnp.where((i >> 1) == j, 1.0, 0.0).astype(BF16)


def lane_tiles(v):
    return [v[..., 128 * k : 128 * (k + 1)] for k in range(v.shape[-1] // 128)]


def join(parts):
    return parts[0] if len(parts) == 1 else jnp.concatenate(parts, axis=-1)


def interleaved(ref, tiles, *at):
    lanes = ref.shape[len(at)]
    return jnp.stack(
        [
            join([ref[(*at, k, pl.ds(t, 8, stride=tiles), slice(None))] for k in range(lanes)])
            for t in range(tiles)
        ]
    )


def to_natural(ref, v, *at):
    tiles = v.shape[0]
    for t in range(tiles):
        for k, part in enumerate(lane_tiles(v[t])):
            ref[(*at, k, pl.ds(t, 8, stride=tiles), slice(None))] = part


def row_pairs(ref, start, *at):
    parts = []
    for k in range(ref.shape[len(at)]):
        a = ref[(*at, k, pl.ds(start, 8, stride=2), slice(None))]
        b = ref[(*at, k, pl.ds(start + 1, 8, stride=2), slice(None))]
        parts.append(a + b)
    return join(parts)


def copy_rows(ref, v, start, *at):
    for k, part in enumerate(lane_tiles(v)):
        ref[(*at, k, pl.ds(start, 8, stride=2), slice(None))] = part
        ref[(*at, k, pl.ds(start + 1, 8, stride=2), slice(None))] = part


UNROLL = {2: 16, 4: 32, 6: 12, 9: 12}


def planes_loop(level, lo, hi, body):
    tiles, _, lanes = level.shape
    unroll = UNROLL[tiles * (lanes // 128)]
    while (hi - lo) % unroll:
        unroll -= 1
    lax.fori_loop(lo, hi, body, 0, unroll=unroll)


class Level:
    def __init__(self, tiles, lanes, wrap_x, wrap_y, gx, gxm, gy, gz, m, w, ms):
        self.shape = (tiles, 8, lanes)
        self.wrap_x, self.wrap_y = wrap_x, wrap_y
        self.gx, self.gxm, self.gy, self.gz = gx, gxm, gy, gz
        self.m, self.w, self.ms = m, w, ms

    def masks(self):
        tiles, _, lanes = self.shape
        t = lax.broadcasted_iota(jnp.int32, self.shape, 0)
        s = lax.broadcasted_iota(jnp.int32, self.shape, 1)
        lane = lax.broadcasted_iota(jnp.int32, self.shape, 2)
        row = tiles * s + t
        return (row == 0, row == 8 * tiles - 1, lane == 0, lane == lanes - 1)

    def after(self, v, axis, masks):
        r = after_y(v) if axis == 1 else after_x(v)
        if axis == 1 and self.wrap_y:
            r = jnp.where(masks[1], 0.0, r)
        if axis == 2 and self.wrap_x:
            r = jnp.where(masks[3], 0.0, r)
        return r

    def before(self, v, axis, masks):
        r = before_y(v) if axis == 1 else before_x(v)
        if axis == 1 and self.wrap_y:
            r = jnp.where(masks[0], 0.0, r)
        if axis == 2 and self.wrap_x:
            r = jnp.where(masks[2], 0.0, r)
        return r


def coefficients(level, rho, lo, hi, first):
    masks = level.masks()

    def shear(z):
        d = rho[z]
        return d * d * d

    def plane(z, _):
        d = rho[z]
        dn = rho[z + 1]
        g = d * d * d
        gn = dn * dn * dn
        gp = shear(z - 1)
        m = g * (0.5 + d)
        mn = gn * (0.5 + dn)
        gx = 0.5 * (g + after_x(g))
        gxm = 0.5 * (g + before_x(g))
        gy = 0.5 * (g + after_y(g))
        gz = 0.5 * (g + gn)
        total = MASS + gz + 0.5 * (g + gp)
        extra = None
        if level.wrap_x:
            gx = jnp.where(masks[3], 0.0, gx)
            gxm = jnp.where(masks[2], 0.0, gxm)
            extra = jnp.where(masks[2] | masks[3], 0.5 * g, 0.0)
        if level.wrap_y:
            gy = jnp.where(masks[1], 0.0, gy)
            more = jnp.where(masks[0] | masks[1], 0.5 * g, 0.0)
            extra = more if extra is None else extra + more
        if extra is not None:
            level.ms[z] = MASS + extra
            total = total + extra
        total = total + (gx + gxm) + (gy + before_y(gy)) + m
        inside = d > 0.0
        level.gx[z] = gx
        level.gxm[z] = gxm
        level.gy[z] = gy
        level.gz[z] = gz
        level.m[z] = m
        for c, beyond in enumerate((mn, level.after(m, 1, masks), level.after(m, 2, masks))):
            w = jnp.where(inside, DAMPING / (total + beyond), 0.0)
            level.w[c, z] = w
            first(z, c, w)
        return 0

    level.gz[lo - 1] = 0.5 * (shear(lo - 1) + shear(lo))
    last = rho[hi]
    level.m[hi] = last * last * last * (0.5 + last)
    planes_loop(level, lo, hi, plane)


def operate(level, u, lo, hi, s_ref, f_ref, emit):
    masks = level.masks()

    def stress(z):
        uz, uy, ux = u[0, z], u[1, z], u[2, z]
        left = level.before(ux, 2, masks)
        s_ref[1] = left
        div = (uz - u[0, z - 1]) + (uy - level.before(uy, 1, masks))
        return level.m[z] * (div + (ux - left))

    s_ref[0] = stress(lo)
    for c in range(3):
        f_ref[c] = level.gz[lo - 1] * (u[c, lo - 1] - u[c, lo])

    def plane(z, _):
        s, left = s_ref[0], s_ref[1]
        sn = stress(z + 1)
        s_ref[0] = sn
        gx, gxm, gy, gz = level.gx[z], level.gxm[z], level.gy[z], level.gz[z]
        for c in range(3):
            v = u[c, z]
            fz = gz * (v - u[c, z + 1])
            fx = gx * (v - after_x(v)) + gxm * (v - (left if c == 2 else before_x(v)))
            fy = gy * (v - after_y(v))
            grad = s - (sn if c == 0 else level.after(s, c, masks))
            mass = MASS if level.ms is None else level.ms[z]
            a = mass * v + (fz - f_ref[c]) + fx + (fy - before_y(fy)) + grad
            f_ref[c] = fz
            emit(z, c, v, a)
        return 0

    planes_loop(level, lo, hi, plane)


def smoothed(level, b, src, dst, lo, hi, s_ref, f_ref):
    def emit(z, c, v, a):
        dst[c, z] = v + level.w[c, z] * (b[c, z] - a)

    operate(level, src, lo, hi, s_ref, f_ref, emit)


def in_grid(shape, own, high, n, last):
    t = lax.broadcasted_iota(jnp.int32, shape, 0)
    s = lax.broadcasted_iota(jnp.int32, shape, 1)
    row = shape[0] * s + t
    bad_high = (row >= own) & (row < own + high) & (n == last)
    bad_low = (row >= own + high) & (n == 0)
    return jnp.where(bad_high | bad_low, 0.0, 1.0)


def down0(
    idx, load, dens, rows, lo, hi,
    b, gx, gxm, gy, gz, m, w, ms, ep, edge_low, edge_high, l1,
    nat, rho, e1, rz, back, s_ref, f_ref,
):
    wide, narrow = idx[0], idx[1]
    for c in range(4):
        first = 0 if c == 3 else 1
        for z in range(first, 14 - first):
            if z < 3:
                own = lo[2 * c + z - first]
            elif z < 11:
                own = dens[z - 3] if c == 3 else load[c, z - 3]
            else:
                own = hi[2 * c + z - 11]
            halo = rows[12 * c + z - first]
            for k in range(3):
                nat[c, z, k, 0:16] = own[:, 128 * k : 128 * (k + 1)]
                nat[c, z, k, 16:24] = halo[:, 128 * k : 128 * (k + 1)]
    grid = in_grid((3, 8, 384), 16, 4, narrow, 7)
    below = jnp.where(wide == 0, 0.0, 1.0) * grid
    above = jnp.where(wide == 15, 0.0, 1.0) * grid
    for z in range(14):
        rho[z] = interleaved(nat, 3, 3, z) * (below if z < 3 else above if z > 10 else grid)
    level = Level(3, 384, True, False, gx, gxm, gy, gz, m, w, ms)

    def first(z, c, scale):
        v = interleaved(nat, 3, c, z)
        b[c, z] = v
        e1[c, z] = scale * v

    coefficients(level, rho, 1, 13, first)
    smoothed(level, b, e1, ep, 2, 12, s_ref, f_ref)
    for c in range(3):
        edge_low[c] = ep[c, 4]
        edge_high[c] = ep[c, 9]
    rz[...] = jnp.zeros_like(rz)

    def residual(z, c, v, a):
        k = ((z + 1) >> 1) - 2
        rz[c, k] = rz[c, k] + (b[c, z] - a)

    operate(level, ep, 3, 11, s_ref, f_ref, residual)
    even, odd = [], []
    for c in range(3):
        for k in range(4):
            to_natural(back, rz[c, k], c, k)
            (odd if k % 2 else even).append(row_pairs(back, 0, c, k))
    for k in range(6):
        d = 0.25 * (row_pairs(nat, 0, 3, 2 * k + 1) + row_pairs(nat, 0, 3, 2 * k + 2))
        if k == 0:
            d = d * jnp.where(wide == 0, 0.0, 1.0)
        if k == 5:
            d = d * jnp.where(wide == 15, 0.0, 1.0)
        (odd if k % 2 else even).append(d)
    left = pair_sum_matrix(384, 384, 0, 0.5)
    right = pair_sum_matrix(384, 384, 192, 0.5)
    out = times01(jnp.concatenate(even, axis=0), left)
    out = out + times01(jnp.concatenate(odd, axis=0), right)
    l1[...] = out.reshape(9, 8, 384)


def halves(v):
    lane = lax.broadcasted_iota(jnp.int32, (v.shape[0], 256), 1)
    first = jnp.where(lane < 192, v[:, :256], 0.0)
    second = jnp.where(lane < 192, pltpu.roll(v, 192, 1)[:, :256], 0.0)
    return first, second


def down1(
    idx, own, lo, hi, after, before,
    b, gx, gxm, gy, gz, m, w, ep, chunk,
    nat, rho, e1, rz, back, s_ref, f_ref,
):
    wide, narrow = idx[0], idx[1]
    row = lax.broadcasted_iota(jnp.int32, (8, 256), 0)

    def put(c, z, r, v):
        for k in range(2):
            nat[c, z, k, pl.ds(r, 8), :] = v[:, 128 * k : 128 * (k + 1)]

    for c in range(4):
        for q in range(3 if c == 3 else 2):
            i = 2 * c + q
            zo = 2 * q - 1 if c == 3 else 2 * q
            for source, (shift, ref) in enumerate(((0, own), (-4, lo), (4, hi))):
                tiles = [halves(ref[i])]
                j = 6 * source + i
                at = j // 2 if c < 3 else 9 + 3 * source + q
                for k, ref in enumerate((after, before)):
                    v = ref[at]
                    tiles.append(halves(pltpu.roll(v, 4, 0) if c < 3 and j % 2 != k else v))
                for s in range(2):
                    z = zo + s + shift
                    if (0 <= z < 4) != (shift == 0):
                        continue
                    put(c, z + 5, 0, tiles[0][s])
                    if c < 3:
                        put(c, z + 5, 8, jnp.where(row < 4, tiles[1][s], 0.0))
                        put(c, z + 5, 16, jnp.where(row >= 4, tiles[2][s], 0.0))
                    else:
                        put(c, z + 5, 8, tiles[1][s])
                        put(c, z + 5, 16, tiles[2][s])
    grid = in_grid((3, 8, 256), 8, 8, narrow, 7)
    below = jnp.where(wide == 0, 0.0, 1.0) * grid
    above = jnp.where(wide == 15, 0.0, 1.0) * grid
    for z in range(14):
        rho[z] = interleaved(nat, 3, 3, z) * (below if z < 5 else above if z > 8 else grid)
    level = Level(3, 256, False, False, gx, gxm, gy, gz, m, w, None)

    def first(z, c, scale):
        v = interleaved(nat, 3, c, z)
        b[c, z] = v
        e1[c, z] = scale * v

    coefficients(level, rho, 1, 13, first)
    smoothed(level, b, e1, ep, 2, 12, s_ref, f_ref)
    rz[...] = jnp.zeros_like(rz)

    def residual(z, c, v, a):
        k = ((z + 1) >> 1) - 3
        rz[c, k] = rz[c, k] + (b[c, z] - a)

    operate(level, ep, 5, 9, s_ref, f_ref, residual)
    parts = []
    for c in range(3):
        for k in range(2):
            to_natural(back, rz[c, k], c, k)
            parts.append(row_pairs(back, 0, c, k))
    for k in range(2):
        d = row_pairs(nat, 0, 3, 2 * k + 5) + row_pairs(nat, 0, 3, 2 * k + 6)
        parts.append(0.25 * d)
    out = times01(jnp.concatenate(parts, axis=0), pair_sum_matrix(256, 128, 0, 0.5))
    row8 = lax.broadcasted_iota(jnp.int32, (8, 128), 0)
    lane = lax.broadcasted_iota(jnp.int32, (8, 128), 1)
    four = []
    for c in range(4):
        low, high = out[16 * c : 16 * c + 8], out[16 * c + 8 : 16 * c + 16]
        four.append(jnp.where(row8 < 4, low, pltpu.roll(high, 4, 0)))
    for c in range(3):
        d = four[3] if c == 3 else pltpu.roll(four[3], 96 - 32 * c, 1)
        chunk[c] = jnp.where(lane < 96, four[c], d)


def rest(
    idx, mine, other, lo, hi,
    b1, gx1, gxm1, gy1, gz1, m1, w1, ep1,
    b0, gx0, gxm0, gy0, gz0, m0, w0, ms0, ep0,
    out,
    rho2, b2, gx2, gxm2, gy2, gz2, m2, w2, ms2, ea, ep2,
    rho3, b3, gx3, gxm3, gy3, gz3, m3, w3, ms3, ec, ed,
    rz, nat2, nat1, nat0, s3, f3, ua, ub, s2, f2, va, vb, s1, f1, xa, xb, s0, f0,
):
    wide, narrow = idx[0], idx[1]
    core = narrow & 1
    zero2 = jnp.zeros((4, 8, 128), F32)
    zero3 = jnp.zeros((2, 8, 128), F32)

    def outside(i, _):
        z = jnp.where(i < 4, i, i + 32)
        for ref in (rho2, gx2, gxm2, gy2, gz2, m2, ms2):
            ref[z] = zero2
        for ref in (b2, w2, ea, ep2):
            for c in range(3):
                ref[c, z] = zero2
        return 0

    lax.fori_loop(0, 8, outside, 0)
    for z in (1, 18):
        rho3[z] = zero3
    for z in (0, 1, 18, 19):
        for c in range(3):
            ec[c, z] = zero3
            ed[c, z] = zero3

    lane = lax.broadcasted_iota(jnp.int32, (4, 8, 128), 2)

    def unpack(w, _):
        for c in range(3):
            for r in range(8):
                own = mine[w, pl.ds(8 * c + r, 4, stride=24), :]
                off = other[w, pl.ds(8 * c + r, 4, stride=24), :]
                ref = ea.at[c, 2 * w + 4 + r // 4, r % 4]
                ref[pl.ds(0, 4, stride=2), :] = jnp.where(core == 0, own, off)
                ref[pl.ds(1, 4, stride=2), :] = jnp.where(core == 0, off, own)
        return 0

    lax.fori_loop(0, 16, unpack, 0)

    def split(z, _):
        d = jnp.zeros((4, 8, 128), F32)
        for c in range(3):
            v = ea[c, z]
            moved = pltpu.roll(v, 32 + 32 * c, 2) if c < 3 else v
            d = jnp.where((lane >> 5) == c, moved, d)
        rho2[z] = d
        return 0

    lax.fori_loop(4, 36, split, 0, unroll=4)

    level2 = Level(4, 128, False, True, gx2, gxm2, gy2, gz2, m2, w2, ms2)

    def first2(z, c, scale):
        v = jnp.where(lane < 96, ea[c, z], 0.0)
        b2[c, z] = v
        ea[c, z] = scale * v

    coefficients(level2, rho2, 4, 36, first2)
    smoothed(level2, b2, ea, ep2, 4, 36, s2, f2)
    rz[...] = jnp.zeros_like(rz)

    def residual(z, c, v, a):
        r = b2[c, z] - a
        k = (z >> 1) - 2
        rz[c, k] = rz[c, k] + jnp.stack([r[0] + r[1], r[2] + r[3]])

    operate(level2, ep2, 4, 36, s2, f2, residual)

    def coarse_density(z, _):
        d = 0.25 * (rho2[2 * z + 4] + rho2[2 * z + 5])
        rz[3, z] = jnp.stack([d[0] + d[1], d[2] + d[3]])
        return 0

    lax.fori_loop(0, 16, coarse_density, 0, unroll=4)
    half = pair_sum_matrix(128, 128, 0, 0.5)
    for c in range(4):
        v = times01(rz[c].reshape(256, 128), half).reshape(16, 2, 8, 128)
        if c < 3:
            b3[c, 2:18] = v
        else:
            rho3[2:18] = v

    level3 = Level(2, 128, False, True, gx3, gxm3, gy3, gz3, m3, w3, ms3)

    def first3(z, c, scale):
        ec[c, z] = scale * b3[c, z]

    coefficients(level3, rho3, 2, 18, first3)
    for src, dst in ((ec, ed), (ed, ec), (ec, ed)):
        smoothed(level3, b3, src, dst, 2, 18, s3, f3)

    near = pl.ds(2 * wide, 10)
    gx2, gxm2, gy2, gz2, m2, ms2 = (v.at[near] for v in (gx2, gxm2, gy2, gz2, m2, ms2))
    b2, w2, ep2 = (v.at[:, near] for v in (b2, w2, ep2))
    parts = [ed[c, wide + k].reshape(16, 128) for c in range(3) for k in range(5)]
    up = times01(jnp.concatenate(parts, axis=0), copy_matrix(128, 128))
    for c in range(3):
        for k in range(5):
            at = 16 * (5 * c + k)
            t = [up[at : at + 8], up[at + 8 : at + 16]]
            both = jnp.stack([t[0], t[0], t[1], t[1]])
            for z in (2 * k, 2 * k + 1):
                ua[c, z] = jnp.where(w2[0, z] > 0.0, ep2[c, z] + both, 0.0)
    at2 = Level(4, 128, False, True, gx2, gxm2, gy2, gz2, m2, w2, ms2)
    smoothed(at2, b2, ua, ub, 1, 9, s2, f2)
    smoothed(at2, b2, ub, ua, 2, 8, s2, f2)

    turn = (8 - narrow) & 7
    parts = []
    for c in range(3):
        for k in range(6):
            v = ua[c, 2 + k]
            to_natural(nat2, jnp.stack([pltpu.roll(v[t], turn, 0) for t in range(4)]), c, k)
            parts += [nat2[c, k, 0, 0:8], nat2[c, k, 0, 24:32]]
    up = times01(jnp.concatenate(parts, axis=0), copy_matrix(128, 256))
    for c in range(3):
        for k in range(6):
            at = 16 * (6 * c + k)
            copy_rows(nat1, up[at + 8 : at + 16], 8, c, k)
            copy_rows(nat1, up[at : at + 8], 0, c, k)
            both = interleaved(nat1, 3, c, k)
            for z in (2 * k + 1, 2 * k + 2):
                if 2 <= z < 12:
                    va[c, z] = jnp.where(w1[0, z] > 0.0, ep1[c, z] + both, 0.0)
    level1 = Level(3, 256, False, False, gx1, gxm1, gy1, gz1, m1, w1, None)
    smoothed(level1, b1, va, vb, 3, 11, s1, f1)
    smoothed(level1, b1, vb, va, 4, 10, s1, f1)

    row8 = lax.broadcasted_iota(jnp.int32, (8, 256), 0)
    parts = []
    for c in range(3):
        for k in range(6):
            to_natural(nat1, va[c, 4 + k], c, k)
            t = [join([nat1[c, k, j, 8 * r : 8 * r + 8] for j in range(2)]) for r in range(3)]
            parts += [t[0], jnp.where(row8 < 2, t[1], pltpu.roll(t[2], 4, 0))]
    up = times01(jnp.concatenate(parts, axis=0), copy_matrix(256, 384))
    for c in range(3):
        for k in range(6):
            at = 16 * (6 * c + k)
            copy_rows(nat0, up[at + 8 : at + 16], 16, c, k)
            copy_rows(nat0, up[at : at + 8], 0, c, k)
            both = interleaved(nat0, 3, c, k)
            for z in (2 * k + 1, 2 * k + 2):
                if z in (1, 12):
                    ref = lo if z == 1 else hi
                    old = jnp.stack([ref[9 + 3 * c + t] for t in range(3)])
                else:
                    old = ep0[c, z]
                xa[c, z] = jnp.where(w0[0, z] > 0.0, old + both, 0.0)
    level0 = Level(3, 384, True, False, gx0, gxm0, gy0, gz0, m0, w0, ms0)
    smoothed(level0, b0, xa, xb, 2, 12, s0, f0)

    def last(z, c, v, a):
        to_natural(nat0, v + w0[c, z] * (b0[c, z] - a), c, 0)
        for k in range(3):
            out[c, z - 3, :, 128 * k : 128 * (k + 1)] = nat0[c, 0, k, 0:16]

    operate(level0, xb, 3, 11, s0, f0, last)


def call(kernel, outs, scratch, args, flops, mib):
    vmem = pl.BlockSpec(memory_space=pltpu.VMEM)
    size = sum(4 * int(a.size) for a in args)
    size += sum(4 * functools.reduce(lambda p, q: p * q, s) for s in outs)
    return pl.pallas_call(
        kernel,
        out_shape=[jax.ShapeDtypeStruct(s, F32) for s in outs],
        in_specs=[pl.BlockSpec(memory_space=pltpu.SMEM)] + [vmem] * (len(args) - 1),
        out_specs=[vmem] * len(outs),
        scratch_shapes=[pltpu.VMEM(s, F32) for s in scratch],
        compiler_params=pltpu.CompilerParams(vmem_limit_bytes=mib * 1024 * 1024),
        cost_estimate=pl.CostEstimate(flops=flops, bytes_accessed=size, transcendentals=0),
    )(*args)


def shards(load, density):
    wide = lax.axis_index("wide")
    narrow = lax.axis_index(NARROW)
    idx = jnp.stack([wide, narrow]).astype(jnp.int32)
    load, density, idx = lax.optimization_barrier((load, density, idx))

    def next_rows(v):
        return lax.ppermute(v, NARROW, cyclic(8, -1))

    def previous_rows(v):
        return lax.ppermute(v, NARROW, cyclic(8, 1))

    def above(v, steps=1):
        return lax.ppermute(v, "wide", cyclic(16, -steps))

    def below(v, steps=1):
        return lax.ppermute(v, "wide", cyclic(16, steps))

    lo = below(jnp.concatenate([load[:, 6:].reshape(6, 16, 384), density[5:]], axis=0))
    hi = above(jnp.concatenate([load[:, :2].reshape(6, 16, 384), density[:3]], axis=0))

    def rows_of(at):
        parts = []
        for c in range(4):
            own = density if c == 3 else load[c]
            end = 9 if c == 3 else 2 * c + 2
            parts += [lo[2 * c : end, at], own[:, at], hi[2 * c : end, at]]
        return jnp.concatenate(parts, axis=0)

    low, high = previous_rows(rows_of(slice(12, 16))), next_rows(rows_of(slice(0, 4)))
    rows = jnp.concatenate([high, low], axis=1)
    p0, c0 = (14, 3, 8, 384), (3, 8, 384)
    b0, gx0, gxm0, gy0, gz0, m0, w0, ms0, ep0, edge_low, edge_high, l1 = call(
        down0,
        [(3,) + p0, p0, p0, p0, p0, p0, (3,) + p0, p0, (3,) + p0, (3,) + c0, (3,) + c0, (9, 8, 384)],
        [(4, 14, 3, 24, 128), p0, (3,) + p0, (3, 4) + c0, (3, 4, 3, 24, 128), (2,) + c0, (3,) + c0],
        [idx, load, density, rows, lo, hi],
        10**7,
        17,
    )

    lo = below(jnp.concatenate([l1, edge_high.reshape(9, 8, 384)], axis=0))
    hi = above(jnp.concatenate([l1, edge_low.reshape(9, 8, 384)], axis=0))

    def level1_rows(at):
        b = [jnp.concatenate([v[0:6:2, at], v[1:6:2, at]], axis=1) for v in (l1, lo, hi)]
        return jnp.concatenate(b + [v[6:9] for v in (l1, lo, hi)], axis=0)

    after, before = next_rows(level1_rows(slice(0, 4))), previous_rows(level1_rows(slice(4, 8)))
    p1, c1 = (14, 3, 8, 256), (3, 8, 256)
    b1, gx1, gxm1, gy1, gz1, m1, w1, ep1, chunk = call(
        down1,
        [(3,) + p1, p1, p1, p1, p1, p1, (3,) + p1, (3,) + p1, (3, 8, 128)],
        [(4, 14, 2, 24, 128), p1, (3,) + p1, (3, 4) + c1, (3, 4, 2, 24, 128), (2,) + c1, (3,) + c1],
        [idx, l1, lo, hi, after, before],
        10**7,
        10,
    )

    chunks = jnp.broadcast_to(chunk[None], (64, 3, 8, 128))
    mine = lax.all_to_all(chunks, ("wide", "y"), 0, 0).reshape(16, 96, 128)
    other = lax.ppermute(mine, "core", cyclic(2, 1))
    p2, c2 = (40, 4, 8, 128), (4, 8, 128)
    u2 = (3, 10, 4, 8, 128)
    p3, c3 = (20, 2, 8, 128), (2, 8, 128)
    (out,) = call(
        rest,
        [(3, 8, 16, 384)],
        [p2, (3,) + p2, p2, p2, p2, p2, p2, (3,) + p2, p2, (3,) + p2, (3,) + p2]
        + [p3, (3,) + p3, p3, p3, p3, p3, p3, (3,) + p3, p3, (3,) + p3, (3,) + p3]
        + [(4, 16, 2, 8, 128), (3, 6, 1, 32, 128), (3, 6, 2, 24, 128), (3, 6, 3, 32, 128)]
        + [(2,) + c3, (3,) + c3, u2, u2, (2,) + c2, (3,) + c2]
        + [(3,) + p1, (3,) + p1, (2,) + c1, (3,) + c1, (3,) + p0, (3,) + p0, (2,) + c0, (3,) + c0],
        [idx, mine, other, lo, hi]
        + [b1, gx1, gxm1, gy1, gz1, m1, w1, ep1]
        + [b0, gx0, gxm0, gy0, gz0, m0, w0, ms0, ep0],
        10**8,
        40,
    )
    return out


def solution(mesh):
    split = Mesh(mesh.devices.reshape(16, 4, 2), ("wide",) + NARROW)
    in_specs = (P(None, "wide", NARROW, None), P("wide", NARROW, None))
    out_specs = P(None, "wide", NARROW, None)
    return jax.shard_map(shards, mesh=split, in_specs=in_specs, out_specs=out_specs, check_vma=False)
```

```python
import functools

import jax
import jax.numpy as jnp
from jax import lax
from jax.experimental import pallas as pl
from jax.experimental.pallas import tpu as pltpu
from jax.sharding import Mesh, PartitionSpec as P

DAMPING = 0.5
MASS = 0.02
NARROW = ("y", "core")
F32 = jnp.float32
BF16 = jnp.bfloat16


def cyclic(count, step):
    return [(i, (i + step) % count) for i in range(count)]


def after_y(v):
    return jnp.concatenate([v[1:], pltpu.roll(v[0], 7, 0)[None]], axis=0)


def before_y(v):
    return jnp.concatenate([pltpu.roll(v[v.shape[0] - 1], 1, 0)[None], v[:-1]], axis=0)


def after_x(v):
    return pltpu.roll(v, v.shape[2] - 1, 2)


def before_x(v):
    return pltpu.roll(v, 1, 2)


def times01(v, matrix):
    high = v.astype(BF16)
    rest = (v - high.astype(F32)).astype(BF16)
    both = jnp.concatenate([high, rest], axis=1)
    return jnp.dot(both, jnp.concatenate([matrix, matrix], axis=0), preferred_element_type=F32)


def pair_sum_matrix(fine, coarse, start, factor):
    i = lax.broadcasted_iota(jnp.int32, (fine, coarse), 0)
    j = lax.broadcasted_iota(jnp.int32, (fine, coarse), 1)
    return jnp.where((i >> 1) + start == j, factor, 0.0).astype(BF16)


def copy_matrix(coarse, fine):
    j = lax.broadcasted_iota(jnp.int32, (coarse, fine), 0)
    i = lax.broadcasted_iota(jnp.int32, (coarse, fine), 1)
    return jnp.where((i >> 1) == j, 1.0, 0.0).astype(BF16)


def lane_tiles(v):
    return [v[..., 128 * k : 128 * (k + 1)] for k in range(v.shape[-1] // 128)]


def join(parts):
    return parts[0] if len(parts) == 1 else jnp.concatenate(parts, axis=-1)


def interleaved(ref, tiles, *at):
    lanes = ref.shape[len(at)]
    return jnp.stack(
        [
            join([ref[(*at, k, pl.ds(t, 8, stride=tiles), slice(None))] for k in range(lanes)])
            for t in range(tiles)
        ]
    )


def to_natural(ref, v, *at):
    tiles = v.shape[0]
    for t in range(tiles):
        for k, part in enumerate(lane_tiles(v[t])):
            ref[(*at, k, pl.ds(t, 8, stride=tiles), slice(None))] = part


def row_pairs(ref, start, *at):
    parts = []
    for k in range(ref.shape[len(at)]):
        a = ref[(*at, k, pl.ds(start, 8, stride=2), slice(None))]
        b = ref[(*at, k, pl.ds(start + 1, 8, stride=2), slice(None))]
        parts.append(a + b)
    return join(parts)


def copy_rows(ref, v, start, *at):
    for k, part in enumerate(lane_tiles(v)):
        ref[(*at, k, pl.ds(start, 8, stride=2), slice(None))] = part
        ref[(*at, k, pl.ds(start + 1, 8, stride=2), slice(None))] = part


UNROLL = {2: 16, 4: 32, 6: 12, 9: 12}


def planes_loop(level, lo, hi, body):
    tiles, _, lanes = level.shape
    unroll = UNROLL[tiles * (lanes // 128)]
    while (hi - lo) % unroll:
        unroll -= 1
    lax.fori_loop(lo, hi, body, 0, unroll=unroll)


class Level:
    def __init__(self, tiles, lanes, wrap_x, wrap_y, gx, gxm, gy, gz, m, w, ms):
        self.shape = (tiles, 8, lanes)
        self.wrap_x, self.wrap_y = wrap_x, wrap_y
        self.gx, self.gxm, self.gy, self.gz = gx, gxm, gy, gz
        self.m, self.w, self.ms = m, w, ms

    def masks(self):
        tiles, _, lanes = self.shape
        t = lax.broadcasted_iota(jnp.int32, self.shape, 0)
        s = lax.broadcasted_iota(jnp.int32, self.shape, 1)
        lane = lax.broadcasted_iota(jnp.int32, self.shape, 2)
        row = tiles * s + t
        return (row == 0, row == 8 * tiles - 1, lane == 0, lane == lanes - 1)

    def after(self, v, axis, masks):
        r = after_y(v) if axis == 1 else after_x(v)
        if axis == 1 and self.wrap_y:
            r = jnp.where(masks[1], 0.0, r)
        if axis == 2 and self.wrap_x:
            r = jnp.where(masks[3], 0.0, r)
        return r

    def before(self, v, axis, masks):
        r = before_y(v) if axis == 1 else before_x(v)
        if axis == 1 and self.wrap_y:
            r = jnp.where(masks[0], 0.0, r)
        if axis == 2 and self.wrap_x:
            r = jnp.where(masks[2], 0.0, r)
        return r


def coefficients(level, rho, lo, hi, first):
    masks = level.masks()

    def shear(z):
        d = rho[z]
        return d * d * d

    def plane(z, _):
        d = rho[z]
        dn = rho[z + 1]
        g = d * d * d
        gn = dn * dn * dn
        gp = shear(z - 1)
        m = g * (0.5 + d)
        mn = gn * (0.5 + dn)
        gx = 0.5 * (g + after_x(g))
        gxm = 0.5 * (g + before_x(g))
        gy = 0.5 * (g + after_y(g))
        gz = 0.5 * (g + gn)
        total = MASS + gz + 0.5 * (g + gp)
        extra = None
        if level.wrap_x:
            gx = jnp.where(masks[3], 0.0, gx)
            gxm = jnp.where(masks[2], 0.0, gxm)
            extra = jnp.where(masks[2] | masks[3], 0.5 * g, 0.0)
        if level.wrap_y:
            gy = jnp.where(masks[1], 0.0, gy)
            more = jnp.where(masks[0] | masks[1], 0.5 * g, 0.0)
            extra = more if extra is None else extra + more
        if extra is not None:
            level.ms[z] = MASS + extra
            total = total + extra
        total = total + (gx + gxm) + (gy + before_y(gy)) + m
        inside = d > 0.0
        level.gx[z] = gx
        level.gxm[z] = gxm
        level.gy[z] = gy
        level.gz[z] = gz
        level.m[z] = m
        for c, beyond in enumerate((mn, level.after(m, 1, masks), level.after(m, 2, masks))):
            w = jnp.where(inside, DAMPING / (total + beyond), 0.0)
            level.w[c, z] = w
            first(z, c, w)
        return 0

    level.gz[lo - 1] = 0.5 * (shear(lo - 1) + shear(lo))
    last = rho[hi]
    level.m[hi] = last * last * last * (0.5 + last)
    planes_loop(level, lo, hi, plane)


def operate(level, u, lo, hi, s_ref, f_ref, emit):
    masks = level.masks()

    def stress(z):
        uz, uy, ux = u[0, z], u[1, z], u[2, z]
        left = level.before(ux, 2, masks)
        s_ref[1] = left
        div = (uz - u[0, z - 1]) + (uy - level.before(uy, 1, masks))
        return level.m[z] * (div + (ux - left))

    s_ref[0] = stress(lo)
    for c in range(3):
        f_ref[c] = level.gz[lo - 1] * (u[c, lo - 1] - u[c, lo])

    def plane(z, _):
        s, left = s_ref[0], s_ref[1]
        sn = stress(z + 1)
        s_ref[0] = sn
        gx, gxm, gy, gz = level.gx[z], level.gxm[z], level.gy[z], level.gz[z]
        for c in range(3):
            v = u[c, z]
            fz = gz * (v - u[c, z + 1])
            fx = gx * (v - after_x(v)) + gxm * (v - (left if c == 2 else before_x(v)))
            fy = gy * (v - after_y(v))
            grad = s - (sn if c == 0 else level.after(s, c, masks))
            mass = MASS if level.ms is None else level.ms[z]
            a = mass * v + (fz - f_ref[c]) + fx + (fy - before_y(fy)) + grad
            f_ref[c] = fz
            emit(z, c, v, a)
        return 0

    planes_loop(level, lo, hi, plane)


def smoothed(level, b, src, dst, lo, hi, s_ref, f_ref):
    def emit(z, c, v, a):
        dst[c, z] = v + level.w[c, z] * (b[c, z] - a)

    operate(level, src, lo, hi, s_ref, f_ref, emit)


def in_grid(shape, own, high, n, last):
    t = lax.broadcasted_iota(jnp.int32, shape, 0)
    s = lax.broadcasted_iota(jnp.int32, shape, 1)
    row = shape[0] * s + t
    bad_high = (row >= own) & (row < own + high) & (n == last)
    bad_low = (row >= own + high) & (n == 0)
    return jnp.where(bad_high | bad_low, 0.0, 1.0)


def down0(
    idx, load, dens, rows, lo, hi,
    b, gx, gxm, gy, gz, m, w, ms, ep, edge_low, edge_high, l1,
    nat, rho, e1, rz, back, s_ref, f_ref,
):
    wide, narrow = idx[0], idx[1]
    for c in range(4):
        first = 0 if c == 3 else 1
        for z in range(first, 14 - first):
            if z < 3:
                own = lo[2 * c + z - first]
            elif z < 11:
                own = dens[z - 3] if c == 3 else load[c, z - 3]
            else:
                own = hi[2 * c + z - 11]
            halo = rows[12 * c + z - first]
            for k in range(3):
                nat[c, z, k, 0:16] = own[:, 128 * k : 128 * (k + 1)]
                nat[c, z, k, 16:24] = halo[:, 128 * k : 128 * (k + 1)]
    grid = in_grid((3, 8, 384), 16, 4, narrow, 7)
    below = jnp.where(wide == 0, 0.0, 1.0) * grid
    above = jnp.where(wide == 15, 0.0, 1.0) * grid
    for z in range(14):
        rho[z] = interleaved(nat, 3, 3, z) * (below if z < 3 else above if z > 10 else grid)
    level = Level(3, 384, True, False, gx, gxm, gy, gz, m, w, ms)

    def first(z, c, scale):
        v = interleaved(nat, 3, c, z)
        b[c, z] = v
        e1[c, z] = scale * v

    coefficients(level, rho, 1, 13, first)
    smoothed(level, b, e1, ep, 2, 12, s_ref, f_ref)
    for c in range(3):
        edge_low[c] = ep[c, 4]
        edge_high[c] = ep[c, 9]
    rz[...] = jnp.zeros_like(rz)

    def residual(z, c, v, a):
        k = ((z + 1) >> 1) - 2
        rz[c, k] = rz[c, k] + (b[c, z] - a)

    operate(level, ep, 3, 11, s_ref, f_ref, residual)
    even, odd = [], []
    for c in range(3):
        for k in range(4):
            to_natural(back, rz[c, k], c, k)
            (odd if k % 2 else even).append(row_pairs(back, 0, c, k))
    for k in range(6):
        d = 0.25 * (row_pairs(nat, 0, 3, 2 * k + 1) + row_pairs(nat, 0, 3, 2 * k + 2))
        if k == 0:
            d = d * jnp.where(wide == 0, 0.0, 1.0)
        if k == 5:
            d = d * jnp.where(wide == 15, 0.0, 1.0)
        (odd if k % 2 else even).append(d)
    left = pair_sum_matrix(384, 384, 0, 0.5)
    right = pair_sum_matrix(384, 384, 192, 0.5)
    out = times01(jnp.concatenate(even, axis=0), left)
    out = out + times01(jnp.concatenate(odd, axis=0), right)
    l1[...] = out.reshape(9, 8, 384)


def halves(v):
    lane = lax.broadcasted_iota(jnp.int32, (v.shape[0], 256), 1)
    first = jnp.where(lane < 192, v[:, :256], 0.0)
    second = jnp.where(lane < 192, pltpu.roll(v, 192, 1)[:, :256], 0.0)
    return first, second


def down1(
    idx, own, lo, hi, after, before,
    b, gx, gxm, gy, gz, m, w, ep, chunk,
    nat, rho, e1, rz, back, s_ref, f_ref,
):
    wide, narrow = idx[0], idx[1]
    row = lax.broadcasted_iota(jnp.int32, (8, 256), 0)

    def put(c, z, r, v):
        for k in range(2):
            nat[c, z, k, pl.ds(r, 8), :] = v[:, 128 * k : 128 * (k + 1)]

    for c in range(4):
        for q in range(3 if c == 3 else 2):
            i = 2 * c + q
            zo = 2 * q - 1 if c == 3 else 2 * q
            for source, (shift, ref) in enumerate(((0, own), (-4, lo), (4, hi))):
                tiles = [halves(ref[i])]
                j = 6 * source + i
                at = j // 2 if c < 3 else 9 + 3 * source + q
                for k, ref in enumerate((after, before)):
                    v = ref[at]
                    tiles.append(halves(pltpu.roll(v, 4, 0) if c < 3 and j % 2 != k else v))
                for s in range(2):
                    z = zo + s + shift
                    if (0 <= z < 4) != (shift == 0):
                        continue
                    put(c, z + 5, 0, tiles[0][s])
                    if c < 3:
                        put(c, z + 5, 8, jnp.where(row < 4, tiles[1][s], 0.0))
                        put(c, z + 5, 16, jnp.where(row >= 4, tiles[2][s], 0.0))
                    else:
                        put(c, z + 5, 8, tiles[1][s])
                        put(c, z + 5, 16, tiles[2][s])
    grid = in_grid((3, 8, 256), 8, 8, narrow, 7)
    below = jnp.where(wide == 0, 0.0, 1.0) * grid
    above = jnp.where(wide == 15, 0.0, 1.0) * grid
    for z in range(14):
        rho[z] = interleaved(nat, 3, 3, z) * (below if z < 5 else above if z > 8 else grid)
    level = Level(3, 256, False, False, gx, gxm, gy, gz, m, w, None)

    def first(z, c, scale):
        v = interleaved(nat, 3, c, z)
        b[c, z] = v
        e1[c, z] = scale * v

    coefficients(level, rho, 1, 13, first)
    smoothed(level, b, e1, ep, 2, 12, s_ref, f_ref)
    rz[...] = jnp.zeros_like(rz)

    def residual(z, c, v, a):
        k = ((z + 1) >> 1) - 3
        rz[c, k] = rz[c, k] + (b[c, z] - a)

    operate(level, ep, 5, 9, s_ref, f_ref, residual)
    parts = []
    for c in range(3):
        for k in range(2):
            to_natural(back, rz[c, k], c, k)
            parts.append(row_pairs(back, 0, c, k))
    for k in range(2):
        d = row_pairs(nat, 0, 3, 2 * k + 5) + row_pairs(nat, 0, 3, 2 * k + 6)
        parts.append(0.25 * d)
    out = times01(jnp.concatenate(parts, axis=0), pair_sum_matrix(256, 128, 0, 0.5))
    row8 = lax.broadcasted_iota(jnp.int32, (8, 128), 0)
    lane = lax.broadcasted_iota(jnp.int32, (8, 128), 1)
    four = []
    for c in range(4):
        low, high = out[16 * c : 16 * c + 8], out[16 * c + 8 : 16 * c + 16]
        four.append(jnp.where(row8 < 4, low, pltpu.roll(high, 4, 0)))
    for c in range(3):
        d = four[3] if c == 3 else pltpu.roll(four[3], 96 - 32 * c, 1)
        chunk[c] = jnp.where(lane < 96, four[c], d)


def rest(
    idx, mine, other, lo, hi,
    b1, gx1, gxm1, gy1, gz1, m1, w1, ep1,
    b0, gx0, gxm0, gy0, gz0, m0, w0, ms0, ep0,
    out,
    rho2, b2, gx2, gxm2, gy2, gz2, m2, w2, ms2, ea, ep2,
    rho3, b3, gx3, gxm3, gy3, gz3, m3, w3, ms3, ec, ed,
    rz, nat2, nat1, nat0, s3, f3, ua, ub, s2, f2, va, vb, s1, f1, xa, xb, s0, f0,
):
    wide, narrow = idx[0], idx[1]
    core = narrow & 1
    zero2 = jnp.zeros((4, 8, 128), F32)
    zero3 = jnp.zeros((2, 8, 128), F32)

    def outside(i, _):
        z = jnp.where(i < 4, i, i + 32)
        for ref in (rho2, gx2, gxm2, gy2, gz2, m2, ms2):
            ref[z] = zero2
        for ref in (b2, w2, ea, ep2):
            for c in range(3):
                ref[c, z] = zero2
        return 0

    lax.fori_loop(0, 8, outside, 0)
    for z in (1, 18):
        rho3[z] = zero3
    for z in (0, 1, 18, 19):
        for c in range(3):
            ec[c, z] = zero3
            ed[c, z] = zero3

    lane = lax.broadcasted_iota(jnp.int32, (4, 8, 128), 2)

    def unpack(w, _):
        for c in range(3):
            for r in range(8):
                own = mine[w, pl.ds(8 * c + r, 4, stride=24), :]
                off = other[w, pl.ds(8 * c + r, 4, stride=24), :]
                ref = ea.at[c, 2 * w + 4 + r // 4, r % 4]
                ref[pl.ds(0, 4, stride=2), :] = jnp.where(core == 0, own, off)
                ref[pl.ds(1, 4, stride=2), :] = jnp.where(core == 0, off, own)
        return 0

    lax.fori_loop(0, 16, unpack, 0)

    def split(z, _):
        d = jnp.zeros((4, 8, 128), F32)
        for c in range(3):
            v = ea[c, z]
            moved = pltpu.roll(v, 32 + 32 * c, 2) if c < 3 else v
            d = jnp.where((lane >> 5) == c, moved, d)
        rho2[z] = d
        return 0

    lax.fori_loop(4, 36, split, 0, unroll=4)

    level2 = Level(4, 128, False, True, gx2, gxm2, gy2, gz2, m2, w2, ms2)

    def first2(z, c, scale):
        v = jnp.where(lane < 96, ea[c, z], 0.0)
        b2[c, z] = v
        ea[c, z] = scale * v

    coefficients(level2, rho2, 4, 36, first2)
    smoothed(level2, b2, ea, ep2, 4, 36, s2, f2)
    rz[...] = jnp.zeros_like(rz)

    def residual(z, c, v, a):
        r = b2[c, z] - a
        k = (z >> 1) - 2
        rz[c, k] = rz[c, k] + jnp.stack([r[0] + r[1], r[2] + r[3]])

    operate(level2, ep2, 4, 36, s2, f2, residual)

    def coarse_density(z, _):
        d = 0.25 * (rho2[2 * z + 4] + rho2[2 * z + 5])
        rz[3, z] = jnp.stack([d[0] + d[1], d[2] + d[3]])
        return 0

    lax.fori_loop(0, 16, coarse_density, 0, unroll=4)
    half = pair_sum_matrix(128, 128, 0, 0.5)
    for c in range(4):
        v = times01(rz[c].reshape(256, 128), half).reshape(16, 2, 8, 128)
        if c < 3:
            b3[c, 2:18] = v
        else:
            rho3[2:18] = v

    level3 = Level(2, 128, False, True, gx3, gxm3, gy3, gz3, m3, w3, ms3)

    def first3(z, c, scale):
        ec[c, z] = scale * b3[c, z]

    coefficients(level3, rho3, 2, 18, first3)
    for src, dst in ((ec, ed), (ed, ec), (ec, ed)):
        smoothed(level3, b3, src, dst, 2, 18, s3, f3)

    near = pl.ds(2 * wide, 10)
    gx2, gxm2, gy2, gz2, m2, ms2 = (v.at[near] for v in (gx2, gxm2, gy2, gz2, m2, ms2))
    b2, w2, ep2 = (v.at[:, near] for v in (b2, w2, ep2))
    parts = [ed[c, wide + k].reshape(16, 128) for c in range(3) for k in range(5)]
    up = times01(jnp.concatenate(parts, axis=0), copy_matrix(128, 128))
    for c in range(3):
        for k in range(5):
            at = 16 * (5 * c + k)
            t = [up[at : at + 8], up[at + 8 : at + 16]]
            both = jnp.stack([t[0], t[0], t[1], t[1]])
            for z in (2 * k, 2 * k + 1):
                ua[c, z] = jnp.where(w2[0, z] > 0.0, ep2[c, z] + both, 0.0)
    at2 = Level(4, 128, False, True, gx2, gxm2, gy2, gz2, m2, w2, ms2)
    smoothed(at2, b2, ua, ub, 1, 9, s2, f2)
    smoothed(at2, b2, ub, ua, 2, 8, s2, f2)

    turn = (8 - narrow) & 7
    parts = []
    for c in range(3):
        for k in range(6):
            v = ua[c, 2 + k]
            to_natural(nat2, jnp.stack([pltpu.roll(v[t], turn, 0) for t in range(4)]), c, k)
            parts += [nat2[c, k, 0, 0:8], nat2[c, k, 0, 24:32]]
    up = times01(jnp.concatenate(parts, axis=0), copy_matrix(128, 256))
    for c in range(3):
        for k in range(6):
            at = 16 * (6 * c + k)
            copy_rows(nat1, up[at + 8 : at + 16], 8, c, k)
            copy_rows(nat1, up[at : at + 8], 0, c, k)
            both = interleaved(nat1, 3, c, k)
            for z in (2 * k + 1, 2 * k + 2):
                if 2 <= z < 12:
                    va[c, z] = jnp.where(w1[0, z] > 0.0, ep1[c, z] + both, 0.0)
    level1 = Level(3, 256, False, False, gx1, gxm1, gy1, gz1, m1, w1, None)
    smoothed(level1, b1, va, vb, 3, 11, s1, f1)
    smoothed(level1, b1, vb, va, 4, 10, s1, f1)

    row8 = lax.broadcasted_iota(jnp.int32, (8, 256), 0)
    parts = []
    for c in range(3):
        for k in range(6):
            to_natural(nat1, va[c, 4 + k], c, k)
            t = [join([nat1[c, k, j, 8 * r : 8 * r + 8] for j in range(2)]) for r in range(3)]
            parts += [t[0], jnp.where(row8 < 2, t[1], pltpu.roll(t[2], 4, 0))]
    up = times01(jnp.concatenate(parts, axis=0), copy_matrix(256, 384))
    for c in range(3):
        for k in range(6):
            at = 16 * (6 * c + k)
            copy_rows(nat0, up[at + 8 : at + 16], 16, c, k)
            copy_rows(nat0, up[at : at + 8], 0, c, k)
            both = interleaved(nat0, 3, c, k)
            for z in (2 * k + 1, 2 * k + 2):
                if z in (1, 12):
                    ref = lo if z == 1 else hi
                    old = jnp.stack([ref[9 + 3 * c + t] for t in range(3)])
                else:
                    old = ep0[c, z]
                xa[c, z] = jnp.where(w0[0, z] > 0.0, old + both, 0.0)
    level0 = Level(3, 384, True, False, gx0, gxm0, gy0, gz0, m0, w0, ms0)
    smoothed(level0, b0, xa, xb, 2, 12, s0, f0)

    def last(z, c, v, a):
        to_natural(nat0, v + w0[c, z] * (b0[c, z] - a), c, 0)
        for k in range(3):
            out[c, z - 3, :, 128 * k : 128 * (k + 1)] = nat0[c, 0, k, 0:16]

    operate(level0, xb, 3, 11, s0, f0, last)


def call(kernel, outs, scratch, args, flops, mib):
    vmem = pl.BlockSpec(memory_space=pltpu.VMEM)
    size = sum(4 * int(a.size) for a in args)
    size += sum(4 * functools.reduce(lambda p, q: p * q, s) for s in outs)
    return pl.pallas_call(
        kernel,
        out_shape=[jax.ShapeDtypeStruct(s, F32) for s in outs],
        in_specs=[pl.BlockSpec(memory_space=pltpu.SMEM)] + [vmem] * (len(args) - 1),
        out_specs=[vmem] * len(outs),
        scratch_shapes=[pltpu.VMEM(s, F32) for s in scratch],
        compiler_params=pltpu.CompilerParams(vmem_limit_bytes=mib * 1024 * 1024),
        cost_estimate=pl.CostEstimate(flops=flops, bytes_accessed=size, transcendentals=0),
    )(*args)


def shards(load, density):
    wide = lax.axis_index("wide")
    narrow = lax.axis_index(NARROW)
    idx = jnp.stack([wide, narrow]).astype(jnp.int32)
    load, density, idx = lax.optimization_barrier((load, density, idx))

    def next_rows(v):
        return lax.ppermute(v, NARROW, cyclic(8, -1))

    def previous_rows(v):
        return lax.ppermute(v, NARROW, cyclic(8, 1))

    def above(v, steps=1):
        return lax.ppermute(v, "wide", cyclic(16, -steps))

    def below(v, steps=1):
        return lax.ppermute(v, "wide", cyclic(16, steps))

    lo = below(jnp.concatenate([load[:, 6:].reshape(6, 16, 384), density[5:]], axis=0))
    hi = above(jnp.concatenate([load[:, :2].reshape(6, 16, 384), density[:3]], axis=0))

    def rows_of(at):
        parts = []
        for c in range(4):
            own = density if c == 3 else load[c]
            end = 9 if c == 3 else 2 * c + 2
            parts += [lo[2 * c : end, at], own[:, at], hi[2 * c : end, at]]
        return jnp.concatenate(parts, axis=0)

    low, high = previous_rows(rows_of(slice(12, 16))), next_rows(rows_of(slice(0, 4)))
    rows = jnp.concatenate([high, low], axis=1)
    p0, c0 = (14, 3, 8, 384), (3, 8, 384)
    b0, gx0, gxm0, gy0, gz0, m0, w0, ms0, ep0, edge_low, edge_high, l1 = call(
        down0,
        [(3,) + p0, p0, p0, p0, p0, p0, (3,) + p0, p0, (3,) + p0, (3,) + c0, (3,) + c0, (9, 8, 384)],
        [(4, 14, 3, 24, 128), p0, (3,) + p0, (3, 4) + c0, (3, 4, 3, 24, 128), (2,) + c0, (3,) + c0],
        [idx, load, density, rows, lo, hi],
        10**7,
        17,
    )

    lo = below(jnp.concatenate([l1, edge_high.reshape(9, 8, 384)], axis=0))
    hi = above(jnp.concatenate([l1, edge_low.reshape(9, 8, 384)], axis=0))

    def level1_rows(at):
        b = [jnp.concatenate([v[0:6:2, at], v[1:6:2, at]], axis=1) for v in (l1, lo, hi)]
        return jnp.concatenate(b + [v[6:9] for v in (l1, lo, hi)], axis=0)

    after, before = next_rows(level1_rows(slice(0, 4))), previous_rows(level1_rows(slice(4, 8)))
    p1, c1 = (14, 3, 8, 256), (3, 8, 256)
    b1, gx1, gxm1, gy1, gz1, m1, w1, ep1, chunk = call(
        down1,
        [(3,) + p1, p1, p1, p1, p1, p1, (3,) + p1, (3,) + p1, (3, 8, 128)],
        [(4, 14, 2, 24, 128), p1, (3,) + p1, (3, 4) + c1, (3, 4, 2, 24, 128), (2,) + c1, (3,) + c1],
        [idx, l1, lo, hi, after, before],
        10**7,
        10,
    )

    chunks = jnp.broadcast_to(chunk[None], (64, 3, 8, 128))
    mine = lax.all_to_all(chunks, ("wide", "y"), 0, 0).reshape(16, 96, 128)
    other = lax.ppermute(mine, "core", cyclic(2, 1))
    p2, c2 = (40, 4, 8, 128), (4, 8, 128)
    u2 = (3, 10, 4, 8, 128)
    p3, c3 = (20, 2, 8, 128), (2, 8, 128)
    (out,) = call(
        rest,
        [(3, 8, 16, 384)],
        [p2, (3,) + p2, p2, p2, p2, p2, p2, (3,) + p2, p2, (3,) + p2, (3,) + p2]
        + [p3, (3,) + p3, p3, p3, p3, p3, p3, (3,) + p3, p3, (3,) + p3, (3,) + p3]
        + [(4, 16, 2, 8, 128), (3, 6, 1, 32, 128), (3, 6, 2, 24, 128), (3, 6, 3, 32, 128)]
        + [(2,) + c3, (3,) + c3, u2, u2, (2,) + c2, (3,) + c2]
        + [(3,) + p1, (3,) + p1, (2,) + c1, (3,) + c1, (3,) + p0, (3,) + p0, (2,) + c0, (3,) + c0],
        [idx, mine, other, lo, hi]
        + [b1, gx1, gxm1, gy1, gz1, m1, w1, ep1]
        + [b0, gx0, gxm0, gy0, gz0, m0, w0, ms0, ep0],
        10**8,
        40,
    )
    return out


def solution(mesh):
    split = Mesh(mesh.devices.reshape(16, 4, 2), ("wide",) + NARROW)
    in_specs = (P(None, "wide", NARROW, None), P("wide", NARROW, None))
    out_specs = P(None, "wide", NARROW, None)
    return jax.shard_map(shards, mesh=split, in_specs=in_specs, out_specs=out_specs, check_vma=False)
```

```python
import functools

import jax
import jax.numpy as jnp
from jax import lax
from jax.experimental import pallas as pl
from jax.experimental.pallas import tpu as pltpu
from jax.sharding import Mesh, PartitionSpec as P

DAMPING = 0.5
MASS = 0.02
NARROW = ("y", "core")
F32 = jnp.float32
BF16 = jnp.bfloat16


def cyclic(count, step):
    return [(i, (i + step) % count) for i in range(count)]


def after_y(v):
    return jnp.concatenate([v[1:], pltpu.roll(v[0], 7, 0)[None]], axis=0)


def before_y(v):
    return jnp.concatenate([pltpu.roll(v[v.shape[0] - 1], 1, 0)[None], v[:-1]], axis=0)


def after_x(v):
    return pltpu.roll(v, v.shape[2] - 1, 2)


def before_x(v):
    return pltpu.roll(v, 1, 2)


def times01(v, matrix):
    high = v.astype(BF16)
    rest = (v - high.astype(F32)).astype(BF16)
    both = jnp.concatenate([high, rest], axis=1)
    return jnp.dot(both, jnp.concatenate([matrix, matrix], axis=0), preferred_element_type=F32)


def pair_sum_matrix(fine, coarse, start, factor):
    i = lax.broadcasted_iota(jnp.int32, (fine, coarse), 0)
    j = lax.broadcasted_iota(jnp.int32, (fine, coarse), 1)
    return jnp.where((i >> 1) + start == j, factor, 0.0).astype(BF16)


def copy_matrix(coarse, fine):
    j = lax.broadcasted_iota(jnp.int32, (coarse, fine), 0)
    i = lax.broadcasted_iota(jnp.int32, (coarse, fine), 1)
    return jnp.where((i >> 1) == j, 1.0, 0.0).astype(BF16)


def lane_tiles(v):
    return [v[..., 128 * k : 128 * (k + 1)] for k in range(v.shape[-1] // 128)]


def join(parts):
    return parts[0] if len(parts) == 1 else jnp.concatenate(parts, axis=-1)


def interleaved(ref, tiles, *at):
    lanes = ref.shape[len(at)]
    return jnp.stack(
        [
            join([ref[(*at, k, pl.ds(t, 8, stride=tiles), slice(None))] for k in range(lanes)])
            for t in range(tiles)
        ]
    )


def to_natural(ref, v, *at):
    tiles = v.shape[0]
    for t in range(tiles):
        for k, part in enumerate(lane_tiles(v[t])):
            ref[(*at, k, pl.ds(t, 8, stride=tiles), slice(None))] = part


def row_pairs(ref, start, *at):
    parts = []
    for k in range(ref.shape[len(at)]):
        a = ref[(*at, k, pl.ds(start, 8, stride=2), slice(None))]
        b = ref[(*at, k, pl.ds(start + 1, 8, stride=2), slice(None))]
        parts.append(a + b)
    return join(parts)


def copy_rows(ref, v, start, *at):
    for k, part in enumerate(lane_tiles(v)):
        ref[(*at, k, pl.ds(start, 8, stride=2), slice(None))] = part
        ref[(*at, k, pl.ds(start + 1, 8, stride=2), slice(None))] = part


UNROLL = {2: 16, 4: 32, 6: 12, 9: 12}


def planes_loop(level, lo, hi, body):
    tiles, _, lanes = level.shape
    unroll = UNROLL[tiles * (lanes // 128)]
    while (hi - lo) % unroll:
        unroll -= 1
    lax.fori_loop(lo, hi, body, 0, unroll=unroll)


class Level:
    def __init__(self, tiles, lanes, wrap_x, wrap_y, gx, gxm, gy, gz, m, w, ms):
        self.shape = (tiles, 8, lanes)
        self.wrap_x, self.wrap_y = wrap_x, wrap_y
        self.gx, self.gxm, self.gy, self.gz = gx, gxm, gy, gz
        self.m, self.w, self.ms = m, w, ms

    def masks(self):
        tiles, _, lanes = self.shape
        t = lax.broadcasted_iota(jnp.int32, self.shape, 0)
        s = lax.broadcasted_iota(jnp.int32, self.shape, 1)
        lane = lax.broadcasted_iota(jnp.int32, self.shape, 2)
        row = tiles * s + t
        return (row == 0, row == 8 * tiles - 1, lane == 0, lane == lanes - 1)

    def after(self, v, axis, masks):
        r = after_y(v) if axis == 1 else after_x(v)
        if axis == 1 and self.wrap_y:
            r = jnp.where(masks[1], 0.0, r)
        if axis == 2 and self.wrap_x:
            r = jnp.where(masks[3], 0.0, r)
        return r

    def before(self, v, axis, masks):
        r = before_y(v) if axis == 1 else before_x(v)
        if axis == 1 and self.wrap_y:
            r = jnp.where(masks[0], 0.0, r)
        if axis == 2 and self.wrap_x:
            r = jnp.where(masks[2], 0.0, r)
        return r


def coefficients(level, rho, lo, hi, first):
    masks = level.masks()

    def shear(z):
        d = rho[z]
        return d * d * d

    def plane(z, _):
        d = rho[z]
        dn = rho[z + 1]
        g = d * d * d
        gn = dn * dn * dn
        gp = shear(z - 1)
        m = g * (0.5 + d)
        mn = gn * (0.5 + dn)
        gx = 0.5 * (g + after_x(g))
        gxm = 0.5 * (g + before_x(g))
        gy = 0.5 * (g + after_y(g))
        gz = 0.5 * (g + gn)
        total = MASS + gz + 0.5 * (g + gp)
        extra = None
        if level.wrap_x:
            gx = jnp.where(masks[3], 0.0, gx)
            gxm = jnp.where(masks[2], 0.0, gxm)
            extra = jnp.where(masks[2] | masks[3], 0.5 * g, 0.0)
        if level.wrap_y:
            gy = jnp.where(masks[1], 0.0, gy)
            more = jnp.where(masks[0] | masks[1], 0.5 * g, 0.0)
            extra = more if extra is None else extra + more
        if extra is not None:
            level.ms[z] = MASS + extra
            total = total + extra
        total = total + (gx + gxm) + (gy + before_y(gy)) + m
        inside = d > 0.0
        level.gx[z] = gx
        level.gxm[z] = gxm
        level.gy[z] = gy
        level.gz[z] = gz
        level.m[z] = m
        for c, beyond in enumerate((mn, level.after(m, 1, masks), level.after(m, 2, masks))):
            w = jnp.where(inside, DAMPING / (total + beyond), 0.0)
            level.w[c, z] = w
            first(z, c, w)
        return 0

    level.gz[lo - 1] = 0.5 * (shear(lo - 1) + shear(lo))
    last = rho[hi]
    level.m[hi] = last * last * last * (0.5 + last)
    planes_loop(level, lo, hi, plane)


def operate(level, u, lo, hi, s_ref, f_ref, emit):
    masks = level.masks()

    def stress(z):
        uz, uy, ux = u[0, z], u[1, z], u[2, z]
        left = level.before(ux, 2, masks)
        s_ref[1] = left
        div = (uz - u[0, z - 1]) + (uy - level.before(uy, 1, masks))
        return level.m[z] * (div + (ux - left))

    s_ref[0] = stress(lo)
    for c in range(3):
        f_ref[c] = level.gz[lo - 1] * (u[c, lo - 1] - u[c, lo])

    def plane(z, _):
        s, left = s_ref[0], s_ref[1]
        sn = stress(z + 1)
        s_ref[0] = sn
        gx, gxm, gy, gz = level.gx[z], level.gxm[z], level.gy[z], level.gz[z]
        for c in range(3):
            v = u[c, z]
            fz = gz * (v - u[c, z + 1])
            fx = gx * (v - after_x(v)) + gxm * (v - (left if c == 2 else before_x(v)))
            fy = gy * (v - after_y(v))
            grad = s - (sn if c == 0 else level.after(s, c, masks))
            mass = MASS if level.ms is None else level.ms[z]
            a = mass * v + (fz - f_ref[c]) + fx + (fy - before_y(fy)) + grad
            f_ref[c] = fz
            emit(z, c, v, a)
        return 0

    planes_loop(level, lo, hi, plane)


def smoothed(level, b, src, dst, lo, hi, s_ref, f_ref):
    def emit(z, c, v, a):
        dst[c, z] = v + level.w[c, z] * (b[c, z] - a)

    operate(level, src, lo, hi, s_ref, f_ref, emit)


def in_grid(shape, own, high, n, last):
    t = lax.broadcasted_iota(jnp.int32, shape, 0)
    s = lax.broadcasted_iota(jnp.int32, shape, 1)
    row = shape[0] * s + t
    bad_high = (row >= own) & (row < own + high) & (n == last)
    bad_low = (row >= own + high) & (n == 0)
    return jnp.where(bad_high | bad_low, 0.0, 1.0)


def down0(
    idx, load, dens, rows, lo, hi,
    b, gx, gxm, gy, gz, m, w, ms, ep, edge_low, edge_high, l1,
    nat, rho, e1, rz, back, s_ref, f_ref,
):
    wide, narrow = idx[0], idx[1]
    for c in range(4):
        first = 0 if c == 3 else 1
        for z in range(first, 14 - first):
            if z < 3:
                own = lo[2 * c + z - first]
            elif z < 11:
                own = dens[z - 3] if c == 3 else load[c, z - 3]
            else:
                own = hi[2 * c + z - 11]
            halo = rows[12 * c + z - first]
            for k in range(3):
                nat[c, z, k, 0:16] = own[:, 128 * k : 128 * (k + 1)]
                nat[c, z, k, 16:24] = halo[:, 128 * k : 128 * (k + 1)]
    grid = in_grid((3, 8, 384), 16, 4, narrow, 7)
    below = jnp.where(wide == 0, 0.0, 1.0) * grid
    above = jnp.where(wide == 15, 0.0, 1.0) * grid
    for z in range(14):
        rho[z] = interleaved(nat, 3, 3, z) * (below if z < 3 else above if z > 10 else grid)
    level = Level(3, 384, True, False, gx, gxm, gy, gz, m, w, ms)

    def first(z, c, scale):
        v = interleaved(nat, 3, c, z)
        b[c, z] = v
        e1[c, z] = scale * v

    coefficients(level, rho, 1, 13, first)
    smoothed(level, b, e1, ep, 2, 12, s_ref, f_ref)
    for c in range(3):
        edge_low[c] = ep[c, 4]
        edge_high[c] = ep[c, 9]
    rz[...] = jnp.zeros_like(rz)

    def residual(z, c, v, a):
        k = ((z + 1) >> 1) - 2
        rz[c, k] = rz[c, k] + (b[c, z] - a)

    operate(level, ep, 3, 11, s_ref, f_ref, residual)
    even, odd = [], []
    for c in range(3):
        for k in range(4):
            to_natural(back, rz[c, k], c, k)
            (odd if k % 2 else even).append(row_pairs(back, 0, c, k))
    for k in range(6):
        d = 0.25 * (row_pairs(nat, 0, 3, 2 * k + 1) + row_pairs(nat, 0, 3, 2 * k + 2))
        if k == 0:
            d = d * jnp.where(wide == 0, 0.0, 1.0)
        if k == 5:
            d = d * jnp.where(wide == 15, 0.0, 1.0)
        (odd if k % 2 else even).append(d)
    left = pair_sum_matrix(384, 384, 0, 0.5)
    right = pair_sum_matrix(384, 384, 192, 0.5)
    out = times01(jnp.concatenate(even, axis=0), left)
    out = out + times01(jnp.concatenate(odd, axis=0), right)
    l1[...] = out.reshape(9, 8, 384)


def halves(v):
    lane = lax.broadcasted_iota(jnp.int32, (v.shape[0], 256), 1)
    first = jnp.where(lane < 192, v[:, :256], 0.0)
    second = jnp.where(lane < 192, pltpu.roll(v, 192, 1)[:, :256], 0.0)
    return first, second


def down1(
    idx, own, lo, hi, after, before,
    b, gx, gxm, gy, gz, m, w, ep, chunk,
    nat, rho, e1, rz, back, s_ref, f_ref,
):
    wide, narrow = idx[0], idx[1]
    row = lax.broadcasted_iota(jnp.int32, (8, 256), 0)

    def put(c, z, r, v):
        for k in range(2):
            nat[c, z, k, pl.ds(r, 8), :] = v[:, 128 * k : 128 * (k + 1)]

    for c in range(4):
        for q in range(3 if c == 3 else 2):
            i = 2 * c + q
            zo = 2 * q - 1 if c == 3 else 2 * q
            for source, (shift, ref) in enumerate(((0, own), (-4, lo), (4, hi))):
                tiles = [halves(ref[i])]
                j = 6 * source + i
                at = j // 2 if c < 3 else 9 + 3 * source + q
                for k, ref in enumerate((after, before)):
                    v = ref[at]
                    tiles.append(halves(pltpu.roll(v, 4, 0) if c < 3 and j % 2 != k else v))
                for s in range(2):
                    z = zo + s + shift
                    if (0 <= z < 4) != (shift == 0):
                        continue
                    put(c, z + 5, 0, tiles[0][s])
                    if c < 3:
                        put(c, z + 5, 8, jnp.where(row < 4, tiles[1][s], 0.0))
                        put(c, z + 5, 16, jnp.where(row >= 4, tiles[2][s], 0.0))
                    else:
                        put(c, z + 5, 8, tiles[1][s])
                        put(c, z + 5, 16, tiles[2][s])
    grid = in_grid((3, 8, 256), 8, 8, narrow, 7)
    below = jnp.where(wide == 0, 0.0, 1.0) * grid
    above = jnp.where(wide == 15, 0.0, 1.0) * grid
    for z in range(14):
        rho[z] = interleaved(nat, 3, 3, z) * (below if z < 5 else above if z > 8 else grid)
    level = Level(3, 256, False, False, gx, gxm, gy, gz, m, w, None)

    def first(z, c, scale):
        v = interleaved(nat, 3, c, z)
        b[c, z] = v
        e1[c, z] = scale * v

    coefficients(level, rho, 1, 13, first)
    smoothed(level, b, e1, ep, 2, 12, s_ref, f_ref)
    rz[...] = jnp.zeros_like(rz)

    def residual(z, c, v, a):
        k = ((z + 1) >> 1) - 3
        rz[c, k] = rz[c, k] + (b[c, z] - a)

    operate(level, ep, 5, 9, s_ref, f_ref, residual)
    parts = []
    for c in range(3):
        for k in range(2):
            to_natural(back, rz[c, k], c, k)
            parts.append(row_pairs(back, 0, c, k))
    for k in range(2):
        d = row_pairs(nat, 0, 3, 2 * k + 5) + row_pairs(nat, 0, 3, 2 * k + 6)
        parts.append(0.25 * d)
    out = times01(jnp.concatenate(parts, axis=0), pair_sum_matrix(256, 128, 0, 0.5))
    row8 = lax.broadcasted_iota(jnp.int32, (8, 128), 0)
    lane = lax.broadcasted_iota(jnp.int32, (8, 128), 1)
    four = []
    for c in range(4):
        low, high = out[16 * c : 16 * c + 8], out[16 * c + 8 : 16 * c + 16]
        four.append(jnp.where(row8 < 4, low, pltpu.roll(high, 4, 0)))
    for c in range(3):
        d = four[3] if c == 3 else pltpu.roll(four[3], 96 - 32 * c, 1)
        chunk[c] = jnp.where(lane < 96, four[c], d)


def rest(
    idx, mine, other, lo, hi,
    b1, gx1, gxm1, gy1, gz1, m1, w1, ep1,
    b0, gx0, gxm0, gy0, gz0, m0, w0, ms0, ep0,
    out,
    rho2, b2, gx2, gxm2, gy2, gz2, m2, w2, ms2, ea, ep2,
    rho3, b3, gx3, gxm3, gy3, gz3, m3, w3, ms3, ec, ed,
    rz, nat2, nat1, nat0, s3, f3, ua, ub, s2, f2, va, vb, s1, f1, xa, xb, s0, f0,
):
    wide, narrow = idx[0], idx[1]
    core = narrow & 1
    zero2 = jnp.zeros((4, 8, 128), F32)
    zero3 = jnp.zeros((2, 8, 128), F32)

    def outside(i, _):
        z = jnp.where(i < 4, i, i + 32)
        for ref in (rho2, gx2, gxm2, gy2, gz2, m2, ms2):
            ref[z] = zero2
        for ref in (b2, w2, ea, ep2):
            for c in range(3):
                ref[c, z] = zero2
        return 0

    lax.fori_loop(0, 8, outside, 0)
    for z in (1, 18):
        rho3[z] = zero3
    for z in (0, 1, 18, 19):
        for c in range(3):
            ec[c, z] = zero3
            ed[c, z] = zero3

    lane = lax.broadcasted_iota(jnp.int32, (4, 8, 128), 2)

    def unpack(w, _):
        for c in range(3):
            for r in range(8):
                own = mine[w, pl.ds(8 * c + r, 4, stride=24), :]
                off = other[w, pl.ds(8 * c + r, 4, stride=24), :]
                ref = ea.at[c, 2 * w + 4 + r // 4, r % 4]
                ref[pl.ds(0, 4, stride=2), :] = jnp.where(core == 0, own, off)
                ref[pl.ds(1, 4, stride=2), :] = jnp.where(core == 0, off, own)
        return 0

    lax.fori_loop(0, 16, unpack, 0)

    def split(z, _):
        d = jnp.zeros((4, 8, 128), F32)
        for c in range(3):
            v = ea[c, z]
            moved = pltpu.roll(v, 32 + 32 * c, 2) if c < 3 else v
            d = jnp.where((lane >> 5) == c, moved, d)
        rho2[z] = d
        return 0

    lax.fori_loop(4, 36, split, 0, unroll=16)

    level2 = Level(4, 128, False, True, gx2, gxm2, gy2, gz2, m2, w2, ms2)

    def first2(z, c, scale):
        v = jnp.where(lane < 96, ea[c, z], 0.0)
        b2[c, z] = v
        ea[c, z] = scale * v

    coefficients(level2, rho2, 4, 36, first2)
    smoothed(level2, b2, ea, ep2, 4, 36, s2, f2)
    rz[...] = jnp.zeros_like(rz)

    def residual(z, c, v, a):
        r = b2[c, z] - a
        k = (z >> 1) - 2
        rz[c, k] = rz[c, k] + jnp.stack([r[0] + r[1], r[2] + r[3]])

    operate(level2, ep2, 4, 36, s2, f2, residual)

    def coarse_density(z, _):
        d = 0.25 * (rho2[2 * z + 4] + rho2[2 * z + 5])
        rz[3, z] = jnp.stack([d[0] + d[1], d[2] + d[3]])
        return 0

    lax.fori_loop(0, 16, coarse_density, 0, unroll=4)
    half = pair_sum_matrix(128, 128, 0, 0.5)
    for c in range(4):
        v = times01(rz[c].reshape(256, 128), half).reshape(16, 2, 8, 128)
        if c < 3:
            b3[c, 2:18] = v
        else:
            rho3[2:18] = v

    level3 = Level(2, 128, False, True, gx3, gxm3, gy3, gz3, m3, w3, ms3)

    def first3(z, c, scale):
        ec[c, z] = scale * b3[c, z]

    coefficients(level3, rho3, 2, 18, first3)
    for src, dst in ((ec, ed), (ed, ec), (ec, ed)):
        smoothed(level3, b3, src, dst, 2, 18, s3, f3)

    near = pl.ds(2 * wide, 10)
    gx2, gxm2, gy2, gz2, m2, ms2 = (v.at[near] for v in (gx2, gxm2, gy2, gz2, m2, ms2))
    b2, w2, ep2 = (v.at[:, near] for v in (b2, w2, ep2))
    parts = [ed[c, wide + k].reshape(16, 128) for c in range(3) for k in range(5)]
    up = times01(jnp.concatenate(parts, axis=0), copy_matrix(128, 128))
    for c in range(3):
        for k in range(5):
            at = 16 * (5 * c + k)
            t = [up[at : at + 8], up[at + 8 : at + 16]]
            both = jnp.stack([t[0], t[0], t[1], t[1]])
            for z in (2 * k, 2 * k + 1):
                ua[c, z] = jnp.where(w2[0, z] > 0.0, ep2[c, z] + both, 0.0)
    at2 = Level(4, 128, False, True, gx2, gxm2, gy2, gz2, m2, w2, ms2)
    smoothed(at2, b2, ua, ub, 1, 9, s2, f2)
    smoothed(at2, b2, ub, ua, 2, 8, s2, f2)

    turn = (8 - narrow) & 7
    parts = []
    for c in range(3):
        for k in range(6):
            v = ua[c, 2 + k]
            to_natural(nat2, jnp.stack([pltpu.roll(v[t], turn, 0) for t in range(4)]), c, k)
            parts += [nat2[c, k, 0, 0:8], nat2[c, k, 0, 24:32]]
    up = times01(jnp.concatenate(parts, axis=0), copy_matrix(128, 256))
    for c in range(3):
        for k in range(6):
            at = 16 * (6 * c + k)
            copy_rows(nat1, up[at + 8 : at + 16], 8, c, k)
            copy_rows(nat1, up[at : at + 8], 0, c, k)
            both = interleaved(nat1, 3, c, k)
            for z in (2 * k + 1, 2 * k + 2):
                if 2 <= z < 12:
                    va[c, z] = jnp.where(w1[0, z] > 0.0, ep1[c, z] + both, 0.0)
    level1 = Level(3, 256, False, False, gx1, gxm1, gy1, gz1, m1, w1, None)
    smoothed(level1, b1, va, vb, 3, 11, s1, f1)
    smoothed(level1, b1, vb, va, 4, 10, s1, f1)

    row8 = lax.broadcasted_iota(jnp.int32, (8, 256), 0)
    parts = []
    for c in range(3):
        for k in range(6):
            to_natural(nat1, va[c, 4 + k], c, k)
            t = [join([nat1[c, k, j, 8 * r : 8 * r + 8] for j in range(2)]) for r in range(3)]
            parts += [t[0], jnp.where(row8 < 2, t[1], pltpu.roll(t[2], 4, 0))]
    up = times01(jnp.concatenate(parts, axis=0), copy_matrix(256, 384))
    for c in range(3):
        for k in range(6):
            at = 16 * (6 * c + k)
            copy_rows(nat0, up[at + 8 : at + 16], 16, c, k)
            copy_rows(nat0, up[at : at + 8], 0, c, k)
            both = interleaved(nat0, 3, c, k)
            for z in (2 * k + 1, 2 * k + 2):
                if z in (1, 12):
                    ref = lo if z == 1 else hi
                    old = jnp.stack([ref[9 + 3 * c + t] for t in range(3)])
                else:
                    old = ep0[c, z]
                xa[c, z] = jnp.where(w0[0, z] > 0.0, old + both, 0.0)
    level0 = Level(3, 384, True, False, gx0, gxm0, gy0, gz0, m0, w0, ms0)
    smoothed(level0, b0, xa, xb, 2, 12, s0, f0)

    def last(z, c, v, a):
        to_natural(nat0, v + w0[c, z] * (b0[c, z] - a), c, 0)
        for k in range(3):
            out[c, z - 3, :, 128 * k : 128 * (k + 1)] = nat0[c, 0, k, 0:16]

    operate(level0, xb, 3, 11, s0, f0, last)


def call(kernel, outs, scratch, args, flops, mib):
    vmem = pl.BlockSpec(memory_space=pltpu.VMEM)
    size = sum(4 * int(a.size) for a in args)
    size += sum(4 * functools.reduce(lambda p, q: p * q, s) for s in outs)
    return pl.pallas_call(
        kernel,
        out_shape=[jax.ShapeDtypeStruct(s, F32) for s in outs],
        in_specs=[pl.BlockSpec(memory_space=pltpu.SMEM)] + [vmem] * (len(args) - 1),
        out_specs=[vmem] * len(outs),
        scratch_shapes=[pltpu.VMEM(s, F32) for s in scratch],
        compiler_params=pltpu.CompilerParams(vmem_limit_bytes=mib * 1024 * 1024),
        cost_estimate=pl.CostEstimate(flops=flops, bytes_accessed=size, transcendentals=0),
    )(*args)


def shards(load, density):
    wide = lax.axis_index("wide")
    narrow = lax.axis_index(NARROW)
    idx = jnp.stack([wide, narrow]).astype(jnp.int32)
    load, density, idx = lax.optimization_barrier((load, density, idx))

    def next_rows(v):
        return lax.ppermute(v, NARROW, cyclic(8, -1))

    def previous_rows(v):
        return lax.ppermute(v, NARROW, cyclic(8, 1))

    def above(v, steps=1):
        return lax.ppermute(v, "wide", cyclic(16, -steps))

    def below(v, steps=1):
        return lax.ppermute(v, "wide", cyclic(16, steps))

    lo = below(jnp.concatenate([load[:, 6:].reshape(6, 16, 384), density[5:]], axis=0))
    hi = above(jnp.concatenate([load[:, :2].reshape(6, 16, 384), density[:3]], axis=0))

    def rows_of(at):
        parts = []
        for c in range(4):
            own = density if c == 3 else load[c]
            end = 9 if c == 3 else 2 * c + 2
            parts += [lo[2 * c : end, at], own[:, at], hi[2 * c : end, at]]
        return jnp.concatenate(parts, axis=0)

    low, high = previous_rows(rows_of(slice(12, 16))), next_rows(rows_of(slice(0, 4)))
    rows = jnp.concatenate([high, low], axis=1)
    p0, c0 = (14, 3, 8, 384), (3, 8, 384)
    b0, gx0, gxm0, gy0, gz0, m0, w0, ms0, ep0, edge_low, edge_high, l1 = call(
        down0,
        [(3,) + p0, p0, p0, p0, p0, p0, (3,) + p0, p0, (3,) + p0, (3,) + c0, (3,) + c0, (9, 8, 384)],
        [(4, 14, 3, 24, 128), p0, (3,) + p0, (3, 4) + c0, (3, 4, 3, 24, 128), (2,) + c0, (3,) + c0],
        [idx, load, density, rows, lo, hi],
        10**7,
        17,
    )

    lo = below(jnp.concatenate([l1, edge_high.reshape(9, 8, 384)], axis=0))
    hi = above(jnp.concatenate([l1, edge_low.reshape(9, 8, 384)], axis=0))

    def level1_rows(at):
        b = [jnp.concatenate([v[0:6:2, at], v[1:6:2, at]], axis=1) for v in (l1, lo, hi)]
        return jnp.concatenate(b + [v[6:9] for v in (l1, lo, hi)], axis=0)

    after, before = next_rows(level1_rows(slice(0, 4))), previous_rows(level1_rows(slice(4, 8)))
    p1, c1 = (14, 3, 8, 256), (3, 8, 256)
    b1, gx1, gxm1, gy1, gz1, m1, w1, ep1, chunk = call(
        down1,
        [(3,) + p1, p1, p1, p1, p1, p1, (3,) + p1, (3,) + p1, (3, 8, 128)],
        [(4, 14, 2, 24, 128), p1, (3,) + p1, (3, 4) + c1, (3, 4, 2, 24, 128), (2,) + c1, (3,) + c1],
        [idx, l1, lo, hi, after, before],
        10**7,
        10,
    )

    chunks = jnp.broadcast_to(chunk[None], (64, 3, 8, 128))
    mine = lax.all_to_all(chunks, ("wide", "y"), 0, 0).reshape(16, 96, 128)
    other = lax.ppermute(mine, "core", cyclic(2, 1))
    p2, c2 = (40, 4, 8, 128), (4, 8, 128)
    u2 = (3, 10, 4, 8, 128)
    p3, c3 = (20, 2, 8, 128), (2, 8, 128)
    (out,) = call(
        rest,
        [(3, 8, 16, 384)],
        [p2, (3,) + p2, p2, p2, p2, p2, p2, (3,) + p2, p2, (3,) + p2, (3,) + p2]
        + [p3, (3,) + p3, p3, p3, p3, p3, p3, (3,) + p3, p3, (3,) + p3, (3,) + p3]
        + [(4, 16, 2, 8, 128), (3, 6, 1, 32, 128), (3, 6, 2, 24, 128), (3, 6, 3, 32, 128)]
        + [(2,) + c3, (3,) + c3, u2, u2, (2,) + c2, (3,) + c2]
        + [(3,) + p1, (3,) + p1, (2,) + c1, (3,) + c1, (3,) + p0, (3,) + p0, (2,) + c0, (3,) + c0],
        [idx, mine, other, lo, hi]
        + [b1, gx1, gxm1, gy1, gz1, m1, w1, ep1]
        + [b0, gx0, gxm0, gy0, gz0, m0, w0, ms0, ep0],
        10**8,
        40,
    )
    return out


def solution(mesh):
    split = Mesh(mesh.devices.reshape(16, 4, 2), ("wide",) + NARROW)
    in_specs = (P(None, "wide", NARROW, None), P("wide", NARROW, None))
    out_specs = P(None, "wide", NARROW, None)
    return jax.shard_map(shards, mesh=split, in_specs=in_specs, out_specs=out_specs, check_vma=False)
```
